32 devices in a mesh: seq: 8 (over z, y), head: 4 (over x, core).
Axes of the slice: x: 2, y: 2, z: 4, core: 2. Of those that a mesh axis runs over, the one named last changes fastest.
Arguments:
- inputs: float32 [2, 2048, 768], P(None, 'seq'), may hold values from -6 to 6
- seq_lengths: int32 [2], replicated, may hold values from 64 to 2048, as said below
- first_gain: float32 [768], replicated, may hold values from 0.5 to 1.5
- first_shift: float32 [768], replicated, may hold values from -3 to 3
- query_weight: float32 [768, 768], P(None, 'head'), may hold values from -0.21875 to 0.21875
- key_weight: float32 [768, 768], P(None, 'head'), may hold values from -0.21875 to 0.21875
- value_weight: float32 [768, 768], P(None, 'head'), may hold values from -0.21875 to 0.21875
- query_kernel: float32 [3, 768], P(None, 'head'), may hold values from -3 to 3
- key_kernel: float32 [3, 768], P(None, 'head'), may hold values from -3 to 3
- value_kernel: float32 [3, 768], P(None, 'head'), may hold values from -3 to 3
- output_weight: float32 [768, 768], P('head'), may hold values from -1.25 to 1.25
- output_bias: float32 [768], replicated, may hold values from -3 to 3
- second_gain: float32 [768], replicated, may hold values from 0.5 to 1.5
- second_shift: float32 [768], replicated, may hold values from -3 to 3
- inner_weight: float32 [768, 3072], P(None, 'head'), may hold values from -0.21875 to 0.21875
- hidden_layer_bias: float32 [3072], P('head'), may hold values from -3 to 3
- outer_weight: float32 [3072, 768], P('head'), may hold values from -0.109375 to 0.109375
- outer_bias: float32 [768], replicated, may hold values from -3 to 3
- cotangent: float32 [2, 2048, 768], P(None, 'seq'), may hold values from -6 to 6
Outputs:
- result: float32 [2, 2048, 768], P(None, 'seq')
- grad_inputs: float32 [2, 2048, 768], P(None, 'seq')
- grad_first_gain: float32 [768], replicated
- grad_first_shift: float32 [768], replicated
- grad_query_weight: float32 [768, 768], P(None, 'head')
- grad_key_weight: float32 [768, 768], P(None, 'head')
- grad_value_weight: float32 [768, 768], P(None, 'head')
- grad_query_kernel: float32 [3, 768], P(None, 'head')
- grad_key_kernel: float32 [3, 768], P(None, 'head')
- grad_value_kernel: float32 [3, 768], P(None, 'head')
- grad_output_weight: float32 [768, 768], P('head')
- grad_output_bias: float32 [768], replicated
- grad_second_gain: float32 [768], replicated
- grad_second_shift: float32 [768], replicated
- grad_inner_weight: float32 [768, 3072], P(None, 'head')
- grad_inner_bias: float32 [3072], P('head')
- grad_outer_weight: float32 [3072, 768], P('head')
- grad_outer_bias: float32 [768], replicated
The draws below stay inside these ranges and needn't reach their ends.
Inputs may be any that keep to these rules, and one draw needn't show every extreme that they name: `seq_lengths`: in every draw one sequence, which one drawn from the seed, has all 2048 positions live.
All inputs are finite; a program needn't handle non-finite values.
Results may differ from the reference program's by a relative error of at most 0.0003.
Values sent between devices are 32-bit elements; how exact they have to be, the bound alone decides.
A program may use at most 512 MiB of HBM per device.

```python
import jax
import jax.numpy as jnp
from jax import lax

D = 768
HSIZE = 64
FF = 3072
SEQS = 2
SHORTEST = 64
LEN = 2048


def draw_seq_lengths(key, part):
    key = jax.random.fold_in(key, 11)
    first, second, third, chosen_key = jax.random.split(key, 4)
    span = LEN - SHORTEST + 1
    draw_one = jax.random.randint(first, (SEQS,), 0, span)
    draw_two = jax.random.randint(second, (SEQS,), 0, span)
    draw_three = jax.random.randint(third, (SEQS,), 0, span)
    lengths = SHORTEST + jnp.minimum(draw_one, jnp.minimum(draw_two, draw_three))
    chosen = jax.random.randint(chosen_key, (), 0, SEQS)
    return jnp.where(jnp.arange(SEQS) == chosen, LEN, lengths).astype(jnp.int32)


def block_scale(stream_key, shape, pieces, least, largest):
    def one(position, shards_of):
        draws = jax.random.uniform(jax.random.fold_in(jax.random.fold_in(stream_key, 6), position), (shards_of,), jnp.float32, least / len(pieces), largest / len(pieces))
        return jnp.repeat(jnp.exp(draws), shape[position] // shards_of).reshape((-1,) + (1,) * (len(shape) - position - 1))

    loudness = one(*pieces[0])
    for cut in pieces[1:]:
        loudness = loudness * one(*cut)
    return loudness


def normal_values(own_key, shape, spread, most, cuts=(), held_as=jnp.bfloat16):
    gain = block_scale(own_key, shape, cuts, -0.22, 0.18) if cuts else 1.0
    drawn = jax.random.normal(own_key, shape, jnp.float32) * spread * gain
    return jnp.minimum(jnp.maximum(drawn, -most), most).astype(held_as)


def setup_inputs(seed: int = 0) -> dict:
    splits = jax.random.split(jax.random.key(seed), 20)
    return {
        "inputs": normal_values(splits[0], (SEQS, LEN, D), 1.0, 6.0, ((1, 8),), jnp.float32),
        "seq_lengths": draw_seq_lengths(jax.random.fold_in(splits[19], 71), 0),
        "first_gain": jnp.clip(1.0 + 0.1 * jax.random.normal(splits[2], (D,), jnp.float32), 0.5, 1.5),
        "first_shift": normal_values(splits[3], (D,), 0.5, 3.0, (), jnp.float32),
        "query_weight": normal_values(splits[4], (D, D), D ** -0.5, 0.21875, ((1, 4),), jnp.float32),
        "key_weight": normal_values(splits[5], (D, D), D ** -0.5, 0.21875, ((1, 4),), jnp.float32),
        "value_weight": normal_values(splits[6], (D, D), D ** -0.5, 0.21875, ((1, 4),), jnp.float32),
        "query_kernel": normal_values(splits[7], (3, D), 0.6, 3.0, ((1, 4),), jnp.float32),
        "key_kernel": normal_values(splits[8], (3, D), 0.6, 3.0, ((1, 4),), jnp.float32),
        "value_kernel": normal_values(splits[9], (3, D), 0.6, 3.0, ((1, 4),), jnp.float32),
        "output_weight": normal_values(splits[10], (D, D), (D // 32) ** -0.5, 1.25, ((0, 4),), jnp.float32),
        "output_bias": normal_values(splits[11], (D,), 0.5, 3.0, (), jnp.float32),
        "second_gain": jnp.clip(1.0 + 0.1 * jax.random.normal(splits[12], (D,), jnp.float32), 0.5, 1.5),
        "second_shift": normal_values(splits[13], (D,), 0.5, 3.0, (), jnp.float32),
        "inner_weight": normal_values(splits[14], (D, FF), D ** -0.5, 0.21875, ((1, 4),), jnp.float32),
        "hidden_layer_bias": normal_values(splits[15], (FF,), 0.5, 3.0, ((0, 4),), jnp.float32),
        "outer_weight": normal_values(splits[16], (FF, D), FF ** -0.5, 0.109375, ((0, 4),), jnp.float32),
        "outer_bias": normal_values(splits[17], (D,), 0.5, 3.0, (), jnp.float32),
        "cotangent": normal_values(splits[18], (SEQS, LEN, D), 1.0, 6.0, ((1, 8),), jnp.float32),
    }


EXACT_FLOAT_MODE = lax.Precision.HIGHEST
NEGATIVE = -1e+30

@jax.custom_vjp
def low(v):
    return lax.optimization_barrier(v.astype(jnp.bfloat16)).astype(jnp.float32)

@jax.custom_vjp
def low_back(v):
    return v

def low_keep(v):
    return (low(v), None)

def low_pass(kept, grad):
    return (grad,)

def back_keep(v):
    return (v, None)

def back_low(kept, grad):
    return (low(grad),)
low.defvjp(low_keep, low_pass)
low_back.defvjp(back_keep, back_low)

def project(input_operand, weight_matrix):
    return jnp.einsum('vcb,bo->vco', input_operand, weight_matrix, precision=EXACT_FLOAT_MODE)

def normalize(stream, norm_gain, norm_shift):
    centered = stream - lax.optimization_barrier(jnp.mean(stream, -1, keepdims=True))
    inverse = lax.rsqrt(lax.optimization_barrier(jnp.mean(centered * centered, -1, keepdims=True)) + 1e-05)
    return centered * inverse * norm_gain + norm_shift

def causal_mix(stream, kernel):
    once = jnp.pad(stream, ((0, 0), (1, 0), (0, 0)))[:, :-1]
    twice = jnp.pad(stream, ((0, 0), (2, 0), (0, 0)))[:, :-2]
    return kernel[0] * stream + kernel[1] * once + kernel[2] * twice

def attend(queries, keys, values, length):
    extent = queries.shape[0]
    heads = queries.shape[1] // HSIZE
    block = min(512, extent)
    query_blocks = queries.reshape(extent // block, block, heads, HSIZE)
    key_heads = keys.reshape(extent, heads, HSIZE)
    value_heads = values.reshape(extent, heads, HSIZE)
    columns = jnp.arange(extent).astype(jnp.int32)
    starts = (jnp.arange(extent // block) * block).astype(jnp.int32)

    def one_block(item):
        query_block, first_row = item
        row_ids = first_row + jnp.arange(block).astype(jnp.int32)
        scores = jnp.einsum('qhe,khe->hqk', query_block, key_heads, precision=EXACT_FLOAT_MODE) * HSIZE ** (-0.5)
        allowed = (columns[None, :] <= row_ids[:, None]) & (columns[None, :] < length)
        masked = jnp.where(allowed[None], scores, NEGATIVE)
        weight_values = jnp.exp(masked - lax.optimization_barrier(jnp.max(masked, -1, keepdims=True)))
        weight_values = weight_values / lax.optimization_barrier(jnp.sum(weight_values, -1, keepdims=True))
        output = jnp.einsum('hqk,khe->qhe', weight_values, value_heads, precision=EXACT_FLOAT_MODE)
        live = (row_ids < length).astype(output.dtype)
        return output.reshape(block, heads * HSIZE) * live[:, None]
    mapped = lax.map(jax.checkpoint(one_block), (query_blocks, starts))
    return mapped.reshape(extent, heads * HSIZE)

def reference(inputs, seq_lengths, first_gain, first_shift, query_weight, key_weight, value_weight, query_kernel, key_kernel, value_kernel, output_weight, output_bias, second_gain, second_shift, inner_weight, hidden_layer_bias, outer_weight, outer_bias, cotangent):

    def forward(stream, gain_one, shift_one, weight_query, weight_key, weight_value, kernel_query, kernel_key, kernel_value, weight_output, bias_output, gain_two, shift_two, weight_inner, bias_inner, weight_outer, bias_outer):
        normed = normalize(stream, gain_one, shift_one)
        queries = causal_mix(project(normed, weight_query), kernel_query)
        keys = causal_mix(project(normed, weight_key), kernel_key)
        values = causal_mix(project(normed, weight_value), kernel_value)
        attended = jax.vmap(attend)(queries, keys, values, seq_lengths)
        mixed = stream + project(attended, weight_output) + bias_output
        hidden = project(normalize(mixed, gain_two, shift_two), weight_inner) + bias_inner
        active = jnp.square(jnp.maximum(hidden, 0.0))
        return mixed + project(active, weight_outer) + bias_outer
    result, pullback = jax.vjp(forward, inputs, first_gain, first_shift, query_weight, key_weight, value_weight, query_kernel, key_kernel, value_kernel, output_weight, output_bias, second_gain, second_shift, inner_weight, hidden_layer_bias, outer_weight, outer_bias)
    grads = pullback(cotangent)
    return (result, grads[0], grads[1], grads[2], grads[3], grads[4], grads[5], grads[6], grads[7], grads[8], grads[9], grads[10], grads[11], grads[12], grads[13], grads[14], grads[15], grads[16])
```

```python
import functools

import jax
import jax.numpy as jnp
from jax import lax
from jax.experimental import pallas as pl
from jax.experimental.pallas import tpu as pltpu
from jax.sharding import PartitionSpec as P

MESH = pl.DeviceIdType.MESH

HSIZE = 64


EXACT_FLOAT_MODE = lax.Precision.HIGH
EPSILON = 1e-05
NEGATIVE = -1e30


def shifted(block, axis, distance):
    devices = range(lax.axis_size(axis))
    route = [(i - distance, i) for i in devices if i - distance in devices]
    return lax.ppermute(block, axis, route)


def matmul(input_operand, weight_matrix):
    return jnp.einsum("scd,df->scf", input_operand, weight_matrix, precision=EXACT_FLOAT_MODE)


def transposed(input_operand, weight_matrix):
    return jnp.einsum("scf,df->scd", input_operand, weight_matrix, precision=EXACT_FLOAT_MODE)


def outer_sum(first_rows, second_rows):
    return jnp.einsum("scd,scf->df", first_rows, second_rows, precision=EXACT_FLOAT_MODE)


def normalize(stream, norm_gain, norm_shift):
    centered = stream - jnp.mean(stream, -1, keepdims=True)
    inverse = lax.rsqrt(jnp.mean(centered * centered, -1, keepdims=True) + EPSILON)
    unit_rows = centered * inverse
    return (unit_rows * norm_gain + norm_shift, unit_rows, inverse)


def normalize_back(gradient, norm_gain, unit_rows, inverse):
    scaled = gradient * norm_gain
    middle = (
        scaled
        - jnp.mean(scaled, -1, keepdims=True)
        - unit_rows * jnp.mean(scaled * unit_rows, -1, keepdims=True)
    )
    return (inverse * middle, jnp.sum(gradient * unit_rows, (0, 1)), jnp.sum(gradient, (0, 1)))


def split_heads(flat):
    return flat.reshape(flat.shape[0], flat.shape[1], flat.shape[2] // HSIZE, HSIZE)


def allowed_pairs(query_pos, key_pos, lengths):
    return (key_pos[None, None, :] <= query_pos[None, :, None]) & (
        key_pos[None, None, :] < lengths[:, None, None]
    )


def pair_terms(queries, gradients, log_total, row_dots, query_pos, keyvals, key_pos, lengths):
    channels = queries.shape[2]
    query_heads = split_heads(queries)
    key_heads = split_heads(keyvals[:, :, :channels])
    value_heads = split_heads(keyvals[:, :, channels:])
    grad_heads = split_heads(gradients)
    scores = jnp.einsum(
        "sqhe,skhe->shqk", query_heads, key_heads, precision=EXACT_FLOAT_MODE
    ) * HSIZE ** (-0.5)
    allowed = allowed_pairs(query_pos, key_pos, lengths)[:, None]
    weight_values = jnp.exp(jnp.where(allowed, scores - log_total[..., None], NEGATIVE))
    weight_grads = jnp.einsum(
        "sqhe,skhe->shqk", grad_heads, value_heads, precision=EXACT_FLOAT_MODE
    )
    score_grads = weight_values * (weight_grads - row_dots[..., None])
    return (weight_values, score_grads, query_heads, key_heads, grad_heads)


def key_facing_term(terms, keyvals, channels):
    value_part = jnp.einsum("shqk,sqhe->skhe", terms[0], terms[4], precision=EXACT_FLOAT_MODE)
    key_part = jnp.einsum(
        "shqk,sqhe->skhe", terms[1], terms[2], precision=EXACT_FLOAT_MODE
    ) * HSIZE ** (-0.5)
    shape = (keyvals.shape[0], keyvals.shape[1], channels)
    return jnp.concatenate([key_part.reshape(shape), value_part.reshape(shape)], 2)


def query_side_term(terms):
    return jnp.einsum(
        "shqk,skhe->sqhe", terms[1], terms[3], precision=EXACT_FLOAT_MODE
    ) * HSIZE ** (-0.5)


def key_terms(queries, gradients, log_total, row_dots, query_pos, keyvals, key_pos, lengths):
    terms = pair_terms(
        queries, gradients, log_total, row_dots, query_pos, keyvals, key_pos, lengths
    )
    return key_facing_term(terms, keyvals, queries.shape[2])


def general_shards(
    inputs,
    seq_lengths,
    first_gain,
    first_shift,
    query_weight,
    key_weight,
    value_weight,
    query_kernel,
    key_kernel,
    value_kernel,
    output_weight,
    output_bias,
    second_gain,
    second_shift,
    inner_weight,
    hidden_layer_bias,
    outer_weight,
    outer_bias,
    cotangent,
):
    sequences, rows, model = inputs.shape
    channels = query_weight.shape[1]
    heads = channels // HSIZE
    positions = lax.axis_index("seq") * rows + jnp.arange(rows, dtype=jnp.int32)
    live_rows = (positions[None, :] < seq_lengths[:, None]).astype(jnp.float32)
    joined_weight = jnp.concatenate([query_weight, key_weight, value_weight], 1)
    joined_kernel = jnp.concatenate([query_kernel, key_kernel, value_kernel], 1)
    normed, leading_unit_value, first_inverse = normalize(inputs, first_gain, first_shift)
    projected = matmul(normed, joined_weight)
    rims = shifted(projected[:, rows - 2 :, :], "seq", 1)
    extended = jnp.concatenate([rims, projected], 1)
    convolved = (
        joined_kernel[0] * extended[:, 2:]
        + joined_kernel[1] * extended[:, 1:-1]
        + joined_kernel[2] * extended[:, :-2]
    )
    queries = convolved[:, :, :channels]
    keyvals = convolved[:, :, channels:]
    query_heads = split_heads(queries)
    portion = lax.all_gather(keyvals, "seq", axis=1, tiled=True)
    highest = jnp.full((sequences, heads, rows), NEGATIVE, jnp.float32)
    key_pos = jnp.arange(portion.shape[1], dtype=jnp.int32)
    key_heads = split_heads(portion[:, :, :channels])
    value_heads = split_heads(portion[:, :, channels:])
    scores = jnp.einsum(
        "sqhe,skhe->shqk", query_heads, key_heads, precision=EXACT_FLOAT_MODE
    ) * HSIZE ** (-0.5)
    allowed = allowed_pairs(positions, key_pos, seq_lengths)[:, None]
    masked = jnp.where(allowed, scores, NEGATIVE)
    new_high = jnp.maximum(highest, jnp.max(masked, -1))
    weight_values = jnp.where(allowed, jnp.exp(masked - new_high[..., None]), 0.0)
    summed = jnp.sum(weight_values, -1)
    weighted = jnp.einsum("shqk,skhe->shqe", weight_values, value_heads, precision=EXACT_FLOAT_MODE)
    highest, summed, weighted = (new_high, summed, weighted)
    log_total = highest + jnp.log(summed)
    attended = (weighted / summed[..., None]).transpose(0, 2, 1, 3).reshape(
        sequences, rows, channels
    ) * live_rows[..., None]
    branch = lax.psum(matmul(attended, output_weight), "head")
    mixed = inputs + branch + output_bias
    normed_two, second_unit, second_inverse = normalize(mixed, second_gain, second_shift)
    hidden = matmul(normed_two, inner_weight) + hidden_layer_bias
    rectified = jnp.maximum(hidden, 0.0)
    active = rectified * rectified
    result = mixed + lax.psum(matmul(active, outer_weight), "head") + outer_bias
    grad_outer_weight = outer_sum(active, cotangent)
    grad_outer_bias = jnp.sum(cotangent, (0, 1))
    grad_hidden = transposed(cotangent, outer_weight) * (2.0 * rectified)
    grad_inner_weight = outer_sum(normed_two, grad_hidden)
    grad_inner_bias = jnp.sum(grad_hidden, (0, 1))
    grad_normed_two = lax.psum(transposed(grad_hidden, inner_weight), "head")
    through_two, grad_second_gain, grad_second_shift = normalize_back(
        grad_normed_two, second_gain, second_unit, second_inverse
    )
    grad_mixed = cotangent + through_two
    grad_output_weight = outer_sum(attended, grad_mixed)
    grad_output_bias = jnp.sum(grad_mixed, (0, 1))
    grad_attended = transposed(grad_mixed, output_weight) * live_rows[..., None]
    row_dots = jnp.sum(split_heads(grad_attended) * split_heads(attended), -1).transpose(0, 2, 1)
    terms = pair_terms(
        queries, grad_attended, log_total, row_dots, positions, portion, key_pos, seq_lengths
    )
    grad_queries = query_side_term(terms).reshape(jnp.zeros_like(queries).shape)
    query_side = jnp.concatenate([queries, grad_attended], 2)
    row_stats = jnp.concatenate([log_total, row_dots], 1).transpose(0, 2, 1)
    side_rows = lax.all_gather(query_side, "seq", axis=1, tiled=True)
    stat_rows = lax.all_gather(row_stats, "seq", axis=1, tiled=True)
    query_pos = jnp.arange(side_rows.shape[1], dtype=jnp.int32)
    portion_total = stat_rows[:, :, :heads].transpose(0, 2, 1)
    portion_dots = stat_rows[:, :, heads:].transpose(0, 2, 1)
    grad_keyvals = key_terms(
        side_rows[:, :, :channels],
        side_rows[:, :, channels:],
        portion_total,
        portion_dots,
        query_pos,
        keyvals,
        positions,
        seq_lengths,
    )
    grad_convolved = jnp.concatenate([grad_queries, grad_keyvals], 2)
    following = shifted(grad_convolved[:, :2, :], "seq", -1)
    grad_extended = jnp.concatenate([grad_convolved, following], 1)
    grad_projected = (
        joined_kernel[0] * grad_extended[:, :rows]
        + joined_kernel[1] * grad_extended[:, 1 : rows + 1]
        + joined_kernel[2] * grad_extended[:, 2:]
    )
    grad_kernel = jnp.stack(
        [
            jnp.sum(grad_convolved * extended[:, 2:], (0, 1)),
            jnp.sum(grad_convolved * extended[:, 1:-1], (0, 1)),
            jnp.sum(grad_convolved * extended[:, :-2], (0, 1)),
        ]
    )
    grad_joined = outer_sum(normed, grad_projected)
    grad_normed = lax.psum(transposed(grad_projected, joined_weight), "head")
    through_one, grad_first_gain, grad_first_shift = normalize_back(
        grad_normed, first_gain, leading_unit_value, first_inverse
    )
    grad_inputs = grad_mixed + through_one
    grad_query_weight = grad_joined[:, :channels]
    grad_key_weight = grad_joined[:, channels : 2 * channels]
    grad_value_weight = grad_joined[:, 2 * channels :]
    grad_query_kernel = grad_kernel[:, :channels]
    grad_key_kernel = grad_kernel[:, channels : 2 * channels]
    grad_value_kernel = grad_kernel[:, 2 * channels :]
    (
        grad_first_gain,
        grad_first_shift,
        grad_query_weight,
        grad_key_weight,
        grad_value_weight,
        grad_query_kernel,
        grad_key_kernel,
        grad_value_kernel,
        grad_output_weight,
        grad_output_bias,
        grad_second_gain,
        grad_second_shift,
        grad_inner_weight,
        grad_inner_bias,
        grad_outer_weight,
        grad_outer_bias,
    ) = lax.psum(
        (
            grad_first_gain,
            grad_first_shift,
            grad_query_weight,
            grad_key_weight,
            grad_value_weight,
            grad_query_kernel,
            grad_key_kernel,
            grad_value_kernel,
            grad_output_weight,
            grad_output_bias,
            grad_second_gain,
            grad_second_shift,
            grad_inner_weight,
            grad_inner_bias,
            grad_outer_weight,
            grad_outer_bias,
        ),
        "seq",
    )
    return (
        result,
        grad_inputs,
        grad_first_gain,
        grad_first_shift,
        grad_query_weight,
        grad_key_weight,
        grad_value_weight,
        grad_query_kernel,
        grad_key_kernel,
        grad_value_kernel,
        grad_output_weight,
        grad_output_bias,
        grad_second_gain,
        grad_second_shift,
        grad_inner_weight,
        grad_inner_bias,
        grad_outer_weight,
        grad_outer_bias,
    )


class Comm:
    def __init__(self, send_sems, recv_sems, local_sems=None):
        self.send_sems, self.recv_sems, self.local_sems = send_sems, recv_sems, local_sems
        self.used = 0
        self.used_local = 0
        self.sent = []
        self.stored = []

    def copy(self, source, target, device, when=None):
        index = self.used
        self.used += 1
        made = pltpu.make_async_remote_copy(
            src_ref=source,
            dst_ref=target,
            send_sem=self.send_sems.at[index],
            recv_sem=self.recv_sems.at[index],
            device_id=device,
            device_id_type=MESH,
        )
        if when is None:
            made.start()
        else:
            pl.when(when)(made.start)
        self.sent.append((made, when))
        return made

    def settle(self, made):
        self.sent = [one for one in self.sent if one[0] is not made]
        made.wait_send()

    def local(self, source, target, when=None, keep=True):
        made = pltpu.make_async_copy(source, target, self.local_sems.at[self.used_local])
        self.used_local += 1
        if when is None:
            made.start()
        else:
            pl.when(when)(made.start)
        if keep:
            self.stored.append((made, when))
        return made

    def finish(self):
        for made, when in self.sent:
            if when is None:
                made.wait_send()
            else:
                pl.when(when)(made.wait_send)
        for made, when in self.stored:
            if when is None:
                made.wait()
            else:
                pl.when(when)(made.wait)


def wait_for(made, when=None):
    if when is None:
        made.wait_recv()
    else:
        pl.when(when)(made.wait_recv)


class Place:
    def __init__(self):
        self.seq = lax.axis_index("seq")
        self.head = lax.axis_index("head")
        self.z = self.seq // 2
        self.y = self.seq % 2
        self.other = 1 - self.y
        self.core = self.head % 2
        self.at_end = (self.z == 0) | (self.z == LINE - 1)
        self.at_middle = jnp.logical_not(self.at_end)
        step = 2 - 4 * (self.z // 2)
        self.pair = (2 * self.z + self.other, self.head)
        self.inward = (self.seq + step, self.head)
        self.outward = (self.seq - step, self.head)
        self.sibling = (self.seq, self.head + 1 - 2 * self.core)
        self.facing = (self.seq, (self.head + 2) % 4)


LINE = 4


def rows_at(ref, start, count):
    return ref.at[pl.ds(pl.multiple_of(start, 8), count)]


class Land:
    def __init__(self, ref):
        self.ref, self.used = ref, 0

    def take(self, rows):
        got = self.ref.at[pl.ds(self.used, rows)]
        self.used += rows
        return got


def sum_pair_first(comm, place, land, source, target, start, count):
    half = count // 2
    line, from_end, from_middle = land.take(half), land.take(half), land.take(half)
    own = rows_at(target, start + place.y * half, half)
    far = rows_at(source, start + place.other * half, half)
    near = rows_at(source, start + place.y * half, half)
    made = comm.copy(far, line, place.pair)
    yield
    made.wait_recv()
    line[...] = line[...] + near[...]
    inward = comm.copy(line, from_end, place.inward, place.at_end)
    yield

    @pl.when(place.at_middle)
    def _():
        inward.wait_recv()
        from_end[...] = from_end[...] + line[...]

    across = comm.copy(from_end, from_middle, place.inward, place.at_middle)
    yield

    @pl.when(place.at_middle)
    def _():
        across.wait_recv()
        from_middle[...] = from_middle[...] + from_end[...]

    outward = comm.copy(from_middle, own, place.outward, place.at_middle)
    early = comm.copy(from_middle, own, place.pair, place.at_middle)
    comm.local(from_middle, own, place.at_middle)
    yield
    wait_for(outward, place.at_end)
    late = comm.copy(own, own, place.pair, place.at_end)
    yield
    wait_for(early, place.at_middle)
    wait_for(late, place.at_end)
    yield


def sum_line_first(comm, place, land, source, target, start, count):
    half = count // 2
    whole, from_middle, from_pair = land.take(count), land.take(half), land.take(half)
    all_rows = rows_at(source, start, count)
    mine, theirs = place.z // 2, 1 - place.z // 2
    own, rest = rows_at(target, start + mine * half, half), rows_at(target, start + theirs * half, half)
    inward = comm.copy(all_rows, whole, place.inward, place.at_end)
    yield

    @pl.when(place.at_middle)
    def _():
        inward.wait_recv()
        whole[...] = whole[...] + all_rows[...]

    across = comm.copy(rows_at(whole, theirs * half, half), from_middle, place.inward, place.at_middle)
    yield

    @pl.when(place.at_middle)
    def _():
        across.wait_recv()
        from_middle[...] = from_middle[...] + rows_at(whole, mine * half, half)[...]

    paired = comm.copy(from_middle, from_pair, place.pair, place.at_middle)
    yield

    @pl.when(place.at_middle)
    def _():
        paired.wait_recv()
        from_pair[...] = from_pair[...] + from_middle[...]

    back = comm.copy(from_pair, own, place.inward, place.at_middle)
    outward = comm.copy(from_pair, own, place.outward, place.at_middle)
    comm.local(from_pair, own, place.at_middle)
    yield
    wait_for(back, place.at_middle)
    last = comm.copy(rest, rest, place.outward, place.at_middle)
    yield
    wait_for(outward, place.at_end)
    wait_for(last, place.at_end)
    yield


class Crew:
    def __init__(self):
        self.waiting = []

    def add(self, one, delay=0):
        self.waiting.append([one, delay])

    def advance(self):
        left = []
        for entry in self.waiting:
            if entry[1] > 0:
                entry[1] -= 1
                left.append(entry)
                continue
            try:
                next(entry[0])
                left.append(entry)
            except StopIteration:
                pass
        self.waiting = left

    def drain(self):
        while self.waiting:
            self.advance()


def split(value):
    high = value.astype(jnp.bfloat16)
    return high, (value - high.astype(jnp.float32)).astype(jnp.bfloat16)


def dot(left, right, dims):
    return lax.dot_general(left, right, (dims, ((), ())), preferred_element_type=jnp.float32)


def dot_three(left, right, dims):
    return dot(left[0], right[0], dims) + (dot(left[0], right[1], dims) + dot(left[1], right[0], dims))


PLAIN, BOTH_LAST, BOTH_FIRST = ((1,), (0,)), ((1,), (1,)), ((0,), (0,))


def product(left, right, dims=PLAIN):
    return dot_three(split(left), split(right), dims)


def beside(value):
    high, low = split(value)
    return jnp.concatenate([high, high, low], 1)


def against(value):
    high, low = split(value)
    return jnp.concatenate([high, low, high], 0)


def unit_rows(rows):
    centered = rows - jnp.mean(rows, -1, keepdims=True)
    inverse = lax.rsqrt(jnp.mean(centered * centered, -1, keepdims=True) + EPSILON)
    return centered * inverse, inverse


def longer_first(lengths):
    return jnp.where(lengths[1] > lengths[0], 1, 0).astype(jnp.int32)


def head_lanes(head, base=0):
    return slice(base + head * HSIZE, base + (head + 1) * HSIZE)


class Spread:
    def __init__(self, comm, place, part, ends, upward=True, own=None):
        self.comm, self.place, self.part, self.ends = comm, place, part, ends
        self.own = own or (lambda half: part(place.seq, half))
        z, y = place.z, place.y
        self.rank = z if upward else ends - 1 - z
        self.inside = z < ends
        self.more = self.inside & ((z < ends - 1) if upward else (z > 0))
        self.leads = (y == 0) if upward else (y == 1)
        self.next = (place.seq + (2 if upward else -2), place.head)
        self.sign = 1 if upward else -1
        self.up = {}
        self.over = {}

    def block(self, level, slot):
        place = self.place
        side = place.y if slot == 0 else place.other
        return 2 * (place.z - self.sign * level) + side

    def begin(self):
        comm, place, part = self.comm, self.place, self.part
        near, far = part(place.seq, place.y), part(place.seq, place.other)
        mine = self.own(place.y)
        self.lend = comm.copy(self.own(place.other), far, place.pair, self.inside & (self.more | self.leads))
        self.up[1, 0] = comm.copy(mine, near, self.next, self.more)
        self.give = comm.copy(mine, near, place.pair, self.inside & self.leads)

    def pass_pair(self):
        comm, place, part = self.comm, self.place, self.part
        follows = jnp.logical_not(self.leads)
        wait_for(self.lend, self.inside & (self.more | follows))
        lent = part(self.block(0, 1), place.y)
        self.up[1, 1] = comm.copy(lent, lent, self.next, self.more)

    def have_pair(self):
        wait_for(self.give, self.inside & jnp.logical_not(self.leads))

    def pass_level(self, level):
        comm, place, part = self.comm, self.place, self.part
        here = self.inside & (self.rank >= level)
        for slot in range(2):
            half = part(self.block(level, slot), place.y)
            wait_for(self.up[level, slot], here)
            if level < LINE - 1:
                self.up[level + 1, slot] = comm.copy(half, half, self.next, here & self.more)
            self.over[level, slot] = comm.copy(half, half, place.pair, here)

    def have_level(self, level):
        here = self.inside & (self.rank >= level)
        for slot in range(2):
            wait_for(self.over[level, slot], here)


def greet(partners):
    barrier = pltpu.get_barrier_semaphore()
    count = jnp.int32(0)
    for device, when in partners:
        def tell(device=device):
            pl.semaphore_signal(barrier, inc=1, device_id=device, device_id_type=MESH)

        if when is None:
            tell()
            count = count + 1
        else:
            pl.when(when)(tell)
            count = count + when.astype(jnp.int32)
    pl.semaphore_wait(barrier, count)


def line_partners(place):
    return [
        (place.pair, None),
        ((place.seq + 2, place.head), place.z < LINE - 1),
        ((place.seq - 2, place.head), place.z > 0),
    ]


def head_partners(place):
    return [(place.sibling, None), (place.facing, None)]


def step_partners(place):
    return [
        ((place.seq + 1, place.head), (place.y == 1) & (place.z < LINE - 1)),
        ((place.seq - 1, place.head), (place.y == 0) & (place.z > 0)),
    ]


def front_kernel(
    ends,
    lengths,
    inputs,
    gain,
    shift,
    query_weight,
    key_weight,
    value_weight,
    query_kernel,
    key_kernel,
    value_kernel,
    output_weight,
    keyvals,
    queries,
    raw,
    attended,
    attended_turned,
    log_total,
    weights,
    joined,
    halo,
    rows_high,
    rows_low,
    query_cat,
    highest,
    summed,
    weighted,
    send_sems,
    recv_sems,
):
    place = Place()
    comm = Comm(send_sems, recv_sems)
    sequences, rows, model = inputs.shape
    channels = query_weight.shape[1]
    heads = channels // HSIZE
    edge = halo.shape[1]
    first = longer_first(lengths)
    order = (first, 1 - first)
    greet(line_partners(place) + head_partners(place) + step_partners(place))
    rim = comm.copy(
        inputs.at[:, pl.ds(rows - edge, edge)],
        halo,
        (place.seq + 1, place.head),
        place.seq < 2 * LINE - 1,
    )
    own_weight = rows_at(weights, place.head * channels, channels)
    own_weight[...] = output_weight[...]
    to_sibling = comm.copy(own_weight, own_weight, place.sibling)
    to_facing = comm.copy(own_weight, own_weight, place.facing)

    def normal(value):
        return unit_rows(value)[0] * gain[...] + shift[...]

    for i in range(sequences):
        high, low = split(normal(inputs[order[i]]))
        rows_high[pl.ds(i * rows, rows)] = high
        rows_low[pl.ds(i * rows, rows)] = low
    wait_for(rim, place.seq > 0)
    inner = (place.seq > 0).astype(jnp.float32)
    rim_rows = jnp.concatenate([normal(halo[order[i]]) for i in range(sequences)], 0)
    rim_split = split(rim_rows)
    for k, weight in enumerate((query_weight, key_weight, value_weight)):
        parts = split(weight[...])
        whole = dot_three((rows_high[...], rows_low[...]), parts, PLAIN)
        before = dot_three(rim_split, parts, PLAIN) * inner
        for i in range(sequences):
            raw[k, i, pl.ds(0, edge)] = before[i * edge : (i + 1) * edge]
            raw[k, i, pl.ds(edge, rows)] = whole[i * rows : (i + 1) * rows]

    def convolved(k, i, kernel):
        return (
            kernel[0:1] * raw[k, i, pl.ds(edge, rows)]
            + kernel[1:2] * raw[k, i, pl.ds(edge - 1, rows)]
            + kernel[2:3] * raw[k, i, pl.ds(edge - 2, rows)]
        )

    spreads = []
    for i in range(sequences):
        own = keyvals.at[place.seq, i]
        own[:, 0:channels] = convolved(1, i, key_kernel)
        own[:, channels : 2 * channels] = convolved(2, i, value_kernel)

        def part(block, half, i=i):
            return keyvals.at[block, i, pl.ds(pl.multiple_of(half * (rows // 2), 8), rows // 2)]

        spreads.append(Spread(comm, place, part, ends[i]))
        spreads[i].begin()
    for i in range(sequences):
        query = convolved(0, i, query_kernel).T
        queries[i] = query
        for head in range(heads):
            query_cat[i, head] = against(query[head_lanes(head)] * HSIZE ** (-0.5))
    to_facing.wait_recv()
    theirs = rows_at(weights, place.facing[1] * channels, channels)
    to_last = comm.copy(theirs, theirs, place.sibling)

    def attend(i, block, diagonal):
        own = keyvals.at[block, i]
        for head in range(heads):
            scores = dot(beside(own[:, head_lanes(head)]), query_cat[i, head], PLAIN)
            lane = pl.ds(head, 1)
            if diagonal:
                key_pos = lax.broadcasted_iota(jnp.int32, scores.shape, 0)
                query_pos = lax.broadcasted_iota(jnp.int32, scores.shape, 1)
                scores = jnp.where(key_pos <= query_pos, scores, NEGATIVE)
                high = jnp.max(scores, 0, keepdims=True)
            else:
                old = highest[i, lane]
                high = jnp.maximum(old, jnp.max(scores, 0, keepdims=True))
            powers = jnp.exp(scores - high)
            total = jnp.sum(powers, 0, keepdims=True)
            power_high, power_low = split(powers)
            value_high, value_low = split(own[:, head_lanes(head, channels)])
            both = dot(jnp.concatenate([value_high, value_low], 1), power_high, BOTH_FIRST)
            term = both[:HSIZE] + both[HSIZE:] + dot(value_high, power_low, BOTH_FIRST)
            at = pl.ds(head * HSIZE, HSIZE)
            if diagonal:
                summed[i, lane] = total
                weighted[i, at] = term
            else:
                scale = jnp.exp(old - high)
                summed[i, lane] = summed[i, lane] * scale + total
                weighted[i, at] = weighted[i, at] * scale + term
            highest[i, lane] = high

    def here(i):
        return place.z < ends[i]

    def both(body):
        def step(i, carry):
            body(i)
            return carry

        lax.fori_loop(0, sequences, step, 0)

    for k, weight in enumerate((query_weight, key_weight, value_weight)):
        joined[k * channels : (k + 1) * channels] = weight[...].T
    for spread in spreads:
        spread.pass_pair()
    both(lambda i: attend(i, place.seq, True))
    for spread in spreads:
        spread.have_pair()

    for level in range(LINE):
        if level:
            for spread in spreads:
                spread.pass_level(level)
            for spread in spreads:
                spread.have_level(level)

        def blocks(k, carry, level=level):
            i, slot = k // 2, k % 2
            block = 2 * (place.z - level) + slot
            limit = jnp.where(i == 0, ends[0], ends[1])
            if level:
                wanted = (place.z >= level) & (place.z < limit)
            else:
                wanted = (slot == 0) & (place.y == 1) & (place.z < limit)

            @pl.when(wanted)
            def _():
                attend(i, block, False)

            return carry

        lax.fori_loop(0, 2 * sequences, blocks, 0)

    for i in range(sequences):
        live = jnp.minimum(lengths[order[i]] - place.seq * rows, rows)
        alive = (lax.broadcasted_iota(jnp.int32, (1, rows), 1) < live).astype(jnp.float32)
        for head in range(heads):
            at = pl.ds(head * HSIZE, HSIZE)
            total = summed[i, pl.ds(head, 1)]
            weighted[i, at] = weighted[i, at] * (alive / total)
            log_total[i, pl.ds(head, 1)] = highest[i, pl.ds(head, 1)] + jnp.log(total)
        attended_turned[i] = weighted[i]
        attended[:, i * channels : (i + 1) * channels] = weighted[i].T
    to_sibling.wait_recv()
    to_last.wait_recv()
    comm.finish()


def front(ends, lengths, inputs, gain, shift, weights, kernels, output_weight):
    sequences, rows, model = inputs.shape
    channels = weights[0].shape[1]
    heads = channels // HSIZE
    blocks = lax.axis_size("seq")
    groups = lax.axis_size("head")
    edge = 8
    vmem = pl.BlockSpec(memory_space=pltpu.VMEM)

    def f32(*shape):
        return jax.ShapeDtypeStruct(shape, jnp.float32)

    copies = 64
    return pl.pallas_call(
        functools.partial(front_kernel, ends),
        out_shape=[
            f32(blocks, sequences, rows, 2 * channels),
            f32(sequences, channels, rows),
            f32(3, sequences, rows + edge, channels),
            f32(rows, sequences * channels),
            f32(sequences, channels, rows),
            f32(sequences, 8, rows),
            f32(groups * channels, model),
            f32(3 * channels, model),
        ],
        in_specs=[pl.BlockSpec(memory_space=pltpu.SMEM)] + [vmem] * 10,
        out_specs=[vmem] * 8,
        scratch_shapes=[
            pltpu.VMEM((sequences, edge, model), jnp.float32),
            pltpu.VMEM((sequences * rows, model), jnp.bfloat16),
            pltpu.VMEM((sequences * rows, model), jnp.bfloat16),
            pltpu.VMEM((sequences, heads, 3 * HSIZE, rows), jnp.bfloat16),
            pltpu.VMEM((sequences, 8, rows), jnp.float32),
            pltpu.VMEM((sequences, 8, rows), jnp.float32),
            pltpu.VMEM((sequences, channels, rows), jnp.float32),
            pltpu.SemaphoreType.DMA((copies,)),
            pltpu.SemaphoreType.DMA((copies,)),
        ],
        compiler_params=pltpu.CompilerParams(
            collective_id=1, has_side_effects=True, vmem_limit_bytes=60 * 2**20
        ),
        name="front",
    )(lengths, inputs, gain[None], shift[None], *weights, *kernels, output_weight)


class HeadSum:
    def __init__(self, comm, place, partial, from_sibling, from_facing, rows, pieces=4):
        self.comm, self.place, self.partial = comm, place, partial
        self.from_sibling, self.from_facing = from_sibling, from_facing
        self.rows, self.pieces = rows, pieces
        self.size = rows // pieces
        self.near = rows_at(partial, place.core * rows, rows)

    def lend(self):
        far = rows_at(self.partial, (1 - self.place.core) * self.rows, self.rows)
        self.lent = self.comm.copy(far, self.from_sibling, self.place.sibling)

    def chip(self):
        self.lent.wait_recv()
        self.near[...] = self.near[...] + self.from_sibling[...]
        self.sent = []
        for p in range(self.pieces):
            at = pl.ds(p * self.size, self.size)
            self.sent.append(self.comm.copy(self.near.at[at], self.from_facing.at[at], self.place.facing))

    def piece(self, p):
        self.sent[p].wait_recv()
        at = pl.ds(p * self.size, self.size)
        return self.near[at] + self.from_facing[at]


def norm_back(grad, gain, unit, inverse):
    scaled = grad * gain
    return inverse * (
        scaled - jnp.mean(scaled, -1, keepdims=True) - unit * jnp.mean(scaled * unit, -1, keepdims=True)
    )


def spread_steps(spreads):
    for spread in spreads:
        spread.begin()
    yield
    for spread in spreads:
        spread.pass_pair()
    yield
    for level in range(1, LINE):
        for spread in spreads:
            spread.pass_level(level)
        yield


TILE = 256


def tiles(width, body):
    def step(j, carry):
        body(pl.ds(pl.multiple_of(j * TILE, TILE), TILE))
        return carry

    lax.fori_loop(0, width // TILE, step, 0)


def down_rows(value):
    return jnp.sum(value, 0, keepdims=True)


def allowed_from(shape, offset):
    key_pos = lax.broadcasted_iota(jnp.int32, shape, 0)
    query_pos = lax.broadcasted_iota(jnp.int32, shape, 1)
    return key_pos <= query_pos + offset


def back_kernel(
    ends,
    plan,
    lengths,
    inputs,
    cotangent,
    attended,
    attended_turned,
    queries,
    log_total,
    output_weight,
    output_bias,
    first_gain,
    first_shift,
    second_gain,
    second_shift,
    hidden_bias,
    outer_bias,
    query_kernel,
    key_kernel,
    value_kernel,
    keyvals,
    weights,
    inner_weight,
    outer_weight,
    joined,
    raw_far,
    result,
    grad_inputs,
    outer_out,
    inner_out,
    rest_out,
    late_out,
    all_queries,
    all_grads,
    weight_a,
    weight_b,
    weight_c,
    raw,
    groups,
    normed_two,
    active,
    grad_hidden,
    grad_normed,
    from_sibling,
    from_facing,
    grad_outer,
    grad_inner,
    grad_rest,
    land_ref,
    key_slots,
    own_keys,
    query_slots,
    grad_slots,
    query_cat,
    grad_cat,
    key_cat,
    value_cat,
    grad_att,
    grad_query,
    grad_keyval,
    grad_conv,
    late_from,
    late_all,
    send_sems,
    recv_sems,
    local_sems,
    slot_sems,
):
    place = Place()
    comm = Comm(send_sems, recv_sems, local_sems)
    land = Land(land_ref)
    crew = Crew()
    sequences, rows, model = inputs.shape
    channels = output_weight.shape[0]
    heads = channels // HSIZE
    hidden_units = hidden_bias.shape[1]
    tokens = sequences * rows
    z, y, seq, core = place.z, place.y, place.seq, place.core
    first = longer_first(lengths)
    order = (first, 1 - first)
    devices = 2 * LINE
    column = [((lax.rem(seq + k, devices), place.head), None) for k in range(1, devices)]
    greet(column + head_partners(place))

    load_a = comm.local(weights, weight_a, keep=False)
    load_b = comm.local(inner_weight, weight_b, keep=False)
    load_c = comm.local(outer_weight, weight_c, keep=False)
    load_raw = comm.local(raw_far, raw, keep=False)
    load_own = [comm.local(keyvals.at[seq, i], own_keys.at[i], keep=False) for i in range(sequences)]
    keep_query = [comm.local(queries.at[i], all_queries.at[seq, i], keep=False) for i in range(sequences)]

    to_sibling = comm.copy(attended, groups.at[place.head], place.sibling)
    to_facing = comm.copy(attended, groups.at[place.head], place.facing)

    def query_part(block, half, i):
        return all_queries.at[block, i, pl.ds(pl.multiple_of(half * (channels // 2), 8), channels // 2)]

    def grad_part(block, half, i):
        size = grad_att.shape[1] // 2
        return all_grads.at[block, i, pl.ds(pl.multiple_of(half * size, 8), size)]

    def query_own(half, i):
        return queries.at[i, pl.ds(pl.multiple_of(half * (channels // 2), 8), channels // 2)]

    def grad_own(half, i):
        size = grad_att.shape[1] // 2
        return grad_att.at[i, pl.ds(pl.multiple_of(half * size, 8), size)]

    query_spreads = [
        Spread(
            comm,
            place,
            functools.partial(query_part, i=i),
            ends[i],
            False,
            functools.partial(query_own, i=i),
        )
        for i in range(sequences)
    ]
    grad_spreads = [
        Spread(
            comm,
            place,
            functools.partial(grad_part, i=i),
            ends[i],
            False,
            functools.partial(grad_own, i=i),
        )
        for i in range(sequences)
    ]
    crew.add(spread_steps(query_spreads))
    crew.advance()

    def chunk(i):
        return pl.ds(i * rows, rows)

    def add_group(ref, weight_ref, total, begin):
        parts = split(weight_ref[...])
        for i in range(sequences):
            piece = split(ref[:, i * channels : (i + 1) * channels])
            term = dot_three(piece, parts, PLAIN)
            total[chunk(i)] = term if begin else total[chunk(i)] + term

    add_group(attended, output_weight, grad_inputs, True)
    crew.advance()
    load_a.wait()

    def group_weight(group):
        return rows_at(weight_a, group * channels, channels)

    sibling, facing = place.sibling[1], place.facing[1]
    last = facing + 1 - 2 * (facing % 2)
    to_sibling.wait_recv()
    add_group(groups.at[sibling], group_weight(sibling), grad_inputs, False)
    to_facing.wait_recv()
    onward = comm.copy(groups.at[facing], groups.at[facing], place.sibling)
    add_group(groups.at[facing], group_weight(facing), result, True)
    crew.advance()
    onward.wait_recv()
    add_group(groups.at[last], group_weight(last), result, False)

    for i in range(sequences):
        result[chunk(i)] = inputs[order[i]] + output_bias[...] + (grad_inputs[chunk(i)] + result[chunk(i)])
        normed_two[chunk(i)] = unit_rows(result[chunk(i)])[0] * second_gain[...] + second_shift[...]
    load_b.wait()
    load_c.wait()

    def cot_columns(columns):
        return jnp.concatenate([cotangent[order[i], :, columns] for i in range(sequences)], 0)

    normed_parts = split(normed_two[...])
    cot_parts = split(jnp.concatenate([cotangent[order[i]] for i in range(sequences)], 0))

    def hidden_tile(columns):
        hidden = dot_three(normed_parts, split(weight_b[:, columns]), PLAIN) + hidden_bias[:, columns]
        rectified = jnp.maximum(hidden, 0.0)
        grad_active = dot_three(cot_parts, split(weight_c[columns]), BOTH_LAST)
        grad = grad_active * (2.0 * rectified)
        active[:, columns] = rectified * rectified
        grad_hidden[:, columns] = grad
        grad_rest[4 * channels + 2 : 4 * channels + 3, columns] = down_rows(grad)

    tiles(hidden_units, hidden_tile)
    crew.advance()

    def grad_normed_chunk(which):
        at = pl.ds(pl.multiple_of(which * rows, rows), rows)
        parts = split(grad_hidden[at])

        def tile(columns):
            grad_normed[at, columns] = dot_three(parts, split(weight_b[columns]), BOTH_LAST)

        tiles(model, tile)

    second_sum = HeadSum(comm, place, grad_normed, from_sibling.at[0], from_facing.at[0], rows)
    grad_normed_chunk(1 - core)
    second_sum.lend()
    grad_normed_chunk(core)
    second_sum.chip()

    active_parts = split(active[...])

    def outer_tile(columns):
        grad_outer[:, columns] = dot_three(active_parts, split(cot_columns(columns)), BOTH_FIRST)

    tiles(model, outer_tile)
    for pair_first, which, start, count in plan:
        if which == 0:
            crew.add(sum_pair_first(comm, place, land, grad_outer, outer_out, start, count))
    crew.advance()

    normed_parts = split(normed_two[...])

    def inner_tile(columns):
        grad_inner[:, columns] = dot_three(normed_parts, split(grad_hidden[:, columns]), BOTH_FIRST)

    tiles(hidden_units, inner_tile)
    for pair_first, which, start, count in plan:
        if which == 1:
            crew.add(sum_line_first(comm, place, land, grad_inner, inner_out, start, count))
    crew.advance()

    outer_term = weight_a.at[pl.ds(0, tokens)]

    def outer_term_tile(columns):
        outer_term[:, columns] = dot_three(active_parts, split(weight_c[:, columns]), PLAIN)

    tiles(model, outer_term_tile)
    load_joined = comm.local(joined, weight_c.at[pl.ds(0, 3 * channels)], keep=False)

    late_out[...] = jnp.zeros_like(late_out)
    swaps = []

    def own_piece(p, size):
        return pl.ds(pl.multiple_of(core * rows + p * size, 8), size)

    for p in range(second_sum.pieces):
        at = own_piece(p, second_sum.size)
        incoming = second_sum.piece(p)
        unit, inverse = unit_rows(result[at])
        through = norm_back(incoming, second_gain[...], unit, inverse)
        here = pl.ds(p * second_sum.size, second_sum.size)
        cot = jnp.where(core == 0, cotangent[order[0], here], cotangent[order[1], here])
        grad_inputs[at] = cot + through
        late_out[2:3] = late_out[2:3] + down_rows(incoming * unit)
        late_out[3:4] = late_out[3:4] + down_rows(incoming)
        swaps.append(comm.copy(grad_inputs.at[at], grad_inputs.at[at], place.sibling))
    result_sum = HeadSum(comm, place, outer_term, from_sibling.at[1], from_facing.at[1], rows)
    result_sum.lend()
    for made in swaps:
        made.wait_recv()

    weight_parts = split(output_weight[...])
    grad_att[:, channels:] = jnp.zeros((sequences, grad_att.shape[1] - channels, rows), jnp.float32)
    for i in range(sequences):
        live = jnp.minimum(lengths[order[i]] - seq * rows, rows)
        alive = (lax.broadcasted_iota(jnp.int32, (1, rows), 1) < live).astype(jnp.float32)
        grad = dot_three(weight_parts, split(grad_inputs[chunk(i)]), BOTH_LAST) * alive
        grad_att[i, 0:channels] = grad
        both = grad * attended_turned[i]
        for head in range(heads):
            at = channels + head
            grad_att[i, at : at + 1] = log_total[i, head : head + 1]
            grad_att[i, at + heads : at + heads + 1] = down_rows(both[head_lanes(head)])
    keep_grad = [comm.local(grad_att.at[i], all_grads.at[seq, i], keep=False) for i in range(sequences)]
    for spread in grad_spreads:
        spread.begin()
    result_sum.chip()
    for i in range(sequences):
        for head in range(heads):
            query_cat[i, head] = against(queries[i, head_lanes(head)] * HSIZE ** (-0.5))
            grad_cat[i, head] = against(grad_att[i, head_lanes(head)])
    output_grad = jnp.zeros((channels, model), jnp.float32)
    for i in range(sequences):
        output_grad = output_grad + dot_three(split(attended_turned[i]), split(grad_inputs[chunk(i)]), PLAIN)
    grad_rest[0:channels] = output_grad
    base = 4 * channels
    grad_rest[base : base + 1] = down_rows(grad_inputs[...])
    outer_row = jnp.zeros((1, model), jnp.float32)
    for i in range(sequences):
        outer_row = outer_row + down_rows(cotangent[order[i]])
    grad_rest[base + 1 : base + 2] = outer_row
    for pair_first, which, start, count in plan:
        if which == 2 and start < channels:
            make = sum_pair_first if pair_first else sum_line_first
            crew.add(make(comm, place, land, grad_rest, rest_out, start, count))
    for spread in grad_spreads:
        spread.pass_pair()
    crew.advance()

    grad_query[...] = jnp.zeros_like(grad_query)
    grad_keyval[...] = jnp.zeros_like(grad_keyval)

    def query_side(i):
        count = jnp.where(z < ends[i], seq + 1, 0)

        def load(slot, block):
            return pltpu.make_async_copy(keyvals.at[block, i], key_slots.at[slot], slot_sems.at[slot])

        pl.when(count > 0)(lambda: load(0, seq).start())

        def step(t, carry):
            slot = lax.rem(t, 2)
            load(slot, seq - t).wait()
            pl.when(t + 1 < count)(lambda: load(1 - slot, seq - t - 1).start())
            block = key_slots.at[slot]
            for head in range(heads):
                key_high, key_low = split(block[:, head_lanes(head)])
                scores = dot(jnp.concatenate([key_high, key_high, key_low], 1), query_cat[i, head], PLAIN)
                at = channels + head
                scores = scores - grad_att[i, at : at + 1]
                powers = jnp.exp(jnp.where(allowed_from(scores.shape, t * rows), scores, NEGATIVE))
                slopes = dot(beside(block[:, head_lanes(head, channels)]), grad_cat[i, head], PLAIN)
                slopes = powers * (slopes - grad_att[i, at + heads : at + heads + 1])
                high, low = split(slopes)
                both = dot(jnp.concatenate([key_high, key_low], 1), high, BOTH_FIRST)
                term = both[:HSIZE] + both[HSIZE:] + dot(key_high, low, BOTH_FIRST)
                grad_query[i, head_lanes(head)] = grad_query[i, head_lanes(head)] + term
            return carry

        lax.fori_loop(0, count, step, 0)

    def key_side(i, offset, query_ref, grad_ref):
        for head in range(heads):
            lanes = head_lanes(head)
            query_high, query_low = split(query_ref[lanes] * HSIZE ** (-0.5))
            grad_high, grad_low = split(grad_ref[lanes])
            scores = dot(
                key_cat[i, head, :, 0 : 3 * HSIZE],
                jnp.concatenate([query_high, query_low, query_high], 0),
                PLAIN,
            )
            at = channels + head
            scores = scores - grad_ref[at : at + 1]
            powers = jnp.exp(jnp.where(allowed_from(scores.shape, offset), scores, NEGATIVE))
            slopes = dot(
                value_cat[i, head, :, 0 : 3 * HSIZE],
                jnp.concatenate([grad_high, grad_low, grad_high], 0),
                PLAIN,
            )
            slopes = powers * (slopes - grad_ref[at + heads : at + heads + 1])
            for base, (far_high, far_low), value in (
                (0, (query_high, query_low), slopes),
                (channels, (grad_high, grad_low), powers),
            ):
                high, low = split(value)
                both = dot(jnp.concatenate([far_high, far_low], 0), high, BOTH_LAST)
                term = both[:HSIZE] + both[HSIZE:] + dot(far_high, low, BOTH_LAST)
                where = slice(base + head * HSIZE, base + (head + 1) * HSIZE)
                grad_keyval[i, where] = grad_keyval[i, where] + term

    def key_level(level, pairs):
        items = [(i, slot) for i in range(sequences) for slot in range(2)]

        def inside(i):
            return z + level < jnp.where(i == 0, ends[0], ends[1])

        def wanted(t):
            i, slot = t // 2, t % 2
            if level:
                return inside(i)
            if pairs:
                return inside(i) & (slot == 1) & (y == 0)
            return inside(i) & (slot == y)

        def loads(t):
            i, slot = t // 2, t % 2
            block = 2 * (z + level) + slot
            return (
                pltpu.make_async_copy(all_queries.at[block, i], query_slots.at[t], slot_sems.at[2 * t]),
                pltpu.make_async_copy(all_grads.at[block, i], grad_slots.at[t], slot_sems.at[2 * t + 1]),
            )

        for t in range(len(items)):
            @pl.when(wanted(t))
            def _(t=t):
                for made in loads(t):
                    made.start()

        def step(t, carry):
            @pl.when(wanted(t))
            def _():
                for made in loads(t):
                    made.wait()
                i, slot = t // 2, t % 2
                offset = (2 * (z + level) + slot - seq) * rows
                key_side(i, offset, query_slots.at[t], grad_slots.at[t])

            return carry

        lax.fori_loop(0, len(items), step, 0)

    query_side(0)
    crew.advance()
    for spread in grad_spreads:
        spread.pass_level(1)
    query_side(1)
    crew.advance()
    for p in range(result_sum.pieces):
        at = own_piece(p, result_sum.size)
        result[at] = result[at] + outer_bias[...] + result_sum.piece(p)
        swaps.append(comm.copy(result.at[at], result.at[at], place.sibling))
    for i in range(sequences):
        load_own[i].wait()
        for head in range(heads):
            key_cat[i, head, :, 0 : 3 * HSIZE] = beside(own_keys[i, :, head_lanes(head)])
            value_cat[i, head, :, 0 : 3 * HSIZE] = beside(own_keys[i, :, head_lanes(head, channels)])
        keep_query[i].wait()
        keep_grad[i].wait()
    key_level(0, False)
    crew.advance()
    for spread in grad_spreads:
        spread.pass_level(2)
    for spread in query_spreads + grad_spreads:
        spread.have_pair()
    key_level(0, True)
    crew.advance()
    for level in range(1, LINE):
        if level == 2:
            for spread in grad_spreads:
                spread.pass_level(3)
        for spread in query_spreads + grad_spreads:
            spread.have_level(level)
        key_level(level, False)
        crew.advance()

    edge = grad_conv.shape[2] - rows
    for i in range(sequences):
        grad_conv[0, i, pl.ds(0, rows)] = (grad_query[i] * HSIZE ** (-0.5)).T
        grad_conv[1, i, pl.ds(0, rows)] = grad_keyval[i, 0:channels].T
        grad_conv[2, i, pl.ds(0, rows)] = grad_keyval[i, channels : 2 * channels].T

    @pl.when(seq == devices - 1)
    def _():
        grad_conv[:, :, pl.ds(rows, edge)] = jnp.zeros((3, sequences, edge, channels), jnp.float32)

    before = (seq - 1, place.head)
    rim = comm.copy(
        grad_conv.at[:, :, pl.ds(0, edge)], grad_conv.at[:, :, pl.ds(rows, edge)], before, seq > 0
    )
    load_raw.wait()
    base = 4 * channels + 3
    grad_rest[base : base + 13] = jnp.zeros((13, model), jnp.float32)
    for k in range(3):
        for j in range(3):
            total = jnp.zeros((1, channels), jnp.float32)
            for i in range(sequences):
                total = total + down_rows(grad_conv[k, i, pl.ds(0, rows)] * raw[k, i, pl.ds(edge - j, rows)])
            grad_rest[base + j : base + j + 1, k * channels : (k + 1) * channels] = total
    wait_for(rim, seq < devices - 1)
    for k, kernel in enumerate((query_kernel, key_kernel, value_kernel)):
        for i in range(sequences):
            grad_hidden[chunk(i), k * channels : (k + 1) * channels] = (
                kernel[0:1] * grad_conv[k, i, pl.ds(0, rows)]
                + kernel[1:2] * grad_conv[k, i, pl.ds(1, rows)]
                + kernel[2:3] * grad_conv[k, i, pl.ds(2, rows)]
            )
    load_joined.wait()

    def first_chunk(which):
        at = pl.ds(pl.multiple_of(which * rows, rows), rows)
        parts = split(grad_hidden[at, 0 : 3 * channels])

        def tile(columns):
            active[at, columns] = dot_three(parts, split(weight_c[0 : 3 * channels, columns]), PLAIN)

        tiles(model, tile)

    first_sum = HeadSum(comm, place, active, from_sibling.at[2], from_facing.at[2], rows)
    first_chunk(1 - core)
    first_sum.lend()
    first_chunk(core)
    first_sum.chip()
    for i in range(sequences):
        normed_two[chunk(i)] = unit_rows(inputs[order[i]])[0] * first_gain[...] + first_shift[...]
    projected_parts = split(grad_hidden[:, 0 : 3 * channels])

    def joined_tile(columns):
        grad_rest[channels : 4 * channels, columns] = dot_three(
            projected_parts, split(normed_two[:, columns]), BOTH_FIRST
        )

    tiles(model, joined_tile)
    for pair_first, which, start, count in plan:
        if which == 2 and start >= channels:
            make = sum_pair_first if pair_first else sum_line_first
            crew.add(make(comm, place, land, grad_rest, rest_out, start, count))
    crew.advance()
    crew.advance()

    pieces = swaps[: second_sum.pieces]
    for made in pieces:
        comm.settle(made)
    returned = []
    for p in range(first_sum.pieces):
        at = own_piece(p, first_sum.size)
        incoming = first_sum.piece(p)
        here = pl.ds(p * first_sum.size, first_sum.size)
        rows_in = jnp.where(core == 0, inputs[order[0], here], inputs[order[1], here])
        unit, inverse = unit_rows(rows_in)
        grad_inputs[at] = grad_inputs[at] + norm_back(incoming, first_gain[...], unit, inverse)
        late_out[0:1] = late_out[0:1] + down_rows(incoming * unit)
        late_out[1:2] = late_out[1:2] + down_rows(incoming)
        returned.append(comm.copy(grad_inputs.at[at], grad_inputs.at[at], place.sibling))
    late_sent = comm.copy(late_out, late_from, place.sibling)
    crew.advance()
    late_sent.wait_recv()
    late_all[seq] = late_out[...] + late_from[...]
    mine = late_all.at[seq]
    shared = [comm.copy(mine, mine, device) for device, _ in column]
    crew.drain()
    for made in swaps[second_sum.pieces :] + returned + shared:
        made.wait_recv()
    comm.settle(late_sent)
    total = late_all[0]
    for k in range(1, devices):
        total = total + late_all[k]
    late_out[...] = total
    comm.finish()


def back(ends, lengths, inputs, cotangent, kept, vectors, kernels, inner_weight, outer_weight, output_weight):
    keyvals, queries, raw, attended, attended_turned, log_total, weights, joined = kept
    sequences, rows, model = inputs.shape
    channels = output_weight.shape[0]
    heads = channels // HSIZE
    hidden_units = inner_weight.shape[1]
    tokens = sequences * rows
    devices = lax.axis_size("seq")
    rest_rows = 4 * channels + 16
    plan = (
        [(True, 0, k * 192, 192) for k in range(hidden_units // 192)]
        + [(False, 1, k * 192, 192) for k in range(model // 192)]
        + [(True, 2, 0, 96), (False, 2, 96, 96)]
        + [(True, 2, 192, 96), (True, 2, 288, 96), (True, 2, 384, 96)]
        + [(False, 2, 480, 96), (False, 2, 576, 96), (False, 2, 672, 112)]
    )
    land_rows = sum(3 * count // 2 if pair_first else 2 * count for pair_first, _, _, count in plan)
    vmem = pl.BlockSpec(memory_space=pltpu.VMEM)
    far = pl.BlockSpec(memory_space=pl.ANY)

    def f32(*shape):
        return jax.ShapeDtypeStruct(shape, jnp.float32)

    def room(*shape, dtype=jnp.float32):
        return pltpu.VMEM(shape, dtype)

    edge = 8
    grad_rows = channels + 16
    half = functools.partial(room, dtype=jnp.bfloat16)
    return pl.pallas_call(
        functools.partial(back_kernel, ends, plan),
        out_shape=[
            f32(tokens, model),
            f32(tokens, model),
            f32(hidden_units, model),
            f32(model, hidden_units),
            f32(rest_rows, model),
            f32(8, model),
            f32(devices, sequences, channels, rows),
            f32(devices, sequences, grad_rows, rows),
        ],
        in_specs=[pl.BlockSpec(memory_space=pltpu.SMEM)] + [vmem] * 17 + [far] * 6,
        out_specs=[vmem] * 2 + [far] * 3 + [vmem] + [far] * 2,
        scratch_shapes=[
            room(model, model),
            room(model, hidden_units),
            room(hidden_units, model),
            room(3, sequences, rows + edge, channels),
            room(4, rows, sequences * channels),
            room(tokens, model),
            room(tokens, hidden_units),
            room(tokens, hidden_units),
            room(tokens, model),
            room(3, rows, model),
            room(3, rows, model),
            room(hidden_units, model),
            room(model, hidden_units),
            room(rest_rows, model),
            room(land_rows, model),
            room(2, rows, 2 * channels),
            room(sequences, rows, 2 * channels),
            room(2 * sequences, channels, rows),
            room(2 * sequences, grad_rows, rows),
            half(sequences, heads, 3 * HSIZE, rows),
            half(sequences, heads, 3 * HSIZE, rows),
            half(sequences, heads, rows, 256),
            half(sequences, heads, rows, 256),
            room(sequences, grad_rows, rows),
            room(sequences, channels, rows),
            room(sequences, 2 * channels, rows),
            room(3, sequences, rows + edge, channels),
            room(8, model),
            room(devices, 8, model),
            pltpu.SemaphoreType.DMA((256,)),
            pltpu.SemaphoreType.DMA((256,)),
            pltpu.SemaphoreType.DMA((64,)),
            pltpu.SemaphoreType.DMA((4 * sequences,)),
        ],
        compiler_params=pltpu.CompilerParams(
            collective_id=2, has_side_effects=True, vmem_limit_bytes=63 * 2**20
        ),
        name="back",
    )(
        lengths,
        inputs,
        cotangent,
        attended,
        attended_turned,
        queries,
        log_total,
        output_weight,
        *[vector[None] for vector in vectors],
        *kernels,
        keyvals,
        weights,
        inner_weight,
        outer_weight,
        joined,
        raw,
    )


def shards(
    inputs,
    seq_lengths,
    first_gain,
    first_shift,
    query_weight,
    key_weight,
    value_weight,
    query_kernel,
    key_kernel,
    value_kernel,
    output_weight,
    output_bias,
    second_gain,
    second_shift,
    inner_weight,
    hidden_layer_bias,
    outer_weight,
    outer_bias,
    cotangent,
):
    channels = query_weight.shape[1]
    kernels = (query_kernel, key_kernel, value_kernel)
    ends = (LINE, LINE)
    kept = front(
        ends,
        seq_lengths,
        inputs,
        first_gain,
        first_shift,
        (query_weight, key_weight, value_weight),
        kernels,
        output_weight,
    )
    result, grad_inputs, grad_outer, grad_inner, rest, late, _, _ = back(
        ends,
        seq_lengths,
        inputs,
        cotangent,
        kept,
        (
            output_bias,
            first_gain,
            first_shift,
            second_gain,
            second_shift,
            hidden_layer_bias,
            outer_bias,
        ),
        kernels,
        inner_weight,
        outer_weight,
        output_weight,
    )
    swap = seq_lengths[1] > seq_lengths[0]

    def placed(array):
        array = array.reshape(inputs.shape)
        return jnp.where(swap, jnp.flip(array, 0), array)

    vectors = rest[4 * channels :]
    mixes = vectors[3:6, : 3 * channels]
    return (
        placed(result),
        placed(grad_inputs),
        late[0],
        late[1],
        rest[channels : 2 * channels].T,
        rest[2 * channels : 3 * channels].T,
        rest[3 * channels : 4 * channels].T,
        mixes[:, :channels],
        mixes[:, channels : 2 * channels],
        mixes[:, 2 * channels :],
        rest[:channels],
        vectors[0],
        late[2],
        late[3],
        grad_inner,
        vectors[2],
        grad_outer,
        vectors[1],
    )


def solution(mesh):
    lines = mesh.shape["seq"] == 2 * LINE and mesh.shape["head"] == 4
    return jax.shard_map(
        shards if lines else general_shards,
        mesh=mesh,
        in_specs=(
            P(None, "seq", None),
            P(),
            P(),
            P(),
            P(None, "head"),
            P(None, "head"),
            P(None, "head"),
            P(None, "head"),
            P(None, "head"),
            P(None, "head"),
            P("head", None),
            P(),
            P(),
            P(),
            P(None, "head"),
            P("head"),
            P("head", None),
            P(),
            P(None, "seq", None),
        ),
        out_specs=(
            P(None, "seq", None),
            P(None, "seq", None),
            P(),
            P(),
            P(None, "head"),
            P(None, "head"),
            P(None, "head"),
            P(None, "head"),
            P(None, "head"),
            P(None, "head"),
            P("head", None),
            P(),
            P(),
            P(),
            P(None, "head"),
            P("head"),
            P("head", None),
            P(),
        ),
        check_vma=False,
    )
```

```python
import functools

import jax
import jax.numpy as jnp
from jax import lax
from jax.experimental import pallas as pl
from jax.experimental.pallas import tpu as pltpu
from jax.sharding import PartitionSpec as P

MESH = pl.DeviceIdType.MESH

HSIZE = 64


EXACT_FLOAT_MODE = lax.Precision.HIGH
EPSILON = 1e-05
NEGATIVE = -1e30


def shifted(block, axis, distance):
    devices = range(lax.axis_size(axis))
    route = [(i - distance, i) for i in devices if i - distance in devices]
    return lax.ppermute(block, axis, route)


def matmul(input_operand, weight_matrix):
    return jnp.einsum("scd,df->scf", input_operand, weight_matrix, precision=EXACT_FLOAT_MODE)


def transposed(input_operand, weight_matrix):
    return jnp.einsum("scf,df->scd", input_operand, weight_matrix, precision=EXACT_FLOAT_MODE)


def outer_sum(first_rows, second_rows):
    return jnp.einsum("scd,scf->df", first_rows, second_rows, precision=EXACT_FLOAT_MODE)


def normalize(stream, norm_gain, norm_shift):
    centered = stream - jnp.mean(stream, -1, keepdims=True)
    inverse = lax.rsqrt(jnp.mean(centered * centered, -1, keepdims=True) + EPSILON)
    unit_rows = centered * inverse
    return (unit_rows * norm_gain + norm_shift, unit_rows, inverse)


def normalize_back(gradient, norm_gain, unit_rows, inverse):
    scaled = gradient * norm_gain
    middle = (
        scaled
        - jnp.mean(scaled, -1, keepdims=True)
        - unit_rows * jnp.mean(scaled * unit_rows, -1, keepdims=True)
    )
    return (inverse * middle, jnp.sum(gradient * unit_rows, (0, 1)), jnp.sum(gradient, (0, 1)))


def split_heads(flat):
    return flat.reshape(flat.shape[0], flat.shape[1], flat.shape[2] // HSIZE, HSIZE)


def allowed_pairs(query_pos, key_pos, lengths):
    return (key_pos[None, None, :] <= query_pos[None, :, None]) & (
        key_pos[None, None, :] < lengths[:, None, None]
    )


def pair_terms(queries, gradients, log_total, row_dots, query_pos, keyvals, key_pos, lengths):
    channels = queries.shape[2]
    query_heads = split_heads(queries)
    key_heads = split_heads(keyvals[:, :, :channels])
    value_heads = split_heads(keyvals[:, :, channels:])
    grad_heads = split_heads(gradients)
    scores = jnp.einsum(
        "sqhe,skhe->shqk", query_heads, key_heads, precision=EXACT_FLOAT_MODE
    ) * HSIZE ** (-0.5)
    allowed = allowed_pairs(query_pos, key_pos, lengths)[:, None]
    weight_values = jnp.exp(jnp.where(allowed, scores - log_total[..., None], NEGATIVE))
    weight_grads = jnp.einsum(
        "sqhe,skhe->shqk", grad_heads, value_heads, precision=EXACT_FLOAT_MODE
    )
    score_grads = weight_values * (weight_grads - row_dots[..., None])
    return (weight_values, score_grads, query_heads, key_heads, grad_heads)


def key_facing_term(terms, keyvals, channels):
    value_part = jnp.einsum("shqk,sqhe->skhe", terms[0], terms[4], precision=EXACT_FLOAT_MODE)
    key_part = jnp.einsum(
        "shqk,sqhe->skhe", terms[1], terms[2], precision=EXACT_FLOAT_MODE
    ) * HSIZE ** (-0.5)
    shape = (keyvals.shape[0], keyvals.shape[1], channels)
    return jnp.concatenate([key_part.reshape(shape), value_part.reshape(shape)], 2)


def query_side_term(terms):
    return jnp.einsum(
        "shqk,skhe->sqhe", terms[1], terms[3], precision=EXACT_FLOAT_MODE
    ) * HSIZE ** (-0.5)


def key_terms(queries, gradients, log_total, row_dots, query_pos, keyvals, key_pos, lengths):
    terms = pair_terms(
        queries, gradients, log_total, row_dots, query_pos, keyvals, key_pos, lengths
    )
    return key_facing_term(terms, keyvals, queries.shape[2])


def general_shards(
    inputs,
    seq_lengths,
    first_gain,
    first_shift,
    query_weight,
    key_weight,
    value_weight,
    query_kernel,
    key_kernel,
    value_kernel,
    output_weight,
    output_bias,
    second_gain,
    second_shift,
    inner_weight,
    hidden_layer_bias,
    outer_weight,
    outer_bias,
    cotangent,
):
    sequences, rows, model = inputs.shape
    channels = query_weight.shape[1]
    heads = channels // HSIZE
    positions = lax.axis_index("seq") * rows + jnp.arange(rows, dtype=jnp.int32)
    live_rows = (positions[None, :] < seq_lengths[:, None]).astype(jnp.float32)
    joined_weight = jnp.concatenate([query_weight, key_weight, value_weight], 1)
    joined_kernel = jnp.concatenate([query_kernel, key_kernel, value_kernel], 1)
    normed, leading_unit_value, first_inverse = normalize(inputs, first_gain, first_shift)
    projected = matmul(normed, joined_weight)
    rims = shifted(projected[:, rows - 2 :, :], "seq", 1)
    extended = jnp.concatenate([rims, projected], 1)
    convolved = (
        joined_kernel[0] * extended[:, 2:]
        + joined_kernel[1] * extended[:, 1:-1]
        + joined_kernel[2] * extended[:, :-2]
    )
    queries = convolved[:, :, :channels]
    keyvals = convolved[:, :, channels:]
    query_heads = split_heads(queries)
    portion = lax.all_gather(keyvals, "seq", axis=1, tiled=True)
    highest = jnp.full((sequences, heads, rows), NEGATIVE, jnp.float32)
    key_pos = jnp.arange(portion.shape[1], dtype=jnp.int32)
    key_heads = split_heads(portion[:, :, :channels])
    value_heads = split_heads(portion[:, :, channels:])
    scores = jnp.einsum(
        "sqhe,skhe->shqk", query_heads, key_heads, precision=EXACT_FLOAT_MODE
    ) * HSIZE ** (-0.5)
    allowed = allowed_pairs(positions, key_pos, seq_lengths)[:, None]
    masked = jnp.where(allowed, scores, NEGATIVE)
    new_high = jnp.maximum(highest, jnp.max(masked, -1))
    weight_values = jnp.where(allowed, jnp.exp(masked - new_high[..., None]), 0.0)
    summed = jnp.sum(weight_values, -1)
    weighted = jnp.einsum("shqk,skhe->shqe", weight_values, value_heads, precision=EXACT_FLOAT_MODE)
    highest, summed, weighted = (new_high, summed, weighted)
    log_total = highest + jnp.log(summed)
    attended = (weighted / summed[..., None]).transpose(0, 2, 1, 3).reshape(
        sequences, rows, channels
    ) * live_rows[..., None]
    branch = lax.psum(matmul(attended, output_weight), "head")
    mixed = inputs + branch + output_bias
    normed_two, second_unit, second_inverse = normalize(mixed, second_gain, second_shift)
    hidden = matmul(normed_two, inner_weight) + hidden_layer_bias
    rectified = jnp.maximum(hidden, 0.0)
    active = rectified * rectified
    result = mixed + lax.psum(matmul(active, outer_weight), "head") + outer_bias
    grad_outer_weight = outer_sum(active, cotangent)
    grad_outer_bias = jnp.sum(cotangent, (0, 1))
    grad_hidden = transposed(cotangent, outer_weight) * (2.0 * rectified)
    grad_inner_weight = outer_sum(normed_two, grad_hidden)
    grad_inner_bias = jnp.sum(grad_hidden, (0, 1))
    grad_normed_two = lax.psum(transposed(grad_hidden, inner_weight), "head")
    through_two, grad_second_gain, grad_second_shift = normalize_back(
        grad_normed_two, second_gain, second_unit, second_inverse
    )
    grad_mixed = cotangent + through_two
    grad_output_weight = outer_sum(attended, grad_mixed)
    grad_output_bias = jnp.sum(grad_mixed, (0, 1))
    grad_attended = transposed(grad_mixed, output_weight) * live_rows[..., None]
    row_dots = jnp.sum(split_heads(grad_attended) * split_heads(attended), -1).transpose(0, 2, 1)
    terms = pair_terms(
        queries, grad_attended, log_total, row_dots, positions, portion, key_pos, seq_lengths
    )
    grad_queries = query_side_term(terms).reshape(jnp.zeros_like(queries).shape)
    query_side = jnp.concatenate([queries, grad_attended], 2)
    row_stats = jnp.concatenate([log_total, row_dots], 1).transpose(0, 2, 1)
    side_rows = lax.all_gather(query_side, "seq", axis=1, tiled=True)
    stat_rows = lax.all_gather(row_stats, "seq", axis=1, tiled=True)
    query_pos = jnp.arange(side_rows.shape[1], dtype=jnp.int32)
    portion_total = stat_rows[:, :, :heads].transpose(0, 2, 1)
    portion_dots = stat_rows[:, :, heads:].transpose(0, 2, 1)
    grad_keyvals = key_terms(
        side_rows[:, :, :channels],
        side_rows[:, :, channels:],
        portion_total,
        portion_dots,
        query_pos,
        keyvals,
        positions,
        seq_lengths,
    )
    grad_convolved = jnp.concatenate([grad_queries, grad_keyvals], 2)
    following = shifted(grad_convolved[:, :2, :], "seq", -1)
    grad_extended = jnp.concatenate([grad_convolved, following], 1)
    grad_projected = (
        joined_kernel[0] * grad_extended[:, :rows]
        + joined_kernel[1] * grad_extended[:, 1 : rows + 1]
        + joined_kernel[2] * grad_extended[:, 2:]
    )
    grad_kernel = jnp.stack(
        [
            jnp.sum(grad_convolved * extended[:, 2:], (0, 1)),
            jnp.sum(grad_convolved * extended[:, 1:-1], (0, 1)),
            jnp.sum(grad_convolved * extended[:, :-2], (0, 1)),
        ]
    )
    grad_joined = outer_sum(normed, grad_projected)
    grad_normed = lax.psum(transposed(grad_projected, joined_weight), "head")
    through_one, grad_first_gain, grad_first_shift = normalize_back(
        grad_normed, first_gain, leading_unit_value, first_inverse
    )
    grad_inputs = grad_mixed + through_one
    grad_query_weight = grad_joined[:, :channels]
    grad_key_weight = grad_joined[:, channels : 2 * channels]
    grad_value_weight = grad_joined[:, 2 * channels :]
    grad_query_kernel = grad_kernel[:, :channels]
    grad_key_kernel = grad_kernel[:, channels : 2 * channels]
    grad_value_kernel = grad_kernel[:, 2 * channels :]
    (
        grad_first_gain,
        grad_first_shift,
        grad_query_weight,
        grad_key_weight,
        grad_value_weight,
        grad_query_kernel,
        grad_key_kernel,
        grad_value_kernel,
        grad_output_weight,
        grad_output_bias,
        grad_second_gain,
        grad_second_shift,
        grad_inner_weight,
        grad_inner_bias,
        grad_outer_weight,
        grad_outer_bias,
    ) = lax.psum(
        (
            grad_first_gain,
            grad_first_shift,
            grad_query_weight,
            grad_key_weight,
            grad_value_weight,
            grad_query_kernel,
            grad_key_kernel,
            grad_value_kernel,
            grad_output_weight,
            grad_output_bias,
            grad_second_gain,
            grad_second_shift,
            grad_inner_weight,
            grad_inner_bias,
            grad_outer_weight,
            grad_outer_bias,
        ),
        "seq",
    )
    return (
        result,
        grad_inputs,
        grad_first_gain,
        grad_first_shift,
        grad_query_weight,
        grad_key_weight,
        grad_value_weight,
        grad_query_kernel,
        grad_key_kernel,
        grad_value_kernel,
        grad_output_weight,
        grad_output_bias,
        grad_second_gain,
        grad_second_shift,
        grad_inner_weight,
        grad_inner_bias,
        grad_outer_weight,
        grad_outer_bias,
    )


class Comm:
    def __init__(self, send_sems, recv_sems, local_sems=None):
        self.send_sems, self.recv_sems, self.local_sems = send_sems, recv_sems, local_sems
        self.used = 0
        self.used_local = 0
        self.sent = []
        self.stored = []

    def copy(self, source, target, device, when=None):
        index = self.used
        self.used += 1
        made = pltpu.make_async_remote_copy(
            src_ref=source,
            dst_ref=target,
            send_sem=self.send_sems.at[index],
            recv_sem=self.recv_sems.at[index],
            device_id=device,
            device_id_type=MESH,
        )
        if when is None:
            made.start()
        else:
            pl.when(when)(made.start)
        self.sent.append((made, when))
        return made

    def settle(self, made):
        self.sent = [one for one in self.sent if one[0] is not made]
        made.wait_send()

    def local(self, source, target, when=None, keep=True):
        made = pltpu.make_async_copy(source, target, self.local_sems.at[self.used_local])
        self.used_local += 1
        if when is None:
            made.start()
        else:
            pl.when(when)(made.start)
        if keep:
            self.stored.append((made, when))
        return made

    def finish(self):
        for made, when in self.sent:
            if when is None:
                made.wait_send()
            else:
                pl.when(when)(made.wait_send)
        for made, when in self.stored:
            if when is None:
                made.wait()
            else:
                pl.when(when)(made.wait)


def wait_for(made, when=None):
    if when is None:
        made.wait_recv()
    else:
        pl.when(when)(made.wait_recv)


class Place:
    def __init__(self):
        self.seq = lax.axis_index("seq")
        self.head = lax.axis_index("head")
        self.z = self.seq // 2
        self.y = self.seq % 2
        self.other = 1 - self.y
        self.core = self.head % 2
        self.at_end = (self.z == 0) | (self.z == LINE - 1)
        self.at_middle = jnp.logical_not(self.at_end)
        step = 2 - 4 * (self.z // 2)
        self.pair = (2 * self.z + self.other, self.head)
        self.inward = (self.seq + step, self.head)
        self.outward = (self.seq - step, self.head)
        self.sibling = (self.seq, self.head + 1 - 2 * self.core)
        self.facing = (self.seq, (self.head + 2) % 4)


LINE = 4


def rows_at(ref, start, count):
    return ref.at[pl.ds(pl.multiple_of(start, 8), count)]


class Land:
    def __init__(self, ref):
        self.ref, self.used = ref, 0

    def take(self, rows):
        got = self.ref.at[pl.ds(self.used, rows)]
        self.used += rows
        return got


def sum_pair_first(comm, place, land, source, target, start, count):
    half = count // 2
    line, from_end, from_middle = land.take(half), land.take(half), land.take(half)
    own = rows_at(target, start + place.y * half, half)
    far = rows_at(source, start + place.other * half, half)
    near = rows_at(source, start + place.y * half, half)
    made = comm.copy(far, line, place.pair)
    yield
    made.wait_recv()
    line[...] = line[...] + near[...]
    inward = comm.copy(line, from_end, place.inward, place.at_end)
    yield

    @pl.when(place.at_middle)
    def _():
        inward.wait_recv()
        from_end[...] = from_end[...] + line[...]

    across = comm.copy(from_end, from_middle, place.inward, place.at_middle)
    yield

    @pl.when(place.at_middle)
    def _():
        across.wait_recv()
        from_middle[...] = from_middle[...] + from_end[...]

    outward = comm.copy(from_middle, own, place.outward, place.at_middle)
    early = comm.copy(from_middle, own, place.pair, place.at_middle)
    comm.local(from_middle, own, place.at_middle)
    yield
    wait_for(outward, place.at_end)
    late = comm.copy(own, own, place.pair, place.at_end)
    yield
    wait_for(early, place.at_middle)
    wait_for(late, place.at_end)
    yield


def sum_line_first(comm, place, land, source, target, start, count):
    half = count // 2
    whole, from_middle, from_pair = land.take(count), land.take(half), land.take(half)
    all_rows = rows_at(source, start, count)
    mine, theirs = place.z // 2, 1 - place.z // 2
    own, rest = rows_at(target, start + mine * half, half), rows_at(target, start + theirs * half, half)
    inward = comm.copy(all_rows, whole, place.inward, place.at_end)
    yield

    @pl.when(place.at_middle)
    def _():
        inward.wait_recv()
        whole[...] = whole[...] + all_rows[...]

    across = comm.copy(rows_at(whole, theirs * half, half), from_middle, place.inward, place.at_middle)
    yield

    @pl.when(place.at_middle)
    def _():
        across.wait_recv()
        from_middle[...] = from_middle[...] + rows_at(whole, mine * half, half)[...]

    paired = comm.copy(from_middle, from_pair, place.pair, place.at_middle)
    yield

    @pl.when(place.at_middle)
    def _():
        paired.wait_recv()
        from_pair[...] = from_pair[...] + from_middle[...]

    back = comm.copy(from_pair, own, place.inward, place.at_middle)
    outward = comm.copy(from_pair, own, place.outward, place.at_middle)
    comm.local(from_pair, own, place.at_middle)
    yield
    wait_for(back, place.at_middle)
    last = comm.copy(rest, rest, place.outward, place.at_middle)
    yield
    wait_for(outward, place.at_end)
    wait_for(last, place.at_end)
    yield


class Crew:
    def __init__(self):
        self.waiting = []

    def add(self, one, delay=0):
        self.waiting.append([one, delay])

    def advance(self):
        left = []
        for entry in self.waiting:
            if entry[1] > 0:
                entry[1] -= 1
                left.append(entry)
                continue
            try:
                next(entry[0])
                left.append(entry)
            except StopIteration:
                pass
        self.waiting = left

    def drain(self):
        while self.waiting:
            self.advance()


def split(value):
    high = value.astype(jnp.bfloat16)
    return high, (value - high.astype(jnp.float32)).astype(jnp.bfloat16)


def dot(left, right, dims):
    return lax.dot_general(left, right, (dims, ((), ())), preferred_element_type=jnp.float32)


def dot_three(left, right, dims):
    return dot(left[0], right[0], dims) + (dot(left[0], right[1], dims) + dot(left[1], right[0], dims))


PLAIN, BOTH_LAST, BOTH_FIRST = ((1,), (0,)), ((1,), (1,)), ((0,), (0,))


def product(left, right, dims=PLAIN):
    return dot_three(split(left), split(right), dims)


def beside(value):
    high, low = split(value)
    return jnp.concatenate([high, high, low], 1)


def against(value):
    high, low = split(value)
    return jnp.concatenate([high, low, high], 0)


def as_row(ref):
    return ref[...].reshape(1, ref.shape[0])


def unit_rows(rows):
    centered = rows - jnp.mean(rows, -1, keepdims=True)
    inverse = lax.rsqrt(jnp.mean(centered * centered, -1, keepdims=True) + EPSILON)
    return centered * inverse, inverse


def longer_first(lengths):
    return jnp.where(lengths[1] > lengths[0], 1, 0).astype(jnp.int32)


def head_lanes(head, base=0):
    return slice(base + head * HSIZE, base + (head + 1) * HSIZE)


class Spread:
    def __init__(self, comm, place, part, ends, upward=True, own=None):
        self.comm, self.place, self.part, self.ends = comm, place, part, ends
        self.own = own or (lambda half: part(place.seq, half))
        z, y = place.z, place.y
        self.rank = z if upward else ends - 1 - z
        self.inside = z < ends
        self.more = self.inside & ((z < ends - 1) if upward else (z > 0))
        self.leads = (y == 0) if upward else (y == 1)
        self.next = (place.seq + (2 if upward else -2), place.head)
        self.sign = 1 if upward else -1
        self.up = {}
        self.over = {}

    def block(self, level, slot):
        place = self.place
        side = place.y if slot == 0 else place.other
        return 2 * (place.z - self.sign * level) + side

    def begin(self):
        comm, place, part = self.comm, self.place, self.part
        near, far = part(place.seq, place.y), part(place.seq, place.other)
        mine = self.own(place.y)
        self.lend = comm.copy(self.own(place.other), far, place.pair, self.inside & (self.more | self.leads))
        self.up[1, 0] = comm.copy(mine, near, self.next, self.more)
        self.give = comm.copy(mine, near, place.pair, self.inside & self.leads)

    def pass_pair(self):
        comm, place, part = self.comm, self.place, self.part
        follows = jnp.logical_not(self.leads)
        wait_for(self.lend, self.inside & (self.more | follows))
        lent = part(self.block(0, 1), place.y)
        self.up[1, 1] = comm.copy(lent, lent, self.next, self.more)

    def have_pair(self):
        wait_for(self.give, self.inside & jnp.logical_not(self.leads))

    def pass_level(self, level):
        comm, place, part = self.comm, self.place, self.part
        here = self.inside & (self.rank >= level)
        for slot in range(2):
            half = part(self.block(level, slot), place.y)
            wait_for(self.up[level, slot], here)
            if level < LINE - 1:
                self.up[level + 1, slot] = comm.copy(half, half, self.next, here & self.more)
            self.over[level, slot] = comm.copy(half, half, place.pair, here)

    def have_level(self, level):
        here = self.inside & (self.rank >= level)
        for slot in range(2):
            wait_for(self.over[level, slot], here)


def greet(partners):
    barrier = pltpu.get_barrier_semaphore()
    count = jnp.int32(0)
    for device, when in partners:
        def tell(device=device):
            pl.semaphore_signal(barrier, inc=1, device_id=device, device_id_type=MESH)

        if when is None:
            tell()
            count = count + 1
        else:
            pl.when(when)(tell)
            count = count + when.astype(jnp.int32)
    pl.semaphore_wait(barrier, count)


def line_partners(place):
    return [
        (place.pair, None),
        ((place.seq + 2, place.head), place.z < LINE - 1),
        ((place.seq - 2, place.head), place.z > 0),
    ]


def head_partners(place):
    return [(place.sibling, None), (place.facing, None)]


def step_partners(place):
    return [
        ((place.seq + 1, place.head), (place.y == 1) & (place.z < LINE - 1)),
        ((place.seq - 1, place.head), (place.y == 0) & (place.z > 0)),
    ]


def front_kernel(
    ends,
    lengths,
    inputs,
    gain,
    shift,
    query_weight,
    key_weight,
    value_weight,
    query_kernel,
    key_kernel,
    value_kernel,
    output_weight,
    keyvals,
    queries,
    raw,
    attended,
    attended_turned,
    log_total,
    weights,
    joined,
    halo,
    rows_high,
    rows_low,
    query_cat,
    highest,
    summed,
    weighted,
    send_sems,
    recv_sems,
):
    place = Place()
    comm = Comm(send_sems, recv_sems)
    sequences, rows, model = inputs.shape
    channels = query_weight.shape[0]
    heads = channels // HSIZE
    edge = halo.shape[1]
    first = longer_first(lengths)
    order = (first, 1 - first)
    greet(line_partners(place) + head_partners(place) + step_partners(place))
    rim = comm.copy(
        inputs.at[:, pl.ds(rows - edge, edge)],
        halo,
        (place.seq + 1, place.head),
        place.seq < 2 * LINE - 1,
    )
    own_weight = rows_at(weights, place.head * channels, channels)
    own_weight[...] = output_weight[...]
    to_sibling = comm.copy(own_weight, own_weight, place.sibling)
    to_facing = comm.copy(own_weight, own_weight, place.facing)

    def normal(value):
        return unit_rows(value)[0] * as_row(gain) + as_row(shift)

    for i in range(sequences):
        high, low = split(normal(inputs[order[i]]))
        rows_high[pl.ds(i * rows, rows)] = high
        rows_low[pl.ds(i * rows, rows)] = low
    wait_for(rim, place.seq > 0)
    inner = (place.seq > 0).astype(jnp.float32)
    rim_rows = jnp.concatenate([normal(halo[order[i]]) for i in range(sequences)], 0)
    rim_split = split(rim_rows)
    for k, weight in enumerate((query_weight, key_weight, value_weight)):
        parts = split(weight[...])
        whole = dot_three((rows_high[...], rows_low[...]), parts, BOTH_LAST)
        before = dot_three(rim_split, parts, BOTH_LAST) * inner
        for i in range(sequences):
            raw[k, i, pl.ds(0, edge)] = before[i * edge : (i + 1) * edge]
            raw[k, i, pl.ds(edge, rows)] = whole[i * rows : (i + 1) * rows]

    def convolved(k, i, kernel):
        return (
            kernel[0:1] * raw[k, i, pl.ds(edge, rows)]
            + kernel[1:2] * raw[k, i, pl.ds(edge - 1, rows)]
            + kernel[2:3] * raw[k, i, pl.ds(edge - 2, rows)]
        )

    spreads = []
    for i in range(sequences):
        own = keyvals.at[place.seq, i]
        own[:, 0:channels] = convolved(1, i, key_kernel)
        own[:, channels : 2 * channels] = convolved(2, i, value_kernel)

        def part(block, half, i=i):
            return keyvals.at[block, i, pl.ds(pl.multiple_of(half * (rows // 2), 8), rows // 2)]

        spreads.append(Spread(comm, place, part, ends[i]))
        spreads[i].begin()
    for i in range(sequences):
        query = convolved(0, i, query_kernel).T
        queries[i] = query
        for head in range(heads):
            query_cat[i, head] = against(query[head_lanes(head)] * HSIZE ** (-0.5))
    to_facing.wait_recv()
    theirs = rows_at(weights, place.facing[1] * channels, channels)
    to_last = comm.copy(theirs, theirs, place.sibling)

    def attend(i, block, diagonal):
        own = keyvals.at[block, i]
        for head in range(heads):
            scores = dot(beside(own[:, head_lanes(head)]), query_cat[i, head], PLAIN)
            lane = pl.ds(head, 1)
            if diagonal:
                key_pos = lax.broadcasted_iota(jnp.int32, scores.shape, 0)
                query_pos = lax.broadcasted_iota(jnp.int32, scores.shape, 1)
                scores = jnp.where(key_pos <= query_pos, scores, NEGATIVE)
                high = jnp.max(scores, 0, keepdims=True)
            else:
                old = highest[i, lane]
                high = jnp.maximum(old, jnp.max(scores, 0, keepdims=True))
            powers = jnp.exp(scores - high)
            total = jnp.sum(powers, 0, keepdims=True)
            power_high, power_low = split(powers)
            value_high, value_low = split(own[:, head_lanes(head, channels)])
            both = dot(jnp.concatenate([value_high, value_low], 1), power_high, BOTH_FIRST)
            term = both[:HSIZE] + both[HSIZE:] + dot(value_high, power_low, BOTH_FIRST)
            at = pl.ds(head * HSIZE, HSIZE)
            if diagonal:
                summed[i, lane] = total
                weighted[i, at] = term
            else:
                scale = jnp.exp(old - high)
                summed[i, lane] = summed[i, lane] * scale + total
                weighted[i, at] = weighted[i, at] * scale + term
            highest[i, lane] = high

    def here(i):
        return place.z < ends[i]

    def both(body):
        def step(i, carry):
            body(i)
            return carry

        lax.fori_loop(0, sequences, step, 0)

    for k, weight in enumerate((query_weight, key_weight, value_weight)):
        joined[k * channels : (k + 1) * channels] = weight[...]
    for spread in spreads:
        spread.pass_pair()
    both(lambda i: attend(i, place.seq, True))
    for spread in spreads:
        spread.have_pair()

    for level in range(LINE):
        if level:
            for spread in spreads:
                spread.pass_level(level)
            for spread in spreads:
                spread.have_level(level)

        def blocks(k, carry, level=level):
            i, slot = k // 2, k % 2
            block = 2 * (place.z - level) + slot
            limit = jnp.where(i == 0, ends[0], ends[1])
            if level:
                wanted = (place.z >= level) & (place.z < limit)
            else:
                wanted = (slot == 0) & (place.y == 1) & (place.z < limit)

            @pl.when(wanted)
            def _():
                attend(i, block, False)

            return carry

        lax.fori_loop(0, 2 * sequences, blocks, 0)

    for i in range(sequences):
        live = jnp.minimum(lengths[order[i]] - place.seq * rows, rows)
        alive = (lax.broadcasted_iota(jnp.int32, (1, rows), 1) < live).astype(jnp.float32)
        for head in range(heads):
            at = pl.ds(head * HSIZE, HSIZE)
            total = summed[i, pl.ds(head, 1)]
            weighted[i, at] = weighted[i, at] * (alive / total)
            log_total[i, pl.ds(head, 1)] = highest[i, pl.ds(head, 1)] + jnp.log(total)
        attended_turned[i] = weighted[i]
        attended[:, i * channels : (i + 1) * channels] = weighted[i].T
    to_sibling.wait_recv()
    to_last.wait_recv()
    comm.finish()


def front(ends, collective, lengths, inputs, gain, shift, weights, kernels, output_weight):
    sequences, rows, model = inputs.shape
    channels = output_weight.shape[0]
    heads = channels // HSIZE
    blocks = lax.axis_size("seq")
    groups = lax.axis_size("head")
    edge = 8
    vmem = pl.BlockSpec(memory_space=pltpu.VMEM)

    def f32(*shape):
        return jax.ShapeDtypeStruct(shape, jnp.float32)

    copies = 64
    return pl.pallas_call(
        functools.partial(front_kernel, ends),
        out_shape=[
            f32(blocks, sequences, rows, 2 * channels),
            f32(sequences, channels, rows),
            f32(3, sequences, rows + edge, channels),
            f32(rows, sequences * channels),
            f32(sequences, channels, rows),
            f32(sequences, 8, rows),
            f32(groups * channels, model),
            f32(3 * channels, model),
        ],
        in_specs=[pl.BlockSpec(memory_space=pltpu.SMEM)] + [vmem] * 10,
        out_specs=[vmem] * 8,
        scratch_shapes=[
            pltpu.VMEM((sequences, edge, model), jnp.float32),
            pltpu.VMEM((sequences * rows, model), jnp.bfloat16),
            pltpu.VMEM((sequences * rows, model), jnp.bfloat16),
            pltpu.VMEM((sequences, heads, 3 * HSIZE, rows), jnp.bfloat16),
            pltpu.VMEM((sequences, 8, rows), jnp.float32),
            pltpu.VMEM((sequences, 8, rows), jnp.float32),
            pltpu.VMEM((sequences, channels, rows), jnp.float32),
            pltpu.SemaphoreType.DMA((copies,)),
            pltpu.SemaphoreType.DMA((copies,)),
        ],
        compiler_params=pltpu.CompilerParams(
            collective_id=collective, has_side_effects=True, vmem_limit_bytes=60 * 2**20
        ),
        name="front",
    )(lengths, inputs, gain, shift, *[weight.T for weight in weights], *kernels, output_weight)


class HeadSum:
    def __init__(self, comm, place, partial, from_sibling, from_facing, rows, pieces=4):
        self.comm, self.place, self.partial = comm, place, partial
        self.from_sibling, self.from_facing = from_sibling, from_facing
        self.rows, self.pieces = rows, pieces
        self.size = rows // pieces
        self.near = rows_at(partial, place.core * rows, rows)

    def lend(self):
        far = rows_at(self.partial, (1 - self.place.core) * self.rows, self.rows)
        self.lent = self.comm.copy(far, self.from_sibling, self.place.sibling)

    def chip(self):
        self.lent.wait_recv()
        self.near[...] = self.near[...] + self.from_sibling[...]
        self.sent = []
        for p in range(self.pieces):
            at = pl.ds(p * self.size, self.size)
            self.sent.append(self.comm.copy(self.near.at[at], self.from_facing.at[at], self.place.facing))

    def piece(self, p):
        self.sent[p].wait_recv()
        at = pl.ds(p * self.size, self.size)
        return self.near[at] + self.from_facing[at]


def norm_back(grad, gain, unit, inverse):
    scaled = grad * gain
    return inverse * (
        scaled - jnp.mean(scaled, -1, keepdims=True) - unit * jnp.mean(scaled * unit, -1, keepdims=True)
    )


def spread_steps(spreads):
    for spread in spreads:
        spread.begin()
    yield
    for spread in spreads:
        spread.pass_pair()
    yield
    for level in range(1, LINE):
        for spread in spreads:
            spread.pass_level(level)
        yield


TILE = 256


def tiles(width, body):
    def step(j, carry):
        body(pl.ds(pl.multiple_of(j * TILE, TILE), TILE))
        return carry

    lax.fori_loop(0, width // TILE, step, 0)


def down_rows(value):
    return jnp.sum(value, 0, keepdims=True)


def allowed_from(shape, offset):
    key_pos = lax.broadcasted_iota(jnp.int32, shape, 0)
    query_pos = lax.broadcasted_iota(jnp.int32, shape, 1)
    return key_pos <= query_pos + offset


def back_kernel(
    ends,
    plan,
    lengths,
    inputs,
    cotangent,
    attended,
    attended_turned,
    queries,
    log_total,
    output_weight,
    output_bias,
    first_gain,
    first_shift,
    second_gain,
    second_shift,
    hidden_bias,
    outer_bias,
    query_kernel,
    key_kernel,
    value_kernel,
    keyvals,
    weights,
    inner_weight,
    outer_weight,
    joined,
    raw_far,
    result,
    grad_inputs,
    outer_out,
    inner_out,
    rest_out,
    late_out,
    all_queries,
    all_grads,
    weight_a,
    weight_b,
    weight_c,
    raw,
    groups,
    normed_two,
    active,
    grad_hidden,
    grad_normed,
    from_sibling,
    from_facing,
    grad_outer,
    grad_inner,
    grad_rest,
    land_ref,
    key_slots,
    own_keys,
    query_slots,
    grad_slots,
    query_cat,
    grad_cat,
    key_cat,
    value_cat,
    grad_att,
    grad_query,
    grad_keyval,
    grad_conv,
    late_from,
    late_all,
    send_sems,
    recv_sems,
    local_sems,
    slot_sems,
):
    place = Place()
    comm = Comm(send_sems, recv_sems, local_sems)
    land = Land(land_ref)
    crew = Crew()
    sequences, rows, model = inputs.shape
    channels = output_weight.shape[0]
    heads = channels // HSIZE
    hidden_units = hidden_bias.shape[0]
    tokens = sequences * rows
    z, y, seq, core = place.z, place.y, place.seq, place.core
    first = longer_first(lengths)
    order = (first, 1 - first)
    devices = 2 * LINE
    column = [((lax.rem(seq + k, devices), place.head), None) for k in range(1, devices)]
    greet(column + head_partners(place))

    load_a = comm.local(weights, weight_a, keep=False)
    load_b = comm.local(inner_weight, weight_b, keep=False)
    load_c = comm.local(outer_weight, weight_c, keep=False)
    load_raw = comm.local(raw_far, raw, keep=False)
    load_own = [comm.local(keyvals.at[seq, i], own_keys.at[i], keep=False) for i in range(sequences)]
    keep_query = [comm.local(queries.at[i], all_queries.at[seq, i], keep=False) for i in range(sequences)]

    to_sibling = comm.copy(attended, groups.at[place.head], place.sibling)
    to_facing = comm.copy(attended, groups.at[place.head], place.facing)

    def query_part(block, half, i):
        return all_queries.at[block, i, pl.ds(pl.multiple_of(half * (channels // 2), 8), channels // 2)]

    def grad_part(block, half, i):
        size = grad_att.shape[1] // 2
        return all_grads.at[block, i, pl.ds(pl.multiple_of(half * size, 8), size)]

    def query_own(half, i):
        return queries.at[i, pl.ds(pl.multiple_of(half * (channels // 2), 8), channels // 2)]

    def grad_own(half, i):
        size = grad_att.shape[1] // 2
        return grad_att.at[i, pl.ds(pl.multiple_of(half * size, 8), size)]

    query_spreads = [
        Spread(
            comm,
            place,
            functools.partial(query_part, i=i),
            ends[i],
            False,
            functools.partial(query_own, i=i),
        )
        for i in range(sequences)
    ]
    grad_spreads = [
        Spread(
            comm,
            place,
            functools.partial(grad_part, i=i),
            ends[i],
            False,
            functools.partial(grad_own, i=i),
        )
        for i in range(sequences)
    ]
    crew.add(spread_steps(query_spreads))
    crew.advance()

    def chunk(i):
        return pl.ds(i * rows, rows)

    def add_group(ref, weight_ref, total, begin):
        parts = split(weight_ref[...])
        for i in range(sequences):
            piece = split(ref[:, i * channels : (i + 1) * channels])
            term = dot_three(piece, parts, PLAIN)
            total[chunk(i)] = term if begin else total[chunk(i)] + term

    add_group(attended, output_weight, grad_inputs, True)
    crew.advance()
    load_a.wait()

    def group_weight(group):
        return rows_at(weight_a, group * channels, channels)

    sibling, facing = place.sibling[1], place.facing[1]
    last = facing + 1 - 2 * (facing % 2)
    to_sibling.wait_recv()
    add_group(groups.at[sibling], group_weight(sibling), grad_inputs, False)
    to_facing.wait_recv()
    onward = comm.copy(groups.at[facing], groups.at[facing], place.sibling)
    add_group(groups.at[facing], group_weight(facing), result, True)
    crew.advance()
    onward.wait_recv()
    add_group(groups.at[last], group_weight(last), result, False)

    for i in range(sequences):
        result[chunk(i)] = inputs[order[i]] + as_row(output_bias) + (grad_inputs[chunk(i)] + result[chunk(i)])
        normed_two[chunk(i)] = unit_rows(result[chunk(i)])[0] * as_row(second_gain) + as_row(second_shift)
    load_b.wait()
    load_c.wait()

    def cot_columns(columns):
        return jnp.concatenate([cotangent[order[i], :, columns] for i in range(sequences)], 0)

    normed_parts = split(normed_two[...])
    cot_parts = split(jnp.concatenate([cotangent[order[i]] for i in range(sequences)], 0))

    def hidden_tile(columns):
        hidden = dot_three(normed_parts, split(weight_b[:, columns]), PLAIN)
        hidden = hidden + hidden_bias[columns].reshape(1, TILE)
        rectified = jnp.maximum(hidden, 0.0)
        grad_active = dot_three(cot_parts, split(weight_c[columns]), BOTH_LAST)
        grad = grad_active * (2.0 * rectified)
        active[:, columns] = rectified * rectified
        grad_hidden[:, columns] = grad
        grad_rest[4 * channels + 2 : 4 * channels + 3, columns] = down_rows(grad)

    tiles(hidden_units, hidden_tile)
    crew.advance()

    def grad_normed_chunk(which):
        at = pl.ds(pl.multiple_of(which * rows, rows), rows)
        parts = split(grad_hidden[at])

        def tile(columns):
            grad_normed[at, columns] = dot_three(parts, split(weight_b[columns]), BOTH_LAST)

        tiles(model, tile)

    second_sum = HeadSum(comm, place, grad_normed, from_sibling.at[0], from_facing.at[0], rows)
    grad_normed_chunk(1 - core)
    second_sum.lend()
    grad_normed_chunk(core)
    second_sum.chip()

    active_parts = split(active[...])

    def outer_tile(columns):
        grad_outer[:, columns] = dot_three(active_parts, split(cot_columns(columns)), BOTH_FIRST)

    tiles(model, outer_tile)
    def add_sums(wanted, source, target):
        for pair_first, which, start, count, delay in plan:
            if which == wanted:
                make = sum_pair_first if pair_first else sum_line_first
                crew.add(make(comm, place, land, source, target, start, count), delay)

    add_sums(0, grad_outer, outer_out)
    crew.advance()

    normed_parts = split(normed_two[...])

    def inner_tile(columns):
        grad_inner[:, columns] = dot_three(normed_parts, split(grad_hidden[:, columns]), BOTH_FIRST)

    tiles(hidden_units, inner_tile)
    add_sums(1, grad_inner, inner_out)
    crew.advance()

    outer_term = weight_a.at[pl.ds(0, tokens)]

    def outer_term_tile(columns):
        outer_term[:, columns] = dot_three(active_parts, split(weight_c[:, columns]), PLAIN)

    tiles(model, outer_term_tile)
    load_joined = comm.local(joined, weight_c.at[pl.ds(0, 3 * channels)], keep=False)
    crew.advance()

    late_out[...] = jnp.zeros_like(late_out)
    swaps = []

    def own_piece(p, size):
        return pl.ds(pl.multiple_of(core * rows + p * size, 8), size)

    for p in range(second_sum.pieces):
        at = own_piece(p, second_sum.size)
        incoming = second_sum.piece(p)
        unit, inverse = unit_rows(result[at])
        through = norm_back(incoming, as_row(second_gain), unit, inverse)
        here = pl.ds(p * second_sum.size, second_sum.size)
        cot = jnp.where(core == 0, cotangent[order[0], here], cotangent[order[1], here])
        grad_inputs[at] = cot + through
        late_out[2:3] = late_out[2:3] + down_rows(incoming * unit)
        late_out[3:4] = late_out[3:4] + down_rows(incoming)
        swaps.append(comm.copy(grad_inputs.at[at], grad_inputs.at[at], place.sibling))
        if p % 2:
            crew.advance()
    result_sum = HeadSum(comm, place, outer_term, from_sibling.at[1], from_facing.at[1], rows)
    result_sum.lend()
    for made in swaps:
        made.wait_recv()

    weight_parts = split(output_weight[...])
    grad_att[:, channels:] = jnp.zeros((sequences, grad_att.shape[1] - channels, rows), jnp.float32)
    for i in range(sequences):
        live = jnp.minimum(lengths[order[i]] - seq * rows, rows)
        alive = (lax.broadcasted_iota(jnp.int32, (1, rows), 1) < live).astype(jnp.float32)
        grad = dot_three(weight_parts, split(grad_inputs[chunk(i)]), BOTH_LAST) * alive
        grad_att[i, 0:channels] = grad
        both = grad * attended_turned[i]
        for head in range(heads):
            at = channels + head
            grad_att[i, at : at + 1] = log_total[i, head : head + 1]
            grad_att[i, at + heads : at + heads + 1] = down_rows(both[head_lanes(head)])
    keep_grad = [comm.local(grad_att.at[i], all_grads.at[seq, i], keep=False) for i in range(sequences)]
    for spread in grad_spreads:
        spread.begin()
    crew.advance()
    result_sum.chip()
    for i in range(sequences):
        for head in range(heads):
            query_cat[i, head] = against(queries[i, head_lanes(head)] * HSIZE ** (-0.5))
            grad_cat[i, head] = against(grad_att[i, head_lanes(head)])
    output_grad = jnp.zeros((channels, model), jnp.float32)
    for i in range(sequences):
        output_grad = output_grad + dot_three(split(attended_turned[i]), split(grad_inputs[chunk(i)]), PLAIN)
    grad_rest[0:channels] = output_grad
    base = 4 * channels
    grad_rest[base : base + 1] = down_rows(grad_inputs[...])
    outer_row = jnp.zeros((1, model), jnp.float32)
    for i in range(sequences):
        outer_row = outer_row + down_rows(cotangent[order[i]])
    grad_rest[base + 1 : base + 2] = outer_row
    add_sums(2, grad_rest, rest_out)
    for spread in grad_spreads:
        spread.pass_pair()
    crew.advance()

    grad_query[...] = jnp.zeros_like(grad_query)
    grad_keyval[...] = jnp.zeros_like(grad_keyval)

    def query_side(i):
        count = jnp.where(z < ends[i], seq + 1, 0)

        def load(slot, block):
            return pltpu.make_async_copy(keyvals.at[block, i], key_slots.at[slot], slot_sems.at[slot])

        pl.when(count > 0)(lambda: load(0, seq).start())

        def step(t, carry):
            slot = lax.rem(t, 2)
            load(slot, seq - t).wait()
            pl.when(t + 1 < count)(lambda: load(1 - slot, seq - t - 1).start())
            block = key_slots.at[slot]
            for head in range(heads):
                key_high, key_low = split(block[:, head_lanes(head)])
                scores = dot(jnp.concatenate([key_high, key_high, key_low], 1), query_cat[i, head], PLAIN)
                at = channels + head
                scores = scores - grad_att[i, at : at + 1]
                powers = jnp.exp(jnp.where(allowed_from(scores.shape, t * rows), scores, NEGATIVE))
                slopes = dot(beside(block[:, head_lanes(head, channels)]), grad_cat[i, head], PLAIN)
                slopes = powers * (slopes - grad_att[i, at + heads : at + heads + 1])
                high, low = split(slopes)
                both = dot(jnp.concatenate([key_high, key_low], 1), high, BOTH_FIRST)
                term = both[:HSIZE] + both[HSIZE:] + dot(key_high, low, BOTH_FIRST)
                grad_query[i, head_lanes(head)] = grad_query[i, head_lanes(head)] + term
            return carry

        lax.fori_loop(0, count, step, 0)

    def key_side(i, offset, query_ref, grad_ref):
        for head in range(heads):
            lanes = head_lanes(head)
            query_high, query_low = split(query_ref[lanes] * HSIZE ** (-0.5))
            grad_high, grad_low = split(grad_ref[lanes])
            scores = dot(
                key_cat[i, head, :, 0 : 3 * HSIZE],
                jnp.concatenate([query_high, query_low, query_high], 0),
                PLAIN,
            )
            at = channels + head
            scores = scores - grad_ref[at : at + 1]
            powers = jnp.exp(jnp.where(allowed_from(scores.shape, offset), scores, NEGATIVE))
            slopes = dot(
                value_cat[i, head, :, 0 : 3 * HSIZE],
                jnp.concatenate([grad_high, grad_low, grad_high], 0),
                PLAIN,
            )
            slopes = powers * (slopes - grad_ref[at + heads : at + heads + 1])
            for base, (far_high, far_low), value in (
                (0, (query_high, query_low), slopes),
                (channels, (grad_high, grad_low), powers),
            ):
                high, low = split(value)
                both = dot(jnp.concatenate([far_high, far_low], 0), high, BOTH_LAST)
                term = both[:HSIZE] + both[HSIZE:] + dot(far_high, low, BOTH_LAST)
                where = slice(base + head * HSIZE, base + (head + 1) * HSIZE)
                grad_keyval[i, where] = grad_keyval[i, where] + term

    def key_level(level, pairs):
        items = [(i, slot) for i in range(sequences) for slot in range(2)]

        def inside(i):
            return z + level < jnp.where(i == 0, ends[0], ends[1])

        def wanted(t):
            i, slot = t // 2, t % 2
            if level:
                return inside(i)
            if pairs:
                return inside(i) & (slot == 1) & (y == 0)
            return inside(i) & (slot == y)

        def loads(t):
            i, slot = t // 2, t % 2
            block = 2 * (z + level) + slot
            return (
                pltpu.make_async_copy(all_queries.at[block, i], query_slots.at[t], slot_sems.at[2 * t]),
                pltpu.make_async_copy(all_grads.at[block, i], grad_slots.at[t], slot_sems.at[2 * t + 1]),
            )

        for t in range(len(items)):
            @pl.when(wanted(t))
            def _(t=t):
                for made in loads(t):
                    made.start()

        def step(t, carry):
            @pl.when(wanted(t))
            def _():
                for made in loads(t):
                    made.wait()
                i, slot = t // 2, t % 2
                offset = (2 * (z + level) + slot - seq) * rows
                key_side(i, offset, query_slots.at[t], grad_slots.at[t])

            return carry

        lax.fori_loop(0, len(items), step, 0)

    query_side(0)
    crew.advance()
    for spread in grad_spreads:
        spread.pass_level(1)
    query_side(1)
    crew.advance()
    for p in range(result_sum.pieces):
        at = own_piece(p, result_sum.size)
        result[at] = result[at] + as_row(outer_bias) + result_sum.piece(p)
        swaps.append(comm.copy(result.at[at], result.at[at], place.sibling))
    for i in range(sequences):
        load_own[i].wait()
        for head in range(heads):
            key_cat[i, head, :, 0 : 3 * HSIZE] = beside(own_keys[i, :, head_lanes(head)])
            value_cat[i, head, :, 0 : 3 * HSIZE] = beside(own_keys[i, :, head_lanes(head, channels)])
        keep_query[i].wait()
        keep_grad[i].wait()
    key_level(0, False)
    crew.advance()
    for spread in grad_spreads:
        spread.pass_level(2)
    for spread in query_spreads + grad_spreads:
        spread.have_pair()
    key_level(0, True)
    crew.advance()
    for level in range(1, LINE):
        if level == 2:
            for spread in grad_spreads:
                spread.pass_level(3)
        for spread in query_spreads + grad_spreads:
            spread.have_level(level)
        key_level(level, False)
        crew.advance()

    edge = grad_conv.shape[2] - rows
    for i in range(sequences):
        grad_conv[0, i, pl.ds(0, rows)] = (grad_query[i] * HSIZE ** (-0.5)).T
        grad_conv[1, i, pl.ds(0, rows)] = grad_keyval[i, 0:channels].T
        grad_conv[2, i, pl.ds(0, rows)] = grad_keyval[i, channels : 2 * channels].T

    @pl.when(seq == devices - 1)
    def _():
        grad_conv[:, :, pl.ds(rows, edge)] = jnp.zeros((3, sequences, edge, channels), jnp.float32)

    before = (seq - 1, place.head)
    rim = comm.copy(
        grad_conv.at[:, :, pl.ds(0, edge)], grad_conv.at[:, :, pl.ds(rows, edge)], before, seq > 0
    )
    load_raw.wait()
    base = 4 * channels + 3
    grad_rest[base : base + 13] = jnp.zeros((13, model), jnp.float32)
    for k in range(3):
        for j in range(3):
            total = jnp.zeros((1, channels), jnp.float32)
            for i in range(sequences):
                total = total + down_rows(grad_conv[k, i, pl.ds(0, rows)] * raw[k, i, pl.ds(edge - j, rows)])
            grad_rest[base + j : base + j + 1, k * channels : (k + 1) * channels] = total
    crew.advance()
    wait_for(rim, seq < devices - 1)
    for k, kernel in enumerate((query_kernel, key_kernel, value_kernel)):
        for i in range(sequences):
            grad_hidden[chunk(i), k * channels : (k + 1) * channels] = (
                kernel[0:1] * grad_conv[k, i, pl.ds(0, rows)]
                + kernel[1:2] * grad_conv[k, i, pl.ds(1, rows)]
                + kernel[2:3] * grad_conv[k, i, pl.ds(2, rows)]
            )
    load_joined.wait()

    def first_chunk(which):
        at = pl.ds(pl.multiple_of(which * rows, rows), rows)
        parts = split(grad_hidden[at, 0 : 3 * channels])

        def tile(columns):
            active[at, columns] = dot_three(parts, split(weight_c[0 : 3 * channels, columns]), PLAIN)

        tiles(model, tile)

    first_sum = HeadSum(comm, place, active, from_sibling.at[2], from_facing.at[2], rows)
    first_chunk(1 - core)
    first_sum.lend()
    first_chunk(core)
    first_sum.chip()
    crew.advance()
    for i in range(sequences):
        normed_two[chunk(i)] = unit_rows(inputs[order[i]])[0] * as_row(first_gain) + as_row(first_shift)
    projected_parts = split(grad_hidden[:, 0 : 3 * channels])

    def joined_tile(columns):
        grad_rest[channels : 4 * channels, columns] = dot_three(
            projected_parts, split(normed_two[:, columns]), BOTH_FIRST
        )

    tiles(model, joined_tile)
    add_sums(3, grad_rest, rest_out)
    crew.advance()
    crew.advance()

    pieces = swaps[: second_sum.pieces]
    for made in pieces:
        comm.settle(made)
    returned = []
    for p in range(first_sum.pieces):
        at = own_piece(p, first_sum.size)
        incoming = first_sum.piece(p)
        here = pl.ds(p * first_sum.size, first_sum.size)
        rows_in = jnp.where(core == 0, inputs[order[0], here], inputs[order[1], here])
        unit, inverse = unit_rows(rows_in)
        grad_inputs[at] = grad_inputs[at] + norm_back(incoming, as_row(first_gain), unit, inverse)
        late_out[0:1] = late_out[0:1] + down_rows(incoming * unit)
        late_out[1:2] = late_out[1:2] + down_rows(incoming)
        returned.append(comm.copy(grad_inputs.at[at], grad_inputs.at[at], place.sibling))
        crew.advance()
    late_sent = comm.copy(late_out, late_from, place.sibling)
    crew.advance()
    late_sent.wait_recv()
    late_all[seq] = late_out[...] + late_from[...]
    mine = late_all.at[seq]
    shared = [comm.copy(mine, mine, device) for device, _ in column]
    crew.drain()
    for made in swaps[second_sum.pieces :] + returned + shared:
        made.wait_recv()
    comm.settle(late_sent)
    total = late_all[0]
    for k in range(1, devices):
        total = total + late_all[k]
    late_out[...] = total
    comm.finish()


def sum_plan(hidden_units, model, channels):
    size = 96
    plan = [(True, 0, k * size, size, k) for k in range(hidden_units // size)]
    plan += [(False, 1, k * size, size, k + 1) for k in range(model // size)]
    plan += [(True, 2, 0, channels // 2, 2), (False, 2, channels // 2, channels // 2, 2)]
    size = channels // 2
    plan += [(True, 3, channels + k * size, size, k) for k in range(3)]
    plan += [(False, 3, channels + (3 + k) * size, size + 16 * (k == 2), k) for k in range(3)]
    return plan


def back(ends, collective, lengths, inputs, cotangent, kept, vectors, kernels, inner_weight, outer_weight, output_weight):
    keyvals, queries, raw, attended, attended_turned, log_total, weights, joined = kept
    sequences, rows, model = inputs.shape
    channels = output_weight.shape[0]
    heads = channels // HSIZE
    hidden_units = inner_weight.shape[1]
    tokens = sequences * rows
    devices = lax.axis_size("seq")
    rest_rows = 4 * channels + 16
    plan = sum_plan(hidden_units, model, channels)
    land_rows = sum(3 * count // 2 if pair_first else 2 * count for pair_first, _, _, count, _ in plan)
    vmem = pl.BlockSpec(memory_space=pltpu.VMEM)
    far = pl.BlockSpec(memory_space=pl.ANY)

    def f32(*shape):
        return jax.ShapeDtypeStruct(shape, jnp.float32)

    def room(*shape, dtype=jnp.float32):
        return pltpu.VMEM(shape, dtype)

    edge = 8
    grad_rows = channels + 16
    half = functools.partial(room, dtype=jnp.bfloat16)
    return pl.pallas_call(
        functools.partial(back_kernel, ends, plan),
        out_shape=[
            f32(tokens, model),
            f32(tokens, model),
            f32(hidden_units, model),
            f32(model, hidden_units),
            f32(rest_rows, model),
            f32(8, model),
            f32(devices, sequences, channels, rows),
            f32(devices, sequences, grad_rows, rows),
        ],
        in_specs=[pl.BlockSpec(memory_space=pltpu.SMEM)] + [vmem] * 17 + [far] * 6,
        out_specs=[vmem] * 2 + [far] * 3 + [vmem] + [far] * 2,
        scratch_shapes=[
            room(model, model),
            room(model, hidden_units),
            room(hidden_units, model),
            room(3, sequences, rows + edge, channels),
            room(4, rows, sequences * channels),
            room(tokens, model),
            room(tokens, hidden_units),
            room(tokens, hidden_units),
            room(tokens, model),
            room(3, rows, model),
            room(3, rows, model),
            room(hidden_units, model),
            room(model, hidden_units),
            room(rest_rows, model),
            room(land_rows, model),
            room(2, rows, 2 * channels),
            room(sequences, rows, 2 * channels),
            room(2 * sequences, channels, rows),
            room(2 * sequences, grad_rows, rows),
            half(sequences, heads, 3 * HSIZE, rows),
            half(sequences, heads, 3 * HSIZE, rows),
            half(sequences, heads, rows, 256),
            half(sequences, heads, rows, 256),
            room(sequences, grad_rows, rows),
            room(sequences, channels, rows),
            room(sequences, 2 * channels, rows),
            room(3, sequences, rows + edge, channels),
            room(8, model),
            room(devices, 8, model),
            pltpu.SemaphoreType.DMA((256,)),
            pltpu.SemaphoreType.DMA((256,)),
            pltpu.SemaphoreType.DMA((64,)),
            pltpu.SemaphoreType.DMA((4 * sequences,)),
        ],
        compiler_params=pltpu.CompilerParams(
            collective_id=collective, has_side_effects=True, vmem_limit_bytes=63 * 2**20
        ),
        name="back",
    )(
        lengths,
        inputs,
        cotangent,
        attended,
        attended_turned,
        queries,
        log_total,
        output_weight,
        *vectors,
        *kernels,
        keyvals,
        weights,
        inner_weight,
        outer_weight,
        joined,
        raw,
    )


def shards(
    inputs,
    seq_lengths,
    first_gain,
    first_shift,
    query_weight,
    key_weight,
    value_weight,
    query_kernel,
    key_kernel,
    value_kernel,
    output_weight,
    output_bias,
    second_gain,
    second_shift,
    inner_weight,
    hidden_layer_bias,
    outer_weight,
    outer_bias,
    cotangent,
):
    channels = query_weight.shape[1]
    kernels = (query_kernel, key_kernel, value_kernel)

    def run(short_end, collective):
        ends = (LINE, short_end)
        kept = front(
            ends,
            collective,
            seq_lengths,
            inputs,
            first_gain,
            first_shift,
            (query_weight, key_weight, value_weight),
            kernels,
            output_weight,
        )
        result, grad_inputs, grad_outer, grad_inner, rest, late = back(
            ends,
            collective + 1,
            seq_lengths,
            inputs,
            cotangent,
            kept,
            (
                output_bias,
                first_gain,
                first_shift,
                second_gain,
                second_shift,
                hidden_layer_bias,
                outer_bias,
            ),
            kernels,
            inner_weight,
            outer_weight,
            output_weight,
        )[:6]
        swap = seq_lengths[1] > seq_lengths[0]

        def placed(array):
            array = array.reshape(inputs.shape)
            return jnp.where(swap, jnp.flip(array, 0), array)

        vectors = rest[4 * channels :]
        mixes = vectors[3:6, : 3 * channels]
        return (
            placed(result),
            placed(grad_inputs),
            late[0],
            late[1],
            rest[channels : 2 * channels].T,
            rest[2 * channels : 3 * channels].T,
            rest[3 * channels : 4 * channels].T,
            mixes[:, :channels],
            mixes[:, channels : 2 * channels],
            mixes[:, 2 * channels :],
            rest[:channels],
            vectors[0],
            late[2],
            late[3],
            grad_inner,
            vectors[2],
            grad_outer,
            vectors[1],
        )

    pair_rows = 2 * inputs.shape[1]
    shorter = jnp.minimum(seq_lengths[0], seq_lengths[1])
    reach = (shorter > pair_rows).astype(jnp.int32) + (shorter > 2 * pair_rows)
    cases = [functools.partial(run, end, 1 + 2 * k) for k, end in enumerate((1, 2, LINE))]
    return lax.switch(reach, cases)


def solution(mesh):
    lines = mesh.shape["seq"] == 2 * LINE and mesh.shape["head"] == 4
    return jax.shard_map(
        shards if lines else general_shards,
        mesh=mesh,
        in_specs=(
            P(None, "seq", None),
            P(),
            P(),
            P(),
            P(None, "head"),
            P(None, "head"),
            P(None, "head"),
            P(None, "head"),
            P(None, "head"),
            P(None, "head"),
            P("head", None),
            P(),
            P(),
            P(),
            P(None, "head"),
            P("head"),
            P("head", None),
            P(),
            P(None, "seq", None),
        ),
        out_specs=(
            P(None, "seq", None),
            P(None, "seq", None),
            P(),
            P(),
            P(None, "head"),
            P(None, "head"),
            P(None, "head"),
            P(None, "head"),
            P(None, "head"),
            P(None, "head"),
            P("head", None),
            P(),
            P(),
            P(),
            P(None, "head"),
            P("head"),
            P("head", None),
            P(),
        ),
        check_vma=False,
    )
```

```python
import functools

import jax
import jax.numpy as jnp
from jax import lax
from jax.experimental import pallas as pl
from jax.experimental.pallas import tpu as pltpu
from jax.sharding import PartitionSpec as P

MESH = pl.DeviceIdType.MESH

HSIZE = 64


EXACT_FLOAT_MODE = lax.Precision.HIGH
EPSILON = 1e-05
NEGATIVE = -1e30


def shifted(block, axis, distance):
    devices = range(lax.axis_size(axis))
    route = [(i - distance, i) for i in devices if i - distance in devices]
    return lax.ppermute(block, axis, route)


def matmul(input_operand, weight_matrix):
    return jnp.einsum("scd,df->scf", input_operand, weight_matrix, precision=EXACT_FLOAT_MODE)


def transposed(input_operand, weight_matrix):
    return jnp.einsum("scf,df->scd", input_operand, weight_matrix, precision=EXACT_FLOAT_MODE)


def outer_sum(first_rows, second_rows):
    return jnp.einsum("scd,scf->df", first_rows, second_rows, precision=EXACT_FLOAT_MODE)


def normalize(stream, norm_gain, norm_shift):
    centered = stream - jnp.mean(stream, -1, keepdims=True)
    inverse = lax.rsqrt(jnp.mean(centered * centered, -1, keepdims=True) + EPSILON)
    unit_rows = centered * inverse
    return (unit_rows * norm_gain + norm_shift, unit_rows, inverse)


def normalize_back(gradient, norm_gain, unit_rows, inverse):
    scaled = gradient * norm_gain
    middle = (
        scaled
        - jnp.mean(scaled, -1, keepdims=True)
        - unit_rows * jnp.mean(scaled * unit_rows, -1, keepdims=True)
    )
    return (inverse * middle, jnp.sum(gradient * unit_rows, (0, 1)), jnp.sum(gradient, (0, 1)))


def split_heads(flat):
    return flat.reshape(flat.shape[0], flat.shape[1], flat.shape[2] // HSIZE, HSIZE)


def allowed_pairs(query_pos, key_pos, lengths):
    return (key_pos[None, None, :] <= query_pos[None, :, None]) & (
        key_pos[None, None, :] < lengths[:, None, None]
    )


def pair_terms(queries, gradients, log_total, row_dots, query_pos, keyvals, key_pos, lengths):
    channels = queries.shape[2]
    query_heads = split_heads(queries)
    key_heads = split_heads(keyvals[:, :, :channels])
    value_heads = split_heads(keyvals[:, :, channels:])
    grad_heads = split_heads(gradients)
    scores = jnp.einsum(
        "sqhe,skhe->shqk", query_heads, key_heads, precision=EXACT_FLOAT_MODE
    ) * HSIZE ** (-0.5)
    allowed = allowed_pairs(query_pos, key_pos, lengths)[:, None]
    weight_values = jnp.exp(jnp.where(allowed, scores - log_total[..., None], NEGATIVE))
    weight_grads = jnp.einsum(
        "sqhe,skhe->shqk", grad_heads, value_heads, precision=EXACT_FLOAT_MODE
    )
    score_grads = weight_values * (weight_grads - row_dots[..., None])
    return (weight_values, score_grads, query_heads, key_heads, grad_heads)


def key_facing_term(terms, keyvals, channels):
    value_part = jnp.einsum("shqk,sqhe->skhe", terms[0], terms[4], precision=EXACT_FLOAT_MODE)
    key_part = jnp.einsum(
        "shqk,sqhe->skhe", terms[1], terms[2], precision=EXACT_FLOAT_MODE
    ) * HSIZE ** (-0.5)
    shape = (keyvals.shape[0], keyvals.shape[1], channels)
    return jnp.concatenate([key_part.reshape(shape), value_part.reshape(shape)], 2)


def query_side_term(terms):
    return jnp.einsum(
        "shqk,skhe->sqhe", terms[1], terms[3], precision=EXACT_FLOAT_MODE
    ) * HSIZE ** (-0.5)


def key_terms(queries, gradients, log_total, row_dots, query_pos, keyvals, key_pos, lengths):
    terms = pair_terms(
        queries, gradients, log_total, row_dots, query_pos, keyvals, key_pos, lengths
    )
    return key_facing_term(terms, keyvals, queries.shape[2])


def general_shards(
    inputs,
    seq_lengths,
    first_gain,
    first_shift,
    query_weight,
    key_weight,
    value_weight,
    query_kernel,
    key_kernel,
    value_kernel,
    output_weight,
    output_bias,
    second_gain,
    second_shift,
    inner_weight,
    hidden_layer_bias,
    outer_weight,
    outer_bias,
    cotangent,
):
    sequences, rows, model = inputs.shape
    channels = query_weight.shape[1]
    heads = channels // HSIZE
    positions = lax.axis_index("seq") * rows + jnp.arange(rows, dtype=jnp.int32)
    live_rows = (positions[None, :] < seq_lengths[:, None]).astype(jnp.float32)
    joined_weight = jnp.concatenate([query_weight, key_weight, value_weight], 1)
    joined_kernel = jnp.concatenate([query_kernel, key_kernel, value_kernel], 1)
    normed, leading_unit_value, first_inverse = normalize(inputs, first_gain, first_shift)
    projected = matmul(normed, joined_weight)
    rims = shifted(projected[:, rows - 2 :, :], "seq", 1)
    extended = jnp.concatenate([rims, projected], 1)
    convolved = (
        joined_kernel[0] * extended[:, 2:]
        + joined_kernel[1] * extended[:, 1:-1]
        + joined_kernel[2] * extended[:, :-2]
    )
    queries = convolved[:, :, :channels]
    keyvals = convolved[:, :, channels:]
    query_heads = split_heads(queries)
    portion = lax.all_gather(keyvals, "seq", axis=1, tiled=True)
    highest = jnp.full((sequences, heads, rows), NEGATIVE, jnp.float32)
    key_pos = jnp.arange(portion.shape[1], dtype=jnp.int32)
    key_heads = split_heads(portion[:, :, :channels])
    value_heads = split_heads(portion[:, :, channels:])
    scores = jnp.einsum(
        "sqhe,skhe->shqk", query_heads, key_heads, precision=EXACT_FLOAT_MODE
    ) * HSIZE ** (-0.5)
    allowed = allowed_pairs(positions, key_pos, seq_lengths)[:, None]
    masked = jnp.where(allowed, scores, NEGATIVE)
    new_high = jnp.maximum(highest, jnp.max(masked, -1))
    weight_values = jnp.where(allowed, jnp.exp(masked - new_high[..., None]), 0.0)
    summed = jnp.sum(weight_values, -1)
    weighted = jnp.einsum("shqk,skhe->shqe", weight_values, value_heads, precision=EXACT_FLOAT_MODE)
    highest, summed, weighted = (new_high, summed, weighted)
    log_total = highest + jnp.log(summed)
    attended = (weighted / summed[..., None]).transpose(0, 2, 1, 3).reshape(
        sequences, rows, channels
    ) * live_rows[..., None]
    branch = lax.psum(matmul(attended, output_weight), "head")
    mixed = inputs + branch + output_bias
    normed_two, second_unit, second_inverse = normalize(mixed, second_gain, second_shift)
    hidden = matmul(normed_two, inner_weight) + hidden_layer_bias
    rectified = jnp.maximum(hidden, 0.0)
    active = rectified * rectified
    result = mixed + lax.psum(matmul(active, outer_weight), "head") + outer_bias
    grad_outer_weight = outer_sum(active, cotangent)
    grad_outer_bias = jnp.sum(cotangent, (0, 1))
    grad_hidden = transposed(cotangent, outer_weight) * (2.0 * rectified)
    grad_inner_weight = outer_sum(normed_two, grad_hidden)
    grad_inner_bias = jnp.sum(grad_hidden, (0, 1))
    grad_normed_two = lax.psum(transposed(grad_hidden, inner_weight), "head")
    through_two, grad_second_gain, grad_second_shift = normalize_back(
        grad_normed_two, second_gain, second_unit, second_inverse
    )
    grad_mixed = cotangent + through_two
    grad_output_weight = outer_sum(attended, grad_mixed)
    grad_output_bias = jnp.sum(grad_mixed, (0, 1))
    grad_attended = transposed(grad_mixed, output_weight) * live_rows[..., None]
    row_dots = jnp.sum(split_heads(grad_attended) * split_heads(attended), -1).transpose(0, 2, 1)
    terms = pair_terms(
        queries, grad_attended, log_total, row_dots, positions, portion, key_pos, seq_lengths
    )
    grad_queries = query_side_term(terms).reshape(jnp.zeros_like(queries).shape)
    query_side = jnp.concatenate([queries, grad_attended], 2)
    row_stats = jnp.concatenate([log_total, row_dots], 1).transpose(0, 2, 1)
    side_rows = lax.all_gather(query_side, "seq", axis=1, tiled=True)
    stat_rows = lax.all_gather(row_stats, "seq", axis=1, tiled=True)
    query_pos = jnp.arange(side_rows.shape[1], dtype=jnp.int32)
    portion_total = stat_rows[:, :, :heads].transpose(0, 2, 1)
    portion_dots = stat_rows[:, :, heads:].transpose(0, 2, 1)
    grad_keyvals = key_terms(
        side_rows[:, :, :channels],
        side_rows[:, :, channels:],
        portion_total,
        portion_dots,
        query_pos,
        keyvals,
        positions,
        seq_lengths,
    )
    grad_convolved = jnp.concatenate([grad_queries, grad_keyvals], 2)
    following = shifted(grad_convolved[:, :2, :], "seq", -1)
    grad_extended = jnp.concatenate([grad_convolved, following], 1)
    grad_projected = (
        joined_kernel[0] * grad_extended[:, :rows]
        + joined_kernel[1] * grad_extended[:, 1 : rows + 1]
        + joined_kernel[2] * grad_extended[:, 2:]
    )
    grad_kernel = jnp.stack(
        [
            jnp.sum(grad_convolved * extended[:, 2:], (0, 1)),
            jnp.sum(grad_convolved * extended[:, 1:-1], (0, 1)),
            jnp.sum(grad_convolved * extended[:, :-2], (0, 1)),
        ]
    )
    grad_joined = outer_sum(normed, grad_projected)
    grad_normed = lax.psum(transposed(grad_projected, joined_weight), "head")
    through_one, grad_first_gain, grad_first_shift = normalize_back(
        grad_normed, first_gain, leading_unit_value, first_inverse
    )
    grad_inputs = grad_mixed + through_one
    grad_query_weight = grad_joined[:, :channels]
    grad_key_weight = grad_joined[:, channels : 2 * channels]
    grad_value_weight = grad_joined[:, 2 * channels :]
    grad_query_kernel = grad_kernel[:, :channels]
    grad_key_kernel = grad_kernel[:, channels : 2 * channels]
    grad_value_kernel = grad_kernel[:, 2 * channels :]
    (
        grad_first_gain,
        grad_first_shift,
        grad_query_weight,
        grad_key_weight,
        grad_value_weight,
        grad_query_kernel,
        grad_key_kernel,
        grad_value_kernel,
        grad_output_weight,
        grad_output_bias,
        grad_second_gain,
        grad_second_shift,
        grad_inner_weight,
        grad_inner_bias,
        grad_outer_weight,
        grad_outer_bias,
    ) = lax.psum(
        (
            grad_first_gain,
            grad_first_shift,
            grad_query_weight,
            grad_key_weight,
            grad_value_weight,
            grad_query_kernel,
            grad_key_kernel,
            grad_value_kernel,
            grad_output_weight,
            grad_output_bias,
            grad_second_gain,
            grad_second_shift,
            grad_inner_weight,
            grad_inner_bias,
            grad_outer_weight,
            grad_outer_bias,
        ),
        "seq",
    )
    return (
        result,
        grad_inputs,
        grad_first_gain,
        grad_first_shift,
        grad_query_weight,
        grad_key_weight,
        grad_value_weight,
        grad_query_kernel,
        grad_key_kernel,
        grad_value_kernel,
        grad_output_weight,
        grad_output_bias,
        grad_second_gain,
        grad_second_shift,
        grad_inner_weight,
        grad_inner_bias,
        grad_outer_weight,
        grad_outer_bias,
    )


class Comm:
    def __init__(self, send_sems, recv_sems, local_sems=None):
        self.send_sems, self.recv_sems, self.local_sems = send_sems, recv_sems, local_sems
        self.used = 0
        self.used_local = 0
        self.sent = []
        self.stored = []

    def copy(self, source, target, device, when=None):
        index = self.used
        self.used += 1
        made = pltpu.make_async_remote_copy(
            src_ref=source,
            dst_ref=target,
            send_sem=self.send_sems.at[index],
            recv_sem=self.recv_sems.at[index],
            device_id=device,
            device_id_type=MESH,
        )
        if when is None:
            made.start()
        else:
            pl.when(when)(made.start)
        self.sent.append((made, when))
        return made

    def settle(self, made):
        self.sent = [one for one in self.sent if one[0] is not made]
        made.wait_send()

    def local(self, source, target, when=None, keep=True):
        made = pltpu.make_async_copy(source, target, self.local_sems.at[self.used_local])
        self.used_local += 1
        if when is None:
            made.start()
        else:
            pl.when(when)(made.start)
        if keep:
            self.stored.append((made, when))
        return made

    def finish(self):
        for made, when in self.sent:
            if when is None:
                made.wait_send()
            else:
                pl.when(when)(made.wait_send)
        for made, when in self.stored:
            if when is None:
                made.wait()
            else:
                pl.when(when)(made.wait)


def wait_for(made, when=None):
    if when is None:
        made.wait_recv()
    else:
        pl.when(when)(made.wait_recv)


class Place:
    def __init__(self):
        self.seq = lax.axis_index("seq")
        self.head = lax.axis_index("head")
        self.z = self.seq // 2
        self.y = self.seq % 2
        self.other = 1 - self.y
        self.core = self.head % 2
        self.at_end = (self.z == 0) | (self.z == LINE - 1)
        self.at_middle = jnp.logical_not(self.at_end)
        step = 2 - 4 * (self.z // 2)
        self.pair = (2 * self.z + self.other, self.head)
        self.inward = (self.seq + step, self.head)
        self.outward = (self.seq - step, self.head)
        self.sibling = (self.seq, self.head + 1 - 2 * self.core)
        self.facing = (self.seq, (self.head + 2) % 4)


LINE = 4


def rows_at(ref, start, count):
    return ref.at[pl.ds(pl.multiple_of(start, 8), count)]


class Land:
    def __init__(self, ref):
        self.ref, self.used = ref, 0

    def take(self, rows):
        got = self.ref.at[pl.ds(self.used, rows)]
        self.used += rows
        return got


def sum_pair_first(comm, place, land, source, target, start, count):
    half = count // 2
    line, from_end, from_middle = land.take(half), land.take(half), land.take(half)
    own = rows_at(target, start + place.y * half, half)
    far = rows_at(source, start + place.other * half, half)
    near = rows_at(source, start + place.y * half, half)
    made = comm.copy(far, line, place.pair)
    yield
    made.wait_recv()
    line[...] = line[...] + near[...]
    inward = comm.copy(line, from_end, place.inward, place.at_end)
    yield

    @pl.when(place.at_middle)
    def _():
        inward.wait_recv()
        from_end[...] = from_end[...] + line[...]

    across = comm.copy(from_end, from_middle, place.inward, place.at_middle)
    yield

    @pl.when(place.at_middle)
    def _():
        across.wait_recv()
        from_middle[...] = from_middle[...] + from_end[...]

    outward = comm.copy(from_middle, own, place.outward, place.at_middle)
    early = comm.copy(from_middle, own, place.pair, place.at_middle)
    comm.local(from_middle, own, place.at_middle)
    yield
    wait_for(outward, place.at_end)
    late = comm.copy(own, own, place.pair, place.at_end)
    yield
    wait_for(early, place.at_middle)
    wait_for(late, place.at_end)
    yield


def sum_line_first(comm, place, land, source, target, start, count):
    half = count // 2
    whole, from_middle, from_pair = land.take(count), land.take(half), land.take(half)
    all_rows = rows_at(source, start, count)
    mine, theirs = place.z // 2, 1 - place.z // 2
    own, rest = rows_at(target, start + mine * half, half), rows_at(target, start + theirs * half, half)
    inward = comm.copy(all_rows, whole, place.inward, place.at_end)
    yield

    @pl.when(place.at_middle)
    def _():
        inward.wait_recv()
        whole[...] = whole[...] + all_rows[...]

    across = comm.copy(rows_at(whole, theirs * half, half), from_middle, place.inward, place.at_middle)
    yield

    @pl.when(place.at_middle)
    def _():
        across.wait_recv()
        from_middle[...] = from_middle[...] + rows_at(whole, mine * half, half)[...]

    paired = comm.copy(from_middle, from_pair, place.pair, place.at_middle)
    yield

    @pl.when(place.at_middle)
    def _():
        paired.wait_recv()
        from_pair[...] = from_pair[...] + from_middle[...]

    back = comm.copy(from_pair, own, place.inward, place.at_middle)
    outward = comm.copy(from_pair, own, place.outward, place.at_middle)
    comm.local(from_pair, own, place.at_middle)
    yield
    wait_for(back, place.at_middle)
    last = comm.copy(rest, rest, place.outward, place.at_middle)
    yield
    wait_for(outward, place.at_end)
    wait_for(last, place.at_end)
    yield


class Crew:
    def __init__(self):
        self.due = []
        self.now = 0.0
        self.added = 0

    def add(self, one, delay=0.0, hop=6.0):
        self.added += 1
        self.due.append((self.now + delay, self.added, one, hop))

    def step(self):
        entry = min(self.due, key=lambda each: each[:2])
        self.due.remove(entry)
        time, number, one, hop = entry
        try:
            next(one)
            self.due.append((time + hop, number, one, hop))
        except StopIteration:
            pass

    def tick(self, length):
        self.now += length
        while self.due and min(each[0] for each in self.due) <= self.now:
            self.step()

    def drain(self):
        while self.due:
            self.step()


def split(value):
    high = value.astype(jnp.bfloat16)
    return high, (value - high.astype(jnp.float32)).astype(jnp.bfloat16)


def dot(left, right, dims):
    return lax.dot_general(left, right, (dims, ((), ())), preferred_element_type=jnp.float32)


def dot_three(left, right, dims):
    return dot(left[0], right[0], dims) + (dot(left[0], right[1], dims) + dot(left[1], right[0], dims))


PLAIN, BOTH_LAST, BOTH_FIRST = ((1,), (0,)), ((1,), (1,)), ((0,), (0,))


def product(left, right, dims=PLAIN):
    return dot_three(split(left), split(right), dims)


def beside(value):
    high, low = split(value)
    return jnp.concatenate([high, high, low], 1)


def against(value):
    high, low = split(value)
    return jnp.concatenate([high, low, high], 0)


def as_row(ref):
    return ref[...].reshape(1, ref.shape[0])


def unit_rows(rows):
    centered = rows - jnp.mean(rows, -1, keepdims=True)
    inverse = lax.rsqrt(jnp.mean(centered * centered, -1, keepdims=True) + EPSILON)
    return centered * inverse, inverse


def longer_first(lengths):
    return jnp.where(lengths[1] > lengths[0], 1, 0).astype(jnp.int32)


def head_lanes(head, base=0):
    return slice(base + head * HSIZE, base + (head + 1) * HSIZE)


class Spread:
    def __init__(self, comm, place, part, ends, upward=True, own=None):
        self.comm, self.place, self.part, self.ends = comm, place, part, ends
        self.own = own or (lambda half: part(place.seq, half))
        z, y = place.z, place.y
        self.rank = z if upward else ends - 1 - z
        self.inside = z < ends
        self.more = self.inside & ((z < ends - 1) if upward else (z > 0))
        self.leads = (y == 0) if upward else (y == 1)
        self.next = (place.seq + (2 if upward else -2), place.head)
        self.sign = 1 if upward else -1
        self.up = {}
        self.over = {}

    def block(self, level, slot):
        place = self.place
        side = place.y if slot == 0 else place.other
        return 2 * (place.z - self.sign * level) + side

    def begin(self):
        comm, place, part = self.comm, self.place, self.part
        near, far = part(place.seq, place.y), part(place.seq, place.other)
        mine = self.own(place.y)
        self.lend = comm.copy(self.own(place.other), far, place.pair, self.inside & (self.more | self.leads))
        self.up[1, 0] = comm.copy(mine, near, self.next, self.more)
        self.give = comm.copy(mine, near, place.pair, self.inside & self.leads)

    def pass_pair(self):
        comm, place, part = self.comm, self.place, self.part
        follows = jnp.logical_not(self.leads)
        wait_for(self.lend, self.inside & (self.more | follows))
        lent = part(self.block(0, 1), place.y)
        self.up[1, 1] = comm.copy(lent, lent, self.next, self.more)

    def have_pair(self):
        wait_for(self.give, self.inside & jnp.logical_not(self.leads))

    def pass_level(self, level):
        comm, place, part = self.comm, self.place, self.part
        here = self.inside & (self.rank >= level)
        for slot in range(2):
            half = part(self.block(level, slot), place.y)
            wait_for(self.up[level, slot], here)
            if level < LINE - 1:
                self.up[level + 1, slot] = comm.copy(half, half, self.next, here & self.more)
            self.over[level, slot] = comm.copy(half, half, place.pair, here)

    def have_level(self, level):
        here = self.inside & (self.rank >= level)
        for slot in range(2):
            wait_for(self.over[level, slot], here)


def greet(partners):
    barrier = pltpu.get_barrier_semaphore()
    count = jnp.int32(0)
    for device, when in partners:
        def tell(device=device):
            pl.semaphore_signal(barrier, inc=1, device_id=device, device_id_type=MESH)

        if when is None:
            tell()
            count = count + 1
        else:
            pl.when(when)(tell)
            count = count + when.astype(jnp.int32)
    pl.semaphore_wait(barrier, count)


def line_partners(place):
    return [
        (place.pair, None),
        ((place.seq + 2, place.head), place.z < LINE - 1),
        ((place.seq - 2, place.head), place.z > 0),
    ]


def head_partners(place):
    return [(place.sibling, None), (place.facing, None)]


def step_partners(place):
    return [
        ((place.seq + 1, place.head), (place.y == 1) & (place.z < LINE - 1)),
        ((place.seq - 1, place.head), (place.y == 0) & (place.z > 0)),
    ]


def front_kernel(
    ends,
    lengths,
    inputs,
    gain,
    shift,
    query_weight,
    key_weight,
    value_weight,
    query_kernel,
    key_kernel,
    value_kernel,
    output_weight,
    keyvals,
    queries,
    raw,
    attended,
    attended_turned,
    log_total,
    weights,
    joined,
    halo,
    rows_high,
    rows_low,
    query_cat,
    highest,
    summed,
    weighted,
    send_sems,
    recv_sems,
):
    place = Place()
    comm = Comm(send_sems, recv_sems)
    sequences, rows, model = inputs.shape
    channels = query_weight.shape[0]
    heads = channels // HSIZE
    edge = halo.shape[1]
    first = longer_first(lengths)
    order = (first, 1 - first)
    greet(line_partners(place) + head_partners(place) + step_partners(place))
    rim = comm.copy(
        inputs.at[:, pl.ds(rows - edge, edge)],
        halo,
        (place.seq + 1, place.head),
        place.seq < 2 * LINE - 1,
    )
    own_weight = rows_at(weights, place.head * channels, channels)
    own_weight[...] = output_weight[...]
    to_sibling = comm.copy(own_weight, own_weight, place.sibling)
    to_facing = comm.copy(own_weight, own_weight, place.facing)

    def normal(value):
        return unit_rows(value)[0] * as_row(gain) + as_row(shift)

    for i in range(sequences):
        high, low = split(normal(inputs[order[i]]))
        rows_high[pl.ds(i * rows, rows)] = high
        rows_low[pl.ds(i * rows, rows)] = low
    wait_for(rim, place.seq > 0)
    inner = (place.seq > 0).astype(jnp.float32)
    rim_rows = jnp.concatenate([normal(halo[order[i]]) for i in range(sequences)], 0)
    rim_split = split(rim_rows)
    for k, weight in enumerate((query_weight, key_weight, value_weight)):
        parts = split(weight[...])
        whole = dot_three((rows_high[...], rows_low[...]), parts, BOTH_LAST)
        before = dot_three(rim_split, parts, BOTH_LAST) * inner
        for i in range(sequences):
            raw[k, i, pl.ds(0, edge)] = before[i * edge : (i + 1) * edge]
            raw[k, i, pl.ds(edge, rows)] = whole[i * rows : (i + 1) * rows]

    def convolved(k, i, kernel):
        return (
            kernel[0:1] * raw[k, i, pl.ds(edge, rows)]
            + kernel[1:2] * raw[k, i, pl.ds(edge - 1, rows)]
            + kernel[2:3] * raw[k, i, pl.ds(edge - 2, rows)]
        )

    spreads = []
    for i in range(sequences):
        own = keyvals.at[place.seq, i]
        own[:, 0:channels] = convolved(1, i, key_kernel)
        own[:, channels : 2 * channels] = convolved(2, i, value_kernel)

        def part(block, half, i=i):
            return keyvals.at[block, i, pl.ds(pl.multiple_of(half * (rows // 2), 8), rows // 2)]

        spreads.append(Spread(comm, place, part, ends[i]))
        spreads[i].begin()
    for i in range(sequences):
        query = convolved(0, i, query_kernel).T
        queries[i] = query
        for head in range(heads):
            query_cat[i, head] = against(query[head_lanes(head)] * HSIZE ** (-0.5))
    to_facing.wait_recv()
    theirs = rows_at(weights, place.facing[1] * channels, channels)
    to_last = comm.copy(theirs, theirs, place.sibling)

    def attend(i, block, diagonal):
        own = keyvals.at[block, i]
        for head in range(heads):
            scores = dot(beside(own[:, head_lanes(head)]), query_cat[i, head], PLAIN)
            lane = pl.ds(head, 1)
            if diagonal:
                key_pos = lax.broadcasted_iota(jnp.int32, scores.shape, 0)
                query_pos = lax.broadcasted_iota(jnp.int32, scores.shape, 1)
                scores = jnp.where(key_pos <= query_pos, scores, NEGATIVE)
                high = jnp.max(scores, 0, keepdims=True)
            else:
                old = highest[i, lane]
                high = jnp.maximum(old, jnp.max(scores, 0, keepdims=True))
            powers = jnp.exp(scores - high)
            total = jnp.sum(powers, 0, keepdims=True)
            power_high, power_low = split(powers)
            value_high, value_low = split(own[:, head_lanes(head, channels)])
            both = dot(jnp.concatenate([value_high, value_low], 1), power_high, BOTH_FIRST)
            term = both[:HSIZE] + both[HSIZE:] + dot(value_high, power_low, BOTH_FIRST)
            at = pl.ds(head * HSIZE, HSIZE)
            if diagonal:
                summed[i, lane] = total
                weighted[i, at] = term
            else:
                scale = jnp.exp(old - high)
                summed[i, lane] = summed[i, lane] * scale + total
                weighted[i, at] = weighted[i, at] * scale + term
            highest[i, lane] = high

    def here(i):
        return place.z < ends[i]

    def both(body):
        def step(i, carry):
            body(i)
            return carry

        lax.fori_loop(0, sequences, step, 0)

    for k, weight in enumerate((query_weight, key_weight, value_weight)):
        joined[k * channels : (k + 1) * channels] = weight[...]
    for spread in spreads:
        spread.pass_pair()
    both(lambda i: attend(i, place.seq, True))
    for spread in spreads:
        spread.have_pair()

    for level in range(LINE):
        if level:
            for spread in spreads:
                spread.pass_level(level)
            for spread in spreads:
                spread.have_level(level)

        def blocks(k, carry, level=level):
            i, slot = k // 2, k % 2
            block = 2 * (place.z - level) + slot
            limit = jnp.where(i == 0, ends[0], ends[1])
            if level:
                wanted = (place.z >= level) & (place.z < limit)
            else:
                wanted = (slot == 0) & (place.y == 1) & (place.z < limit)

            @pl.when(wanted)
            def _():
                attend(i, block, False)

            return carry

        lax.fori_loop(0, 2 * sequences, blocks, 0)

    for i in range(sequences):
        live = jnp.minimum(lengths[order[i]] - place.seq * rows, rows)
        alive = (lax.broadcasted_iota(jnp.int32, (1, rows), 1) < live).astype(jnp.float32)
        for head in range(heads):
            at = pl.ds(head * HSIZE, HSIZE)
            total = summed[i, pl.ds(head, 1)]
            weighted[i, at] = weighted[i, at] * (alive / total)
            log_total[i, pl.ds(head, 1)] = highest[i, pl.ds(head, 1)] + jnp.log(total)
        attended_turned[i] = weighted[i]
        attended[:, i * channels : (i + 1) * channels] = weighted[i].T
    to_sibling.wait_recv()
    to_last.wait_recv()
    comm.finish()


def front(ends, collective, lengths, inputs, gain, shift, weights, kernels, output_weight):
    sequences, rows, model = inputs.shape
    channels = output_weight.shape[0]
    heads = channels // HSIZE
    blocks = lax.axis_size("seq")
    groups = lax.axis_size("head")
    edge = 8
    vmem = pl.BlockSpec(memory_space=pltpu.VMEM)

    def f32(*shape):
        return jax.ShapeDtypeStruct(shape, jnp.float32)

    copies = 64
    return pl.pallas_call(
        functools.partial(front_kernel, ends),
        out_shape=[
            f32(blocks, sequences, rows, 2 * channels),
            f32(sequences, channels, rows),
            f32(3, sequences, rows + edge, channels),
            f32(rows, sequences * channels),
            f32(sequences, channels, rows),
            f32(sequences, 8, rows),
            f32(groups * channels, model),
            f32(3 * channels, model),
        ],
        in_specs=[pl.BlockSpec(memory_space=pltpu.SMEM)] + [vmem] * 10,
        out_specs=[vmem] * 8,
        scratch_shapes=[
            pltpu.VMEM((sequences, edge, model), jnp.float32),
            pltpu.VMEM((sequences * rows, model), jnp.bfloat16),
            pltpu.VMEM((sequences * rows, model), jnp.bfloat16),
            pltpu.VMEM((sequences, heads, 3 * HSIZE, rows), jnp.bfloat16),
            pltpu.VMEM((sequences, 8, rows), jnp.float32),
            pltpu.VMEM((sequences, 8, rows), jnp.float32),
            pltpu.VMEM((sequences, channels, rows), jnp.float32),
            pltpu.SemaphoreType.DMA((copies,)),
            pltpu.SemaphoreType.DMA((copies,)),
        ],
        compiler_params=pltpu.CompilerParams(
            collective_id=collective, has_side_effects=True, vmem_limit_bytes=60 * 2**20
        ),
        name="front",
    )(lengths, inputs, gain, shift, *[weight.T for weight in weights], *kernels, output_weight)


class HeadSum:
    def __init__(self, comm, place, partial, from_sibling, from_facing, rows, pieces=4):
        self.comm, self.place, self.partial = comm, place, partial
        self.from_sibling, self.from_facing = from_sibling, from_facing
        self.rows, self.pieces = rows, pieces
        self.size = rows // pieces
        self.near = rows_at(partial, place.core * rows, rows)

    def lend(self):
        far = rows_at(self.partial, (1 - self.place.core) * self.rows, self.rows)
        self.lent = self.comm.copy(far, self.from_sibling, self.place.sibling)

    def chip(self):
        self.lent.wait_recv()
        self.near[...] = self.near[...] + self.from_sibling[...]
        self.sent = []
        for p in range(self.pieces):
            at = pl.ds(p * self.size, self.size)
            self.sent.append(self.comm.copy(self.near.at[at], self.from_facing.at[at], self.place.facing))

    def piece(self, p):
        self.sent[p].wait_recv()
        at = pl.ds(p * self.size, self.size)
        return self.near[at] + self.from_facing[at]


def norm_back(grad, gain, unit, inverse):
    scaled = grad * gain
    return inverse * (
        scaled - jnp.mean(scaled, -1, keepdims=True) - unit * jnp.mean(scaled * unit, -1, keepdims=True)
    )


def spread_steps(spreads):
    for spread in spreads:
        spread.begin()
    yield
    for spread in spreads:
        spread.pass_pair()
    yield
    for level in range(1, LINE):
        for spread in spreads:
            spread.pass_level(level)
        yield


TILE = 256


def tiles(width, body, crew=None, length=0.0):
    if crew is not None:
        for j in range(width // TILE):
            body(pl.ds(j * TILE, TILE))
            crew.tick(length)
        return

    def step(j, carry):
        body(pl.ds(pl.multiple_of(j * TILE, TILE), TILE))
        return carry

    lax.fori_loop(0, width // TILE, step, 0)


def down_rows(value):
    return jnp.sum(value, 0, keepdims=True)


def allowed_from(shape, offset):
    key_pos = lax.broadcasted_iota(jnp.int32, shape, 0)
    query_pos = lax.broadcasted_iota(jnp.int32, shape, 1)
    return key_pos <= query_pos + offset


def back_kernel(
    ends,
    plan,
    lengths,
    inputs,
    cotangent,
    attended,
    attended_turned,
    queries,
    log_total,
    output_weight,
    output_bias,
    first_gain,
    first_shift,
    second_gain,
    second_shift,
    hidden_bias,
    outer_bias,
    query_kernel,
    key_kernel,
    value_kernel,
    keyvals,
    weights,
    inner_weight,
    outer_weight,
    joined,
    raw_far,
    result,
    grad_inputs,
    outer_out,
    inner_out,
    rest_out,
    late_out,
    all_queries,
    all_grads,
    weight_a,
    weight_b,
    weight_c,
    raw,
    groups,
    normed_two,
    active,
    grad_hidden,
    grad_normed,
    from_sibling,
    from_facing,
    grad_outer,
    grad_inner,
    grad_rest,
    land_ref,
    key_slots,
    own_keys,
    query_slots,
    grad_slots,
    query_cat,
    grad_cat,
    key_cat,
    value_cat,
    grad_att,
    grad_query,
    grad_keyval,
    grad_conv,
    late_from,
    late_all,
    send_sems,
    recv_sems,
    local_sems,
    slot_sems,
):
    place = Place()
    comm = Comm(send_sems, recv_sems, local_sems)
    land = Land(land_ref)
    crew = Crew()
    sequences, rows, model = inputs.shape
    channels = output_weight.shape[0]
    heads = channels // HSIZE
    hidden_units = hidden_bias.shape[0]
    tokens = sequences * rows
    z, y, seq, core = place.z, place.y, place.seq, place.core
    first = longer_first(lengths)
    order = (first, 1 - first)
    devices = 2 * LINE
    column = [((lax.rem(seq + k, devices), place.head), None) for k in range(1, devices)]
    greet(column + head_partners(place))

    load_a = comm.local(weights, weight_a, keep=False)
    load_b = comm.local(inner_weight, weight_b, keep=False)
    load_c = comm.local(outer_weight, weight_c, keep=False)
    load_raw = comm.local(raw_far, raw, keep=False)
    load_own = [comm.local(keyvals.at[seq, i], own_keys.at[i], keep=False) for i in range(sequences)]
    keep_query = [comm.local(queries.at[i], all_queries.at[seq, i], keep=False) for i in range(sequences)]

    to_sibling = comm.copy(attended, groups.at[place.head], place.sibling)
    to_facing = comm.copy(attended, groups.at[place.head], place.facing)

    def query_part(block, half, i):
        return all_queries.at[block, i, pl.ds(pl.multiple_of(half * (channels // 2), 8), channels // 2)]

    def grad_part(block, half, i):
        size = grad_att.shape[1] // 2
        return all_grads.at[block, i, pl.ds(pl.multiple_of(half * size, 8), size)]

    def query_own(half, i):
        return queries.at[i, pl.ds(pl.multiple_of(half * (channels // 2), 8), channels // 2)]

    def grad_own(half, i):
        size = grad_att.shape[1] // 2
        return grad_att.at[i, pl.ds(pl.multiple_of(half * size, 8), size)]

    query_spreads = [
        Spread(
            comm,
            place,
            functools.partial(query_part, i=i),
            ends[i],
            False,
            functools.partial(query_own, i=i),
        )
        for i in range(sequences)
    ]
    grad_spreads = [
        Spread(
            comm,
            place,
            functools.partial(grad_part, i=i),
            ends[i],
            False,
            functools.partial(grad_own, i=i),
        )
        for i in range(sequences)
    ]
    crew.add(spread_steps(query_spreads), 0.0, 4.0)
    crew.tick(0.0)

    def chunk(i):
        return pl.ds(i * rows, rows)

    def add_group(ref, weight_ref, total, begin):
        parts = split(weight_ref[...])
        for i in range(sequences):
            piece = split(ref[:, i * channels : (i + 1) * channels])
            term = dot_three(piece, parts, PLAIN)
            total[chunk(i)] = term if begin else total[chunk(i)] + term

    add_group(attended, output_weight, grad_inputs, True)
    crew.tick(3.0)
    load_a.wait()

    def group_weight(group):
        return rows_at(weight_a, group * channels, channels)

    sibling, facing = place.sibling[1], place.facing[1]
    last = facing + 1 - 2 * (facing % 2)
    to_sibling.wait_recv()
    add_group(groups.at[sibling], group_weight(sibling), grad_inputs, False)
    to_facing.wait_recv()
    onward = comm.copy(groups.at[facing], groups.at[facing], place.sibling)
    add_group(groups.at[facing], group_weight(facing), result, True)
    crew.tick(12.0)
    onward.wait_recv()
    add_group(groups.at[last], group_weight(last), result, False)

    for i in range(sequences):
        result[chunk(i)] = inputs[order[i]] + as_row(output_bias) + (grad_inputs[chunk(i)] + result[chunk(i)])
        normed_two[chunk(i)] = unit_rows(result[chunk(i)])[0] * as_row(second_gain) + as_row(second_shift)
    load_b.wait()
    load_c.wait()

    def cot_columns(columns):
        return jnp.concatenate([cotangent[order[i], :, columns] for i in range(sequences)], 0)

    normed_parts = split(normed_two[...])
    cot_parts = split(jnp.concatenate([cotangent[order[i]] for i in range(sequences)], 0))

    def hidden_tile(columns):
        hidden = dot_three(normed_parts, split(weight_b[:, columns]), PLAIN)
        hidden = hidden + hidden_bias[columns].reshape(1, TILE)
        rectified = jnp.maximum(hidden, 0.0)
        grad_active = dot_three(cot_parts, split(weight_c[columns]), BOTH_LAST)
        grad = grad_active * (2.0 * rectified)
        active[:, columns] = rectified * rectified
        grad_hidden[:, columns] = grad
        grad_rest[4 * channels + 2 : 4 * channels + 3, columns] = down_rows(grad)

    tiles(hidden_units, hidden_tile, crew, 2.0)

    def grad_normed_chunk(which):
        at = pl.ds(pl.multiple_of(which * rows, rows), rows)
        parts = split(grad_hidden[at])

        def tile(columns):
            grad_normed[at, columns] = dot_three(parts, split(weight_b[columns]), BOTH_LAST)

        tiles(model, tile)

    second_sum = HeadSum(comm, place, grad_normed, from_sibling.at[0], from_facing.at[0], rows)
    grad_normed_chunk(1 - core)
    second_sum.lend()
    grad_normed_chunk(core)
    second_sum.chip()

    active_parts = split(active[...])

    def outer_tile(columns):
        grad_outer[:, columns] = dot_three(active_parts, split(cot_columns(columns)), BOTH_FIRST)

    tiles(model, outer_tile, crew, 0.9)
    def add_sums(wanted, source, target):
        for pair_first, which, start, count, delay in plan:
            if which == wanted:
                make = sum_pair_first if pair_first else sum_line_first
                crew.add(make(comm, place, land, source, target, start, count), delay, HOP)

    add_sums(0, grad_outer, outer_out)

    normed_parts = split(normed_two[...])

    def inner_tile(columns):
        grad_inner[:, columns] = dot_three(normed_parts, split(grad_hidden[:, columns]), BOTH_FIRST)

    tiles(hidden_units, inner_tile, crew, 0.9)
    add_sums(1, grad_inner, inner_out)

    outer_term = weight_a.at[pl.ds(0, tokens)]

    def outer_term_tile(columns):
        outer_term[:, columns] = dot_three(active_parts, split(weight_c[:, columns]), PLAIN)

    tiles(model, outer_term_tile, crew, 0.9)
    load_joined = comm.local(joined, weight_c.at[pl.ds(0, 3 * channels)], keep=False)

    late_out[...] = jnp.zeros_like(late_out)
    swaps = []

    def own_piece(p, size):
        return pl.ds(pl.multiple_of(core * rows + p * size, 8), size)

    for p in range(second_sum.pieces):
        at = own_piece(p, second_sum.size)
        incoming = second_sum.piece(p)
        unit, inverse = unit_rows(result[at])
        through = norm_back(incoming, as_row(second_gain), unit, inverse)
        here = pl.ds(p * second_sum.size, second_sum.size)
        cot = jnp.where(core == 0, cotangent[order[0], here], cotangent[order[1], here])
        grad_inputs[at] = cot + through
        late_out[2:3] = late_out[2:3] + down_rows(incoming * unit)
        late_out[3:4] = late_out[3:4] + down_rows(incoming)
        swaps.append(comm.copy(grad_inputs.at[at], grad_inputs.at[at], place.sibling))
        crew.tick(3.5)
    result_sum = HeadSum(comm, place, outer_term, from_sibling.at[1], from_facing.at[1], rows)
    result_sum.lend()
    for made in swaps:
        made.wait_recv()

    weight_parts = split(output_weight[...])
    grad_att[:, channels:] = jnp.zeros((sequences, grad_att.shape[1] - channels, rows), jnp.float32)
    keep_grad = []
    for i in range(sequences):
        live = jnp.minimum(lengths[order[i]] - seq * rows, rows)
        alive = (lax.broadcasted_iota(jnp.int32, (1, rows), 1) < live).astype(jnp.float32)
        grad = dot_three(weight_parts, split(grad_inputs[chunk(i)]), BOTH_LAST) * alive
        grad_att[i, 0:channels] = grad
        both = grad * attended_turned[i]
        for head in range(heads):
            at = channels + head
            grad_att[i, at : at + 1] = log_total[i, head : head + 1]
            grad_att[i, at + heads : at + heads + 1] = down_rows(both[head_lanes(head)])
        grad_spreads[i].begin()
        keep_grad.append(comm.local(grad_att.at[i], all_grads.at[seq, i], keep=False))
    result_sum.chip()
    for i in range(sequences):
        for head in range(heads):
            query_cat[i, head] = against(queries[i, head_lanes(head)] * HSIZE ** (-0.5))
            grad_cat[i, head] = against(grad_att[i, head_lanes(head)])
    for spread in grad_spreads:
        spread.pass_pair()
    output_grad = jnp.zeros((channels, model), jnp.float32)
    for i in range(sequences):
        output_grad = output_grad + dot_three(split(attended_turned[i]), split(grad_inputs[chunk(i)]), PLAIN)
    grad_rest[0:channels] = output_grad
    base = 4 * channels
    grad_rest[base : base + 1] = down_rows(grad_inputs[...])
    outer_row = jnp.zeros((1, model), jnp.float32)
    for i in range(sequences):
        outer_row = outer_row + down_rows(cotangent[order[i]])
    grad_rest[base + 1 : base + 2] = outer_row
    add_sums(2, grad_rest, rest_out)
    crew.tick(TICKS)

    grad_query[...] = jnp.zeros_like(grad_query)
    grad_keyval[...] = jnp.zeros_like(grad_keyval)

    def query_side(i, start, end):
        count = jnp.where(z < ends[i], jnp.minimum(seq + 1, end), 0)

        def load(slot, block):
            return pltpu.make_async_copy(keyvals.at[block, i], key_slots.at[slot], slot_sems.at[slot])

        pl.when(count > start)(lambda: load(start % 2, seq - start).start())

        def step(t, carry):
            slot = lax.rem(t, 2)
            load(slot, seq - t).wait()
            pl.when(t + 1 < count)(lambda: load(1 - slot, seq - t - 1).start())
            block = key_slots.at[slot]
            for head in range(heads):
                key_high, key_low = split(block[:, head_lanes(head)])
                scores = dot(jnp.concatenate([key_high, key_high, key_low], 1), query_cat[i, head], PLAIN)
                at = channels + head
                scores = scores - grad_att[i, at : at + 1]
                powers = jnp.exp(jnp.where(allowed_from(scores.shape, t * rows), scores, NEGATIVE))
                slopes = dot(beside(block[:, head_lanes(head, channels)]), grad_cat[i, head], PLAIN)
                slopes = powers * (slopes - grad_att[i, at + heads : at + heads + 1])
                high, low = split(slopes)
                both = dot(jnp.concatenate([key_high, key_low], 1), high, BOTH_FIRST)
                term = both[:HSIZE] + both[HSIZE:] + dot(key_high, low, BOTH_FIRST)
                grad_query[i, head_lanes(head)] = grad_query[i, head_lanes(head)] + term
            return carry

        lax.fori_loop(start, jnp.maximum(count, start), step, 0)

    def key_side(i, offset, query_ref, grad_ref):
        for head in range(heads):
            lanes = head_lanes(head)
            query_high, query_low = split(query_ref[lanes] * HSIZE ** (-0.5))
            grad_high, grad_low = split(grad_ref[lanes])
            scores = dot(
                key_cat[i, head, :, 0 : 3 * HSIZE],
                jnp.concatenate([query_high, query_low, query_high], 0),
                PLAIN,
            )
            at = channels + head
            scores = scores - grad_ref[at : at + 1]
            powers = jnp.exp(jnp.where(allowed_from(scores.shape, offset), scores, NEGATIVE))
            slopes = dot(
                value_cat[i, head, :, 0 : 3 * HSIZE],
                jnp.concatenate([grad_high, grad_low, grad_high], 0),
                PLAIN,
            )
            slopes = powers * (slopes - grad_ref[at + heads : at + heads + 1])
            for base, (far_high, far_low), value in (
                (0, (query_high, query_low), slopes),
                (channels, (grad_high, grad_low), powers),
            ):
                high, low = split(value)
                both = dot(jnp.concatenate([far_high, far_low], 0), high, BOTH_LAST)
                term = both[:HSIZE] + both[HSIZE:] + dot(far_high, low, BOTH_LAST)
                where = slice(base + head * HSIZE, base + (head + 1) * HSIZE)
                grad_keyval[i, where] = grad_keyval[i, where] + term

    def key_level(level, pairs):
        items = [(i, slot) for i in range(sequences) for slot in range(2)]

        def inside(i):
            return z + level < jnp.where(i == 0, ends[0], ends[1])

        def wanted(t):
            i, slot = t // 2, t % 2
            if level:
                return inside(i)
            if pairs:
                return inside(i) & (slot == 1) & (y == 0)
            return inside(i) & (slot == y)

        def loads(t):
            i, slot = t // 2, t % 2
            block = 2 * (z + level) + slot
            return (
                pltpu.make_async_copy(all_queries.at[block, i], query_slots.at[t], slot_sems.at[2 * t]),
                pltpu.make_async_copy(all_grads.at[block, i], grad_slots.at[t], slot_sems.at[2 * t + 1]),
            )

        for t in range(len(items)):
            @pl.when(wanted(t))
            def _(t=t):
                for made in loads(t):
                    made.start()

        def step(t, carry):
            @pl.when(wanted(t))
            def _():
                for made in loads(t):
                    made.wait()
                i, slot = t // 2, t % 2
                offset = (2 * (z + level) + slot - seq) * rows
                key_side(i, offset, query_slots.at[t], grad_slots.at[t])

            return carry

        lax.fori_loop(0, len(items), step, 0)

    def pass_level(level):
        for spread in grad_spreads:
            spread.pass_level(level)

    def have_level(level):
        for spread in query_spreads + grad_spreads:
            spread.have_level(level)

    pass_level(1)
    for i in range(sequences):
        load_own[i].wait()
        for head in range(heads):
            key_cat[i, head, :, 0 : 3 * HSIZE] = beside(own_keys[i, :, head_lanes(head)])
            value_cat[i, head, :, 0 : 3 * HSIZE] = beside(own_keys[i, :, head_lanes(head, channels)])
        keep_query[i].wait()
        keep_grad[i].wait()
    key_level(0, False)
    crew.tick(TICKS)
    for spread in query_spreads + grad_spreads:
        spread.have_pair()
    key_level(0, True)
    query_side(0, 0, 4)
    pass_level(2)
    crew.tick(TICKS)
    query_side(0, 4, 8)
    query_side(1, 0, 8)
    have_level(1)
    key_level(1, False)
    crew.tick(TICKS)
    pass_level(3)
    have_level(2)
    key_level(2, False)
    crew.tick(TICKS)
    have_level(3)
    key_level(3, False)
    crew.tick(TICKS)
    for p in range(result_sum.pieces):
        at = own_piece(p, result_sum.size)
        result[at] = result[at] + as_row(outer_bias) + result_sum.piece(p)
        swaps.append(comm.copy(result.at[at], result.at[at], place.sibling))

    edge = grad_conv.shape[2] - rows
    for i in range(sequences):
        grad_conv[0, i, pl.ds(0, rows)] = (grad_query[i] * HSIZE ** (-0.5)).T
        grad_conv[1, i, pl.ds(0, rows)] = grad_keyval[i, 0:channels].T
        grad_conv[2, i, pl.ds(0, rows)] = grad_keyval[i, channels : 2 * channels].T

    @pl.when(seq == devices - 1)
    def _():
        grad_conv[:, :, pl.ds(rows, edge)] = jnp.zeros((3, sequences, edge, channels), jnp.float32)

    before = (seq - 1, place.head)
    rim = comm.copy(
        grad_conv.at[:, :, pl.ds(0, edge)], grad_conv.at[:, :, pl.ds(rows, edge)], before, seq > 0
    )
    load_raw.wait()
    base = 4 * channels + 3
    grad_rest[base : base + 13] = jnp.zeros((13, model), jnp.float32)
    for k in range(3):
        for j in range(3):
            total = jnp.zeros((1, channels), jnp.float32)
            for i in range(sequences):
                total = total + down_rows(grad_conv[k, i, pl.ds(0, rows)] * raw[k, i, pl.ds(edge - j, rows)])
            grad_rest[base + j : base + j + 1, k * channels : (k + 1) * channels] = total
    crew.tick(2.0)
    wait_for(rim, seq < devices - 1)
    for k, kernel in enumerate((query_kernel, key_kernel, value_kernel)):
        for i in range(sequences):
            grad_hidden[chunk(i), k * channels : (k + 1) * channels] = (
                kernel[0:1] * grad_conv[k, i, pl.ds(0, rows)]
                + kernel[1:2] * grad_conv[k, i, pl.ds(1, rows)]
                + kernel[2:3] * grad_conv[k, i, pl.ds(2, rows)]
            )
    load_joined.wait()

    def first_chunk(which):
        at = pl.ds(pl.multiple_of(which * rows, rows), rows)
        parts = split(grad_hidden[at, 0 : 3 * channels])

        def tile(columns):
            active[at, columns] = dot_three(parts, split(weight_c[0 : 3 * channels, columns]), PLAIN)

        tiles(model, tile)

    first_sum = HeadSum(comm, place, active, from_sibling.at[2], from_facing.at[2], rows)
    first_chunk(1 - core)
    first_sum.lend()
    first_chunk(core)
    first_sum.chip()
    crew.tick(3.0)
    for i in range(sequences):
        normed_two[chunk(i)] = unit_rows(inputs[order[i]])[0] * as_row(first_gain) + as_row(first_shift)
    projected_parts = split(grad_hidden[:, 0 : 3 * channels])

    def joined_tile(columns):
        grad_rest[channels : 4 * channels, columns] = dot_three(
            projected_parts, split(normed_two[:, columns]), BOTH_FIRST
        )

    tiles(model, joined_tile, crew, 0.9)
    add_sums(3, grad_rest, rest_out)
    crew.tick(0.0)

    pieces = swaps[: second_sum.pieces]
    for made in pieces:
        comm.settle(made)
    returned = []
    for p in range(first_sum.pieces):
        at = own_piece(p, first_sum.size)
        incoming = first_sum.piece(p)
        here = pl.ds(p * first_sum.size, first_sum.size)
        rows_in = jnp.where(core == 0, inputs[order[0], here], inputs[order[1], here])
        unit, inverse = unit_rows(rows_in)
        grad_inputs[at] = grad_inputs[at] + norm_back(incoming, as_row(first_gain), unit, inverse)
        late_out[0:1] = late_out[0:1] + down_rows(incoming * unit)
        late_out[1:2] = late_out[1:2] + down_rows(incoming)
        returned.append(comm.copy(grad_inputs.at[at], grad_inputs.at[at], place.sibling))
        crew.tick(3.5)
    late_sent = comm.copy(late_out, late_from, place.sibling)
    crew.tick(0.0)
    late_sent.wait_recv()
    late_all[seq] = late_out[...] + late_from[...]
    mine = late_all.at[seq]
    shared = [comm.copy(mine, mine, device) for device, _ in column]
    crew.drain()
    for made in swaps[second_sum.pieces :] + returned + shared:
        made.wait_recv()
    comm.settle(late_sent)
    total = late_all[0]
    for k in range(1, devices):
        total = total + late_all[k]
    late_out[...] = total
    comm.finish()
    assert comm.used <= COPIES and comm.used_local <= local_sems.shape[0]


COPIES = 320
SPACE = 7.5
HOP = 6.0
TICKS = 4.0


def sum_plan(hidden_units, model, channels):
    size = channels // 2
    plan = [(True, 0, k * size, size, k * SPACE) for k in range(hidden_units // size)]
    plan += [(False, 1, k * size, size, k * SPACE) for k in range(model // size)]
    plan += [(True, 2, 0, size, 0.0), (False, 2, size, size, SPACE / 2)]
    size = channels // 4
    plan += [(True, 3, channels + k * size, size, k * SPACE / 2) for k in range(6)]
    plan += [
        (False, 3, channels + (6 + k) * size, size + 16 * (k == 5), (k + 0.5) * SPACE / 2) for k in range(6)
    ]
    return plan


def back(ends, collective, lengths, inputs, cotangent, kept, vectors, kernels, inner_weight, outer_weight, output_weight):
    keyvals, queries, raw, attended, attended_turned, log_total, weights, joined = kept
    sequences, rows, model = inputs.shape
    channels = output_weight.shape[0]
    heads = channels // HSIZE
    hidden_units = inner_weight.shape[1]
    tokens = sequences * rows
    devices = lax.axis_size("seq")
    rest_rows = 4 * channels + 16
    plan = sum_plan(hidden_units, model, channels)
    land_rows = sum(3 * count // 2 if pair_first else 2 * count for pair_first, _, _, count, _ in plan)
    vmem = pl.BlockSpec(memory_space=pltpu.VMEM)
    far = pl.BlockSpec(memory_space=pl.ANY)

    def f32(*shape):
        return jax.ShapeDtypeStruct(shape, jnp.float32)

    def room(*shape, dtype=jnp.float32):
        return pltpu.VMEM(shape, dtype)

    edge = 8
    grad_rows = channels + 16
    half = functools.partial(room, dtype=jnp.bfloat16)
    return pl.pallas_call(
        functools.partial(back_kernel, ends, plan),
        out_shape=[
            f32(tokens, model),
            f32(tokens, model),
            f32(hidden_units, model),
            f32(model, hidden_units),
            f32(rest_rows, model),
            f32(8, model),
            f32(devices, sequences, channels, rows),
            f32(devices, sequences, grad_rows, rows),
        ],
        in_specs=[pl.BlockSpec(memory_space=pltpu.SMEM)] + [vmem] * 17 + [far] * 6,
        out_specs=[vmem] * 2 + [far] * 3 + [vmem] + [far] * 2,
        scratch_shapes=[
            room(model, model),
            room(model, hidden_units),
            room(hidden_units, model),
            room(3, sequences, rows + edge, channels),
            room(4, rows, sequences * channels),
            room(tokens, model),
            room(tokens, hidden_units),
            room(tokens, hidden_units),
            room(tokens, model),
            room(3, rows, model),
            room(3, rows, model),
            room(hidden_units, model),
            room(model, hidden_units),
            room(rest_rows, model),
            room(land_rows, model),
            room(2, rows, 2 * channels),
            room(sequences, rows, 2 * channels),
            room(2 * sequences, channels, rows),
            room(2 * sequences, grad_rows, rows),
            half(sequences, heads, 3 * HSIZE, rows),
            half(sequences, heads, 3 * HSIZE, rows),
            half(sequences, heads, rows, 256),
            half(sequences, heads, rows, 256),
            room(sequences, grad_rows, rows),
            room(sequences, channels, rows),
            room(sequences, 2 * channels, rows),
            room(3, sequences, rows + edge, channels),
            room(8, model),
            room(devices, 8, model),
            pltpu.SemaphoreType.DMA((COPIES,)),
            pltpu.SemaphoreType.DMA((COPIES,)),
            pltpu.SemaphoreType.DMA((64,)),
            pltpu.SemaphoreType.DMA((4 * sequences,)),
        ],
        compiler_params=pltpu.CompilerParams(
            collective_id=collective, has_side_effects=True, vmem_limit_bytes=63 * 2**20
        ),
        name="back",
    )(
        lengths,
        inputs,
        cotangent,
        attended,
        attended_turned,
        queries,
        log_total,
        output_weight,
        *vectors,
        *kernels,
        keyvals,
        weights,
        inner_weight,
        outer_weight,
        joined,
        raw,
    )


def shards(
    inputs,
    seq_lengths,
    first_gain,
    first_shift,
    query_weight,
    key_weight,
    value_weight,
    query_kernel,
    key_kernel,
    value_kernel,
    output_weight,
    output_bias,
    second_gain,
    second_shift,
    inner_weight,
    hidden_layer_bias,
    outer_weight,
    outer_bias,
    cotangent,
):
    channels = query_weight.shape[1]
    kernels = (query_kernel, key_kernel, value_kernel)

    def run(short_end, collective):
        ends = (LINE, short_end)
        kept = front(
            ends,
            collective,
            seq_lengths,
            inputs,
            first_gain,
            first_shift,
            (query_weight, key_weight, value_weight),
            kernels,
            output_weight,
        )
        result, grad_inputs, grad_outer, grad_inner, rest, late = back(
            ends,
            collective + 1,
            seq_lengths,
            inputs,
            cotangent,
            kept,
            (
                output_bias,
                first_gain,
                first_shift,
                second_gain,
                second_shift,
                hidden_layer_bias,
                outer_bias,
            ),
            kernels,
            inner_weight,
            outer_weight,
            output_weight,
        )[:6]
        swap = seq_lengths[1] > seq_lengths[0]

        def placed(array):
            array = array.reshape(inputs.shape)
            return jnp.where(swap, jnp.flip(array, 0), array)

        vectors = rest[4 * channels :]
        mixes = vectors[3:6, : 3 * channels]
        return (
            placed(result),
            placed(grad_inputs),
            late[0],
            late[1],
            rest[channels : 2 * channels].T,
            rest[2 * channels : 3 * channels].T,
            rest[3 * channels : 4 * channels].T,
            mixes[:, :channels],
            mixes[:, channels : 2 * channels],
            mixes[:, 2 * channels :],
            rest[:channels],
            vectors[0],
            late[2],
            late[3],
            grad_inner,
            vectors[2],
            grad_outer,
            vectors[1],
        )

    pair_rows = 2 * inputs.shape[1]
    shorter = jnp.minimum(seq_lengths[0], seq_lengths[1])
    reach = (shorter > pair_rows).astype(jnp.int32) + (shorter > 2 * pair_rows)
    cases = [functools.partial(run, end, 1 + 2 * k) for k, end in enumerate((1, 2, LINE))]
    return lax.switch(reach, cases)


def solution(mesh):
    lines = mesh.shape["seq"] == 2 * LINE and mesh.shape["head"] == 4
    return jax.shard_map(
        shards if lines else general_shards,
        mesh=mesh,
        in_specs=(
            P(None, "seq", None),
            P(),
            P(),
            P(),
            P(None, "head"),
            P(None, "head"),
            P(None, "head"),
            P(None, "head"),
            P(None, "head"),
            P(None, "head"),
            P("head", None),
            P(),
            P(),
            P(),
            P(None, "head"),
            P("head"),
            P("head", None),
            P(),
            P(None, "seq", None),
        ),
        out_specs=(
            P(None, "seq", None),
            P(None, "seq", None),
            P(),
            P(),
            P(None, "head"),
            P(None, "head"),
            P(None, "head"),
            P(None, "head"),
            P(None, "head"),
            P(None, "head"),
            P("head", None),
            P(),
            P(),
            P(),
            P(None, "head"),
            P("head"),
            P("head", None),
            P(),
        ),
        check_vma=False,
    )
```

```python
import functools

import jax
import jax.numpy as jnp
from jax import lax
from jax.experimental import pallas as pl
from jax.experimental.pallas import tpu as pltpu
from jax.sharding import PartitionSpec as P

MESH = pl.DeviceIdType.MESH

HSIZE = 64


EXACT_FLOAT_MODE = lax.Precision.HIGH
EPSILON = 1e-05
NEGATIVE = -1e30


def shifted(block, axis, distance):
    devices = range(lax.axis_size(axis))
    route = [(i - distance, i) for i in devices if i - distance in devices]
    return lax.ppermute(block, axis, route)


def matmul(input_operand, weight_matrix):
    return jnp.einsum("scd,df->scf", input_operand, weight_matrix, precision=EXACT_FLOAT_MODE)


def transposed(input_operand, weight_matrix):
    return jnp.einsum("scf,df->scd", input_operand, weight_matrix, precision=EXACT_FLOAT_MODE)


def outer_sum(first_rows, second_rows):
    return jnp.einsum("scd,scf->df", first_rows, second_rows, precision=EXACT_FLOAT_MODE)


def normalize(stream, norm_gain, norm_shift):
    centered = stream - jnp.mean(stream, -1, keepdims=True)
    inverse = lax.rsqrt(jnp.mean(centered * centered, -1, keepdims=True) + EPSILON)
    unit_rows = centered * inverse
    return (unit_rows * norm_gain + norm_shift, unit_rows, inverse)


def normalize_back(gradient, norm_gain, unit_rows, inverse):
    scaled = gradient * norm_gain
    middle = (
        scaled
        - jnp.mean(scaled, -1, keepdims=True)
        - unit_rows * jnp.mean(scaled * unit_rows, -1, keepdims=True)
    )
    return (inverse * middle, jnp.sum(gradient * unit_rows, (0, 1)), jnp.sum(gradient, (0, 1)))


def split_heads(flat):
    return flat.reshape(flat.shape[0], flat.shape[1], flat.shape[2] // HSIZE, HSIZE)


def allowed_pairs(query_pos, key_pos, lengths):
    return (key_pos[None, None, :] <= query_pos[None, :, None]) & (
        key_pos[None, None, :] < lengths[:, None, None]
    )


def pair_terms(queries, gradients, log_total, row_dots, query_pos, keyvals, key_pos, lengths):
    channels = queries.shape[2]
    query_heads = split_heads(queries)
    key_heads = split_heads(keyvals[:, :, :channels])
    value_heads = split_heads(keyvals[:, :, channels:])
    grad_heads = split_heads(gradients)
    scores = jnp.einsum(
        "sqhe,skhe->shqk", query_heads, key_heads, precision=EXACT_FLOAT_MODE
    ) * HSIZE ** (-0.5)
    allowed = allowed_pairs(query_pos, key_pos, lengths)[:, None]
    weight_values = jnp.exp(jnp.where(allowed, scores - log_total[..., None], NEGATIVE))
    weight_grads = jnp.einsum(
        "sqhe,skhe->shqk", grad_heads, value_heads, precision=EXACT_FLOAT_MODE
    )
    score_grads = weight_values * (weight_grads - row_dots[..., None])
    return (weight_values, score_grads, query_heads, key_heads, grad_heads)


def key_facing_term(terms, keyvals, channels):
    value_part = jnp.einsum("shqk,sqhe->skhe", terms[0], terms[4], precision=EXACT_FLOAT_MODE)
    key_part = jnp.einsum(
        "shqk,sqhe->skhe", terms[1], terms[2], precision=EXACT_FLOAT_MODE
    ) * HSIZE ** (-0.5)
    shape = (keyvals.shape[0], keyvals.shape[1], channels)
    return jnp.concatenate([key_part.reshape(shape), value_part.reshape(shape)], 2)


def query_side_term(terms):
    return jnp.einsum(
        "shqk,skhe->sqhe", terms[1], terms[3], precision=EXACT_FLOAT_MODE
    ) * HSIZE ** (-0.5)


def key_terms(queries, gradients, log_total, row_dots, query_pos, keyvals, key_pos, lengths):
    terms = pair_terms(
        queries, gradients, log_total, row_dots, query_pos, keyvals, key_pos, lengths
    )
    return key_facing_term(terms, keyvals, queries.shape[2])


def general_shards(
    inputs,
    seq_lengths,
    first_gain,
    first_shift,
    query_weight,
    key_weight,
    value_weight,
    query_kernel,
    key_kernel,
    value_kernel,
    output_weight,
    output_bias,
    second_gain,
    second_shift,
    inner_weight,
    hidden_layer_bias,
    outer_weight,
    outer_bias,
    cotangent,
):
    sequences, rows, model = inputs.shape
    channels = query_weight.shape[1]
    heads = channels // HSIZE
    positions = lax.axis_index("seq") * rows + jnp.arange(rows, dtype=jnp.int32)
    live_rows = (positions[None, :] < seq_lengths[:, None]).astype(jnp.float32)
    joined_weight = jnp.concatenate([query_weight, key_weight, value_weight], 1)
    joined_kernel = jnp.concatenate([query_kernel, key_kernel, value_kernel], 1)
    normed, leading_unit_value, first_inverse = normalize(inputs, first_gain, first_shift)
    projected = matmul(normed, joined_weight)
    rims = shifted(projected[:, rows - 2 :, :], "seq", 1)
    extended = jnp.concatenate([rims, projected], 1)
    convolved = (
        joined_kernel[0] * extended[:, 2:]
        + joined_kernel[1] * extended[:, 1:-1]
        + joined_kernel[2] * extended[:, :-2]
    )
    queries = convolved[:, :, :channels]
    keyvals = convolved[:, :, channels:]
    query_heads = split_heads(queries)
    portion = lax.all_gather(keyvals, "seq", axis=1, tiled=True)
    highest = jnp.full((sequences, heads, rows), NEGATIVE, jnp.float32)
    key_pos = jnp.arange(portion.shape[1], dtype=jnp.int32)
    key_heads = split_heads(portion[:, :, :channels])
    value_heads = split_heads(portion[:, :, channels:])
    scores = jnp.einsum(
        "sqhe,skhe->shqk", query_heads, key_heads, precision=EXACT_FLOAT_MODE
    ) * HSIZE ** (-0.5)
    allowed = allowed_pairs(positions, key_pos, seq_lengths)[:, None]
    masked = jnp.where(allowed, scores, NEGATIVE)
    new_high = jnp.maximum(highest, jnp.max(masked, -1))
    weight_values = jnp.where(allowed, jnp.exp(masked - new_high[..., None]), 0.0)
    summed = jnp.sum(weight_values, -1)
    weighted = jnp.einsum("shqk,skhe->shqe", weight_values, value_heads, precision=EXACT_FLOAT_MODE)
    highest, summed, weighted = (new_high, summed, weighted)
    log_total = highest + jnp.log(summed)
    attended = (weighted / summed[..., None]).transpose(0, 2, 1, 3).reshape(
        sequences, rows, channels
    ) * live_rows[..., None]
    branch = lax.psum(matmul(attended, output_weight), "head")
    mixed = inputs + branch + output_bias
    normed_two, second_unit, second_inverse = normalize(mixed, second_gain, second_shift)
    hidden = matmul(normed_two, inner_weight) + hidden_layer_bias
    rectified = jnp.maximum(hidden, 0.0)
    active = rectified * rectified
    result = mixed + lax.psum(matmul(active, outer_weight), "head") + outer_bias
    grad_outer_weight = outer_sum(active, cotangent)
    grad_outer_bias = jnp.sum(cotangent, (0, 1))
    grad_hidden = transposed(cotangent, outer_weight) * (2.0 * rectified)
    grad_inner_weight = outer_sum(normed_two, grad_hidden)
    grad_inner_bias = jnp.sum(grad_hidden, (0, 1))
    grad_normed_two = lax.psum(transposed(grad_hidden, inner_weight), "head")
    through_two, grad_second_gain, grad_second_shift = normalize_back(
        grad_normed_two, second_gain, second_unit, second_inverse
    )
    grad_mixed = cotangent + through_two
    grad_output_weight = outer_sum(attended, grad_mixed)
    grad_output_bias = jnp.sum(grad_mixed, (0, 1))
    grad_attended = transposed(grad_mixed, output_weight) * live_rows[..., None]
    row_dots = jnp.sum(split_heads(grad_attended) * split_heads(attended), -1).transpose(0, 2, 1)
    terms = pair_terms(
        queries, grad_attended, log_total, row_dots, positions, portion, key_pos, seq_lengths
    )
    grad_queries = query_side_term(terms).reshape(jnp.zeros_like(queries).shape)
    query_side = jnp.concatenate([queries, grad_attended], 2)
    row_stats = jnp.concatenate([log_total, row_dots], 1).transpose(0, 2, 1)
    side_rows = lax.all_gather(query_side, "seq", axis=1, tiled=True)
    stat_rows = lax.all_gather(row_stats, "seq", axis=1, tiled=True)
    query_pos = jnp.arange(side_rows.shape[1], dtype=jnp.int32)
    portion_total = stat_rows[:, :, :heads].transpose(0, 2, 1)
    portion_dots = stat_rows[:, :, heads:].transpose(0, 2, 1)
    grad_keyvals = key_terms(
        side_rows[:, :, :channels],
        side_rows[:, :, channels:],
        portion_total,
        portion_dots,
        query_pos,
        keyvals,
        positions,
        seq_lengths,
    )
    grad_convolved = jnp.concatenate([grad_queries, grad_keyvals], 2)
    following = shifted(grad_convolved[:, :2, :], "seq", -1)
    grad_extended = jnp.concatenate([grad_convolved, following], 1)
    grad_projected = (
        joined_kernel[0] * grad_extended[:, :rows]
        + joined_kernel[1] * grad_extended[:, 1 : rows + 1]
        + joined_kernel[2] * grad_extended[:, 2:]
    )
    grad_kernel = jnp.stack(
        [
            jnp.sum(grad_convolved * extended[:, 2:], (0, 1)),
            jnp.sum(grad_convolved * extended[:, 1:-1], (0, 1)),
            jnp.sum(grad_convolved * extended[:, :-2], (0, 1)),
        ]
    )
    grad_joined = outer_sum(normed, grad_projected)
    grad_normed = lax.psum(transposed(grad_projected, joined_weight), "head")
    through_one, grad_first_gain, grad_first_shift = normalize_back(
        grad_normed, first_gain, leading_unit_value, first_inverse
    )
    grad_inputs = grad_mixed + through_one
    grad_query_weight = grad_joined[:, :channels]
    grad_key_weight = grad_joined[:, channels : 2 * channels]
    grad_value_weight = grad_joined[:, 2 * channels :]
    grad_query_kernel = grad_kernel[:, :channels]
    grad_key_kernel = grad_kernel[:, channels : 2 * channels]
    grad_value_kernel = grad_kernel[:, 2 * channels :]
    (
        grad_first_gain,
        grad_first_shift,
        grad_query_weight,
        grad_key_weight,
        grad_value_weight,
        grad_query_kernel,
        grad_key_kernel,
        grad_value_kernel,
        grad_output_weight,
        grad_output_bias,
        grad_second_gain,
        grad_second_shift,
        grad_inner_weight,
        grad_inner_bias,
        grad_outer_weight,
        grad_outer_bias,
    ) = lax.psum(
        (
            grad_first_gain,
            grad_first_shift,
            grad_query_weight,
            grad_key_weight,
            grad_value_weight,
            grad_query_kernel,
            grad_key_kernel,
            grad_value_kernel,
            grad_output_weight,
            grad_output_bias,
            grad_second_gain,
            grad_second_shift,
            grad_inner_weight,
            grad_inner_bias,
            grad_outer_weight,
            grad_outer_bias,
        ),
        "seq",
    )
    return (
        result,
        grad_inputs,
        grad_first_gain,
        grad_first_shift,
        grad_query_weight,
        grad_key_weight,
        grad_value_weight,
        grad_query_kernel,
        grad_key_kernel,
        grad_value_kernel,
        grad_output_weight,
        grad_output_bias,
        grad_second_gain,
        grad_second_shift,
        grad_inner_weight,
        grad_inner_bias,
        grad_outer_weight,
        grad_outer_bias,
    )


class Comm:
    def __init__(self, send_sems, recv_sems, local_sems=None):
        self.send_sems, self.recv_sems, self.local_sems = send_sems, recv_sems, local_sems
        self.used = 0
        self.used_local = 0
        self.sent = []
        self.stored = []

    def copy(self, source, target, device, when=None):
        index = self.used
        self.used += 1
        made = pltpu.make_async_remote_copy(
            src_ref=source,
            dst_ref=target,
            send_sem=self.send_sems.at[index],
            recv_sem=self.recv_sems.at[index],
            device_id=device,
            device_id_type=MESH,
        )
        if when is None:
            made.start()
        else:
            pl.when(when)(made.start)
        self.sent.append((made, when))
        return made

    def settle(self, made):
        self.sent = [one for one in self.sent if one[0] is not made]
        made.wait_send()

    def local(self, source, target, when=None, keep=True):
        made = pltpu.make_async_copy(source, target, self.local_sems.at[self.used_local])
        self.used_local += 1
        if when is None:
            made.start()
        else:
            pl.when(when)(made.start)
        if keep:
            self.stored.append((made, when))
        return made

    def finish(self):
        for made, when in self.sent:
            if when is None:
                made.wait_send()
            else:
                pl.when(when)(made.wait_send)
        for made, when in self.stored:
            if when is None:
                made.wait()
            else:
                pl.when(when)(made.wait)


def wait_for(made, when=None):
    if when is None:
        made.wait_recv()
    else:
        pl.when(when)(made.wait_recv)


class Place:
    def __init__(self):
        self.seq = lax.axis_index("seq")
        self.head = lax.axis_index("head")
        self.z = self.seq // 2
        self.y = self.seq % 2
        self.other = 1 - self.y
        self.core = self.head % 2
        self.at_end = (self.z == 0) | (self.z == LINE - 1)
        self.at_middle = jnp.logical_not(self.at_end)
        step = 2 - 4 * (self.z // 2)
        self.pair = (2 * self.z + self.other, self.head)
        self.inward = (self.seq + step, self.head)
        self.outward = (self.seq - step, self.head)
        self.sibling = (self.seq, self.head + 1 - 2 * self.core)
        self.facing = (self.seq, (self.head + 2) % 4)


LINE = 4


def rows_at(ref, start, count):
    return ref.at[pl.ds(pl.multiple_of(start, 8), count)]


class Land:
    def __init__(self, ref):
        self.ref, self.used = ref, 0

    def take(self, rows):
        got = self.ref.at[pl.ds(self.used, rows)]
        self.used += rows
        return got


def sum_pair_first(comm, place, land, source, target, start, count):
    half = count // 2
    line, from_end, from_middle = land.take(half), land.take(half), land.take(half)
    own = rows_at(target, start + place.y * half, half)
    far = rows_at(source, start + place.other * half, half)
    near = rows_at(source, start + place.y * half, half)
    made = comm.copy(far, line, place.pair)
    yield
    made.wait_recv()
    line[...] = line[...] + near[...]
    inward = comm.copy(line, from_end, place.inward, place.at_end)
    yield

    @pl.when(place.at_middle)
    def _():
        inward.wait_recv()
        from_end[...] = from_end[...] + line[...]

    across = comm.copy(from_end, from_middle, place.inward, place.at_middle)
    yield

    @pl.when(place.at_middle)
    def _():
        across.wait_recv()
        from_middle[...] = from_middle[...] + from_end[...]

    outward = comm.copy(from_middle, own, place.outward, place.at_middle)
    early = comm.copy(from_middle, own, place.pair, place.at_middle)
    comm.local(from_middle, own, place.at_middle)
    yield
    wait_for(outward, place.at_end)
    late = comm.copy(own, own, place.pair, place.at_end)
    yield
    wait_for(early, place.at_middle)
    wait_for(late, place.at_end)
    yield


def sum_line_first(comm, place, land, source, target, start, count):
    half = count // 2
    whole, from_middle, from_pair = land.take(count), land.take(half), land.take(half)
    all_rows = rows_at(source, start, count)
    mine, theirs = place.z // 2, 1 - place.z // 2
    own, rest = rows_at(target, start + mine * half, half), rows_at(target, start + theirs * half, half)
    inward = comm.copy(all_rows, whole, place.inward, place.at_end)
    yield

    @pl.when(place.at_middle)
    def _():
        inward.wait_recv()
        whole[...] = whole[...] + all_rows[...]

    across = comm.copy(rows_at(whole, theirs * half, half), from_middle, place.inward, place.at_middle)
    yield

    @pl.when(place.at_middle)
    def _():
        across.wait_recv()
        from_middle[...] = from_middle[...] + rows_at(whole, mine * half, half)[...]

    paired = comm.copy(from_middle, from_pair, place.pair, place.at_middle)
    yield

    @pl.when(place.at_middle)
    def _():
        paired.wait_recv()
        from_pair[...] = from_pair[...] + from_middle[...]

    back = comm.copy(from_pair, own, place.inward, place.at_middle)
    outward = comm.copy(from_pair, own, place.outward, place.at_middle)
    comm.local(from_pair, own, place.at_middle)
    yield
    wait_for(back, place.at_middle)
    last = comm.copy(rest, rest, place.outward, place.at_middle)
    yield
    wait_for(outward, place.at_end)
    wait_for(last, place.at_end)
    yield


class Crew:
    def __init__(self):
        self.due = []
        self.now = 0.0
        self.added = 0

    def add(self, one, delay=0.0, hop=6.0):
        self.added += 1
        self.due.append((self.now + delay, self.added, one, hop))

    def step(self):
        entry = min(self.due, key=lambda each: each[:2])
        self.due.remove(entry)
        time, number, one, hop = entry
        try:
            next(one)
            self.due.append((time + hop, number, one, hop))
        except StopIteration:
            pass

    def tick(self, length):
        self.now += length
        while self.due and min(each[0] for each in self.due) <= self.now:
            self.step()

    def drain(self):
        while self.due:
            self.step()


def split(value):
    high = value.astype(jnp.bfloat16)
    return high, (value - high.astype(jnp.float32)).astype(jnp.bfloat16)


def dot(left, right, dims):
    return lax.dot_general(left, right, (dims, ((), ())), preferred_element_type=jnp.float32)


def dot_three(left, right, dims):
    return dot(left[0], right[0], dims) + (dot(left[0], right[1], dims) + dot(left[1], right[0], dims))


PLAIN, BOTH_LAST, BOTH_FIRST = ((1,), (0,)), ((1,), (1,)), ((0,), (0,))


def product(left, right, dims=PLAIN):
    return dot_three(split(left), split(right), dims)


def beside(value):
    high, low = split(value)
    return jnp.concatenate([high, high, low], 1)


def against(value):
    high, low = split(value)
    return jnp.concatenate([high, low, high], 0)


def as_row(ref):
    return ref[...].reshape(1, ref.shape[0])


def unit_rows(rows):
    centered = rows - jnp.mean(rows, -1, keepdims=True)
    inverse = lax.rsqrt(jnp.mean(centered * centered, -1, keepdims=True) + EPSILON)
    return centered * inverse, inverse


def longer_first(lengths):
    return jnp.where(lengths[1] > lengths[0], 1, 0).astype(jnp.int32)


def head_lanes(head, base=0):
    return slice(base + head * HSIZE, base + (head + 1) * HSIZE)


class Spread:
    def __init__(self, comm, place, part, ends, upward=True, own=None):
        self.comm, self.place, self.part, self.ends = comm, place, part, ends
        self.own = own or (lambda half: part(place.seq, half))
        z, y = place.z, place.y
        self.rank = z if upward else ends - 1 - z
        self.inside = z < ends
        self.more = self.inside & ((z < ends - 1) if upward else (z > 0))
        self.leads = (y == 0) if upward else (y == 1)
        self.next = (place.seq + (2 if upward else -2), place.head)
        self.sign = 1 if upward else -1
        self.up = {}
        self.over = {}

    def block(self, level, slot):
        place = self.place
        side = place.y if slot == 0 else place.other
        return 2 * (place.z - self.sign * level) + side

    def begin(self):
        comm, place, part = self.comm, self.place, self.part
        near, far = part(place.seq, place.y), part(place.seq, place.other)
        mine = self.own(place.y)
        self.lend = comm.copy(self.own(place.other), far, place.pair, self.inside & (self.more | self.leads))
        self.up[1, 0] = comm.copy(mine, near, self.next, self.more)
        self.give = comm.copy(mine, near, place.pair, self.inside & self.leads)

    def pass_pair(self):
        comm, place, part = self.comm, self.place, self.part
        follows = jnp.logical_not(self.leads)
        wait_for(self.lend, self.inside & (self.more | follows))
        lent = part(self.block(0, 1), place.y)
        self.up[1, 1] = comm.copy(lent, lent, self.next, self.more)

    def have_pair(self):
        wait_for(self.give, self.inside & jnp.logical_not(self.leads))

    def pass_level(self, level):
        comm, place, part = self.comm, self.place, self.part
        if level >= self.ends:
            return
        here = self.inside & (self.rank >= level)
        for slot in range(2):
            half = part(self.block(level, slot), place.y)
            wait_for(self.up[level, slot], here)
            if level < self.ends - 1:
                self.up[level + 1, slot] = comm.copy(half, half, self.next, here & self.more)
            self.over[level, slot] = comm.copy(half, half, place.pair, here)

    def have_level(self, level):
        if level >= self.ends:
            return
        here = self.inside & (self.rank >= level)
        for slot in range(2):
            wait_for(self.over[level, slot], here)


def greet(partners):
    barrier = pltpu.get_barrier_semaphore()
    count = jnp.int32(0)
    for device, when in partners:
        def tell(device=device):
            pl.semaphore_signal(barrier, inc=1, device_id=device, device_id_type=MESH)

        if when is None:
            tell()
            count = count + 1
        else:
            pl.when(when)(tell)
            count = count + when.astype(jnp.int32)
    pl.semaphore_wait(barrier, count)


def line_partners(place):
    return [
        (place.pair, None),
        ((place.seq + 2, place.head), place.z < LINE - 1),
        ((place.seq - 2, place.head), place.z > 0),
    ]


def head_partners(place):
    return [(place.sibling, None), (place.facing, None)]


def step_partners(place):
    return [
        ((place.seq + 1, place.head), (place.y == 1) & (place.z < LINE - 1)),
        ((place.seq - 1, place.head), (place.y == 0) & (place.z > 0)),
    ]


class HeadSum:
    def __init__(self, comm, place, partial, from_sibling, from_facing, start, rows, pieces):
        self.comm, self.place = comm, place
        self.from_sibling, self.from_facing = from_sibling, from_facing
        self.rows, self.pieces, self.start = rows, pieces, start
        self.size = rows // pieces
        self.near = rows_at(partial, start + place.core * rows, rows)
        self.far = rows_at(partial, start + (1 - place.core) * rows, rows)

    def lend(self):
        self.lent = self.comm.copy(self.far, self.from_sibling, self.place.sibling)

    def rows_of(self, p):
        return pl.ds(pl.multiple_of(self.start + self.place.core * self.rows + p * self.size, 8), self.size)

    def chip(self):
        self.lent.wait_recv()
        self.near[...] = self.near[...] + self.from_sibling[...]
        self.sent = []
        for p in range(self.pieces):
            at = pl.ds(p * self.size, self.size)
            self.sent.append(self.comm.copy(self.near.at[at], self.from_facing.at[at], self.place.facing))

    def piece(self, p):
        self.sent[p].wait_recv()
        at = pl.ds(p * self.size, self.size)
        return self.near[at] + self.from_facing[at]


def norm_back(grad, gain, unit, inverse):
    scaled = grad * gain
    return inverse * (
        scaled - jnp.mean(scaled, -1, keepdims=True) - unit * jnp.mean(scaled * unit, -1, keepdims=True)
    )


def spread_steps(spreads):
    for spread in spreads:
        spread.begin()
    yield
    for spread in spreads:
        spread.pass_pair()
    yield
    for level in range(1, LINE):
        for spread in spreads:
            spread.pass_level(level)
        yield


TILE = 256


def tiles(width, body, crew=None, length=0.0):
    if crew is not None:
        for j in range(width // TILE):
            body(pl.ds(j * TILE, TILE))
            crew.tick(length)
        return

    def step(j, carry):
        body(pl.ds(pl.multiple_of(j * TILE, TILE), TILE))
        return carry

    lax.fori_loop(0, width // TILE, step, 0)


def down_rows(value):
    return jnp.sum(value, 0, keepdims=True)


def allowed_from(shape, offset):
    key_pos = lax.broadcasted_iota(jnp.int32, shape, 0)
    query_pos = lax.broadcasted_iota(jnp.int32, shape, 1)
    return key_pos <= query_pos + offset


def layer_kernel(
    ends,
    plan,
    lengths,
    inputs,
    cotangent,
    query_weight,
    key_weight,
    value_weight,
    output_weight,
    output_bias,
    first_gain,
    first_shift,
    second_gain,
    second_shift,
    hidden_bias,
    outer_bias,
    query_kernel,
    key_kernel,
    value_kernel,
    inner_weight,
    outer_weight,
    result,
    grad_inputs,
    outer_out,
    inner_out,
    rest_out,
    vectors_out,
    late_out,
    keyvals,
    all_queries,
    all_grads,
    halo,
    weight_a,
    weight_b,
    weight_c,
    raw,
    groups,
    attended_turned,
    queries,
    highest,
    summed,
    weighted,
    log_total,
    normed_two,
    active,
    grad_hidden,
    grad_normed,
    from_sibling,
    from_facing,
    grad_outer,
    grad_inner,
    vectors,
    land_ref,
    key_slots,
    own_keys,
    query_slots,
    grad_slots,
    query_cat,
    grad_cat,
    key_cat,
    value_cat,
    grad_att,
    grad_query,
    grad_keyval,
    grad_conv,
    late_from,
    late_all,
    send_sems,
    recv_sems,
    local_sems,
    slot_sems,
):
    place = Place()
    comm = Comm(send_sems, recv_sems, local_sems)
    land = Land(land_ref)
    crew = Crew()
    sequences, rows, model = inputs.shape
    channels = output_weight.shape[0]
    heads = channels // HSIZE
    hidden_units = hidden_bias.shape[0]
    tokens = sequences * rows
    z, y, seq, core = place.z, place.y, place.seq, place.core
    first = longer_first(lengths)
    order = (first, 1 - first)
    devices = 2 * LINE
    edge = halo.shape[1]
    long, short = 0, 1
    joined = (query_weight, key_weight, value_weight)
    column = [((lax.rem(seq + k, devices), place.head), None) for k in range(1, devices)]
    greet(column + head_partners(place))

    def chunk(i):
        return pl.ds(i * rows, rows)

    rim = comm.copy(
        inputs.at[:, pl.ds(rows - edge, edge)], halo, (seq + 1, place.head), seq < devices - 1
    )
    own_weight = rows_at(weight_a, place.head * channels, channels)
    own_weight[...] = output_weight[...]
    weight_to_sibling = comm.copy(own_weight, own_weight, place.sibling)
    weight_to_facing = comm.copy(own_weight, own_weight, place.facing)
    load_b = comm.local(inner_weight, weight_b, keep=False)
    load_c = comm.local(outer_weight, weight_c, keep=False)

    def first_normed(value):
        return unit_rows(value)[0] * as_row(first_gain) + as_row(first_shift)

    for i in range(sequences):
        normed_two[chunk(i)] = first_normed(inputs[order[i]])
    wait_for(rim, seq > 0)
    rim_parts = split(jnp.concatenate([first_normed(halo[order[i]]) for i in range(sequences)], 0))
    normed_parts = split(normed_two[...])
    for k, weight in enumerate(joined):
        parts = split(weight[...])
        whole = dot_three(normed_parts, parts, BOTH_LAST)
        before = jnp.where(seq > 0, dot_three(rim_parts, parts, BOTH_LAST), 0.0)
        for i in range(sequences):
            raw[k, i, pl.ds(0, edge)] = before[i * edge : (i + 1) * edge]
            raw[k, i, pl.ds(edge, rows)] = whole[i * rows : (i + 1) * rows]

    def convolved(k, i, kernel):
        return (
            kernel[0:1] * raw[k, i, pl.ds(edge, rows)]
            + kernel[1:2] * raw[k, i, pl.ds(edge - 1, rows)]
            + kernel[2:3] * raw[k, i, pl.ds(edge - 2, rows)]
        )

    def key_part(block, half, i):
        return keyvals.at[block, i, pl.ds(pl.multiple_of(half * (rows // 2), 8), rows // 2)]

    def key_own(half, i):
        return own_keys.at[i, pl.ds(pl.multiple_of(half * (rows // 2), 8), rows // 2)]

    key_spreads = []
    keep_keys = []
    for i in range(sequences):
        own_keys[i, :, 0:channels] = convolved(1, i, key_kernel)
        own_keys[i, :, channels : 2 * channels] = convolved(2, i, value_kernel)
        key_spreads.append(
            Spread(
                comm,
                place,
                functools.partial(key_part, i=i),
                ends[i],
                True,
                functools.partial(key_own, i=i),
            )
        )
        key_spreads[i].begin()
        keep_keys.append(comm.local(own_keys.at[i], keyvals.at[seq, i], keep=False))
    keep_query = []
    for i in range(sequences):
        query = convolved(0, i, query_kernel).T
        queries[i] = query
        for head in range(heads):
            query_cat[i, head] = against(query[head_lanes(head)] * HSIZE ** (-0.5))
        keep_query.append(comm.local(queries.at[i], all_queries.at[seq, i], keep=False))

    def query_part(block, half, i):
        return all_queries.at[block, i, pl.ds(pl.multiple_of(half * (channels // 2), 8), channels // 2)]

    def query_own(half, i):
        return queries.at[i, pl.ds(pl.multiple_of(half * (channels // 2), 8), channels // 2)]

    def grad_part(block, half, i):
        size = grad_att.shape[1] // 2
        return all_grads.at[block, i, pl.ds(pl.multiple_of(half * size, 8), size)]

    def grad_own(half, i):
        size = grad_att.shape[1] // 2
        return grad_att.at[i, pl.ds(pl.multiple_of(half * size, 8), size)]

    query_spreads = [
        Spread(
            comm,
            place,
            functools.partial(query_part, i=i),
            ends[i],
            False,
            functools.partial(query_own, i=i),
        )
        for i in range(sequences)
    ]
    grad_spreads = [
        Spread(
            comm,
            place,
            functools.partial(grad_part, i=i),
            ends[i],
            False,
            functools.partial(grad_own, i=i),
        )
        for i in range(sequences)
    ]

    def attend(i, own, diagonal):
        for head in range(heads):
            scores = dot(beside(own[:, head_lanes(head)]), query_cat[i, head], PLAIN)
            lane = pl.ds(head, 1)
            if diagonal:
                scores = jnp.where(allowed_from(scores.shape, 0), scores, NEGATIVE)
                high = jnp.max(scores, 0, keepdims=True)
            else:
                old = highest[i, lane]
                high = jnp.maximum(old, jnp.max(scores, 0, keepdims=True))
            powers = jnp.exp(scores - high)
            total = jnp.sum(powers, 0, keepdims=True)
            power_high, power_low = split(powers)
            value_high, value_low = split(own[:, head_lanes(head, channels)])
            both = dot(jnp.concatenate([value_high, value_low], 1), power_high, BOTH_FIRST)
            term = both[:HSIZE] + both[HSIZE:] + dot(value_high, power_low, BOTH_FIRST)
            at = pl.ds(head * HSIZE, HSIZE)
            if diagonal:
                summed[i, lane] = total
                weighted[i, at] = term
            else:
                scale = jnp.exp(old - high)
                summed[i, lane] = summed[i, lane] * scale + total
                weighted[i, at] = weighted[i, at] * scale + term
            highest[i, lane] = high

    def attend_level(i, level):
        if level and level >= ends[i]:
            return
        here = (z >= level) & (z < ends[i]) if level else (y == 1) & (z < ends[i])
        count = jnp.where(here, 2 if level else 1, 0)

        def load(slot):
            at = 2 * i + slot
            return pltpu.make_async_copy(
                keyvals.at[2 * (z - level) + slot, i], key_slots.at[at], slot_sems.at[at]
            )

        lax.fori_loop(0, count, lambda slot, carry: (load(slot).start(), carry)[1], 0)

        def step(slot, carry):
            load(slot).wait()
            attend(i, key_slots.at[2 * i + slot], False)
            return carry

        lax.fori_loop(0, count, step, 0)

    def alive_lanes(i):
        live = jnp.minimum(lengths[order[i]] - seq * rows, rows)
        return (lax.broadcasted_iota(jnp.int32, (1, rows), 1) < live).astype(jnp.float32)

    to_sibling, to_facing, onward = {}, {}, {}
    sibling, facing = place.sibling[1], place.facing[1]
    last = facing + 1 - 2 * (facing % 2)

    def finish_attention(i):
        alive = alive_lanes(i)
        for head in range(heads):
            at = pl.ds(head * HSIZE, HSIZE)
            total = summed[i, pl.ds(head, 1)]
            attended_turned[i, at] = weighted[i, at] * (alive / total)
            log_total[i, pl.ds(head, 1)] = highest[i, pl.ds(head, 1)] + jnp.log(total)
        mine = attended_turned.at[i]
        there = groups.at[place.head, i]
        to_sibling[i] = comm.copy(mine, there, place.sibling)
        to_facing[i] = comm.copy(mine, there, place.facing)

    def group_term(i, source, group):
        weight = weight_a[pl.ds(pl.multiple_of(group * channels, 8), channels)]
        return product(source, weight, BOTH_FIRST)

    def mix_near(i):
        own = group_term(i, attended_turned[i], place.head)
        to_sibling[i].wait_recv()
        grad_inputs[chunk(i)] = own + group_term(i, groups[sibling, i], sibling)

    def mix_far(i):
        to_facing[i].wait_recv()
        theirs = groups.at[facing, i]
        onward[i] = comm.copy(theirs, theirs, place.sibling)
        term = group_term(i, groups[facing, i], facing)
        onward[i].wait_recv()
        far = term + group_term(i, groups[last, i], last)
        mixed = inputs[order[i]] + as_row(output_bias) + (grad_inputs[chunk(i)] + far)
        result[chunk(i)] = mixed
        normed_two[chunk(i)] = unit_rows(mixed)[0] * as_row(second_gain) + as_row(second_shift)

    half_rows = rows // 2
    second_sums = [
        HeadSum(
            comm,
            place,
            grad_normed,
            from_sibling.at[0, pl.ds(i * half_rows, half_rows)],
            from_facing.at[0, pl.ds(i * half_rows, half_rows)],
            i * rows,
            half_rows,
            2,
        )
        for i in range(sequences)
    ]

    def feed(i, begin):
        parts = split(normed_two[chunk(i)])
        cot_parts = split(cotangent[order[i]])

        def tile(columns):
            hidden = dot_three(parts, split(weight_b[:, columns]), PLAIN)
            hidden = hidden + hidden_bias[columns].reshape(1, TILE)
            rectified = jnp.maximum(hidden, 0.0)
            grad = dot_three(cot_parts, split(weight_c[columns]), BOTH_LAST) * (2.0 * rectified)
            active[chunk(i), columns] = rectified * rectified
            grad_hidden[chunk(i), columns] = grad
            row = down_rows(grad)
            vectors[2:3, columns] = row if begin else vectors[2:3, columns] + row

        tiles(hidden_units, tile)

    def second_grad(i):
        parts = split(grad_hidden[chunk(i)])

        def tile(columns):
            grad_normed[chunk(i), columns] = dot_three(parts, split(weight_b[columns]), BOTH_LAST)

        tiles(model, tile)
        second_sums[i].lend()

    swaps = {}

    def second_back(i):
        head_sum = second_sums[i]
        swaps[i] = []
        for p in range(head_sum.pieces):
            at = head_sum.rows_of(p)
            incoming = head_sum.piece(p)
            unit, inverse = unit_rows(result[at])
            through = norm_back(incoming, as_row(second_gain), unit, inverse)
            here = pl.ds(pl.multiple_of(core * half_rows + p * head_sum.size, 8), head_sum.size)
            grad_inputs[at] = cotangent[order[i], here] + through
            late_out[2:3] = late_out[2:3] + down_rows(incoming * unit)
            late_out[3:4] = late_out[3:4] + down_rows(incoming)
            swaps[i].append(comm.copy(grad_inputs.at[at], grad_inputs.at[at], place.sibling))

    late_out[...] = jnp.zeros_like(late_out)
    vectors[...] = jnp.zeros_like(vectors)
    attend(long, own_keys.at[long], True)
    for spread in key_spreads:
        spread.pass_pair()
    attend(short, own_keys.at[short], True)
    weight_to_facing.wait_recv()
    far_weight = rows_at(weight_a, facing * channels, channels)
    weight_onward = comm.copy(far_weight, far_weight, place.sibling)
    key_spreads[short].have_pair()
    attend_level(short, 0)
    for level in range(1, ends[short]):
        key_spreads[short].pass_level(level)
        key_spreads[short].have_level(level)
        attend_level(short, level)
    finish_attention(short)
    key_spreads[long].pass_level(1)
    key_spreads[long].have_pair()
    attend_level(long, 0)
    weight_to_sibling.wait_recv()
    weight_onward.wait_recv()
    mix_near(short)
    key_spreads[long].pass_level(2)
    mix_far(short)
    key_spreads[long].have_level(1)
    attend_level(long, 1)
    load_b.wait()
    load_c.wait()
    key_spreads[long].pass_level(3)
    feed(short, True)
    second_grad(short)
    key_spreads[long].have_level(2)
    attend_level(long, 2)
    second_sums[short].chip()
    crew.add(spread_steps(query_spreads), 0.0, 4.0)
    crew.tick(0.0)
    key_spreads[long].have_level(3)
    attend_level(long, 3)
    finish_attention(long)
    second_back(short)
    crew.tick(4.0)
    mix_near(long)
    crew.tick(4.0)
    mix_far(long)
    crew.tick(4.0)
    feed(long, False)
    crew.tick(4.0)
    second_grad(long)

    def cot_columns(columns):
        return jnp.concatenate([cotangent[order[i], :, columns] for i in range(sequences)], 0)

    active_parts = split(active[...])

    def outer_tile(columns):
        grad_outer[:, columns] = dot_three(active_parts, split(cot_columns(columns)), BOTH_FIRST)

    tiles(model, outer_tile, crew, 0.9)
    def add_sums(wanted, source, target):
        for pair_first, which, start, count, delay in plan:
            if which == wanted:
                make = sum_pair_first if pair_first else sum_line_first
                crew.add(make(comm, place, land, source, target, start, count), delay, HOP)

    add_sums(0, grad_outer, outer_out)

    second_sums[long].chip()

    normed_parts = split(normed_two[...])

    def inner_tile(columns):
        grad_inner[:, columns] = dot_three(normed_parts, split(grad_hidden[:, columns]), BOTH_FIRST)

    tiles(hidden_units, inner_tile, crew, 0.9)
    add_sums(1, grad_inner, inner_out)

    for made in (weight_to_sibling, weight_to_facing, weight_onward):
        comm.settle(made)
    outer_term = weight_a.at[pl.ds(0, tokens)]

    def outer_term_tile(columns):
        outer_term[:, columns] = dot_three(active_parts, split(weight_c[:, columns]), PLAIN)

    tiles(model, outer_term_tile, crew, 0.9)
    second_back(long)
    result_sum = HeadSum(comm, place, outer_term, from_sibling.at[1], from_facing.at[1], 0, rows, 4)
    result_sum.lend()
    for i in (short, long):
        for made in swaps[i]:
            made.wait_recv()
            comm.settle(made)
    crew.tick(8.0)

    weight_parts = split(output_weight[...])
    grad_att[:, channels:] = jnp.zeros((sequences, grad_att.shape[1] - channels, rows), jnp.float32)
    keep_grad = []
    for i in range(sequences):
        alive = alive_lanes(i)
        grad = dot_three(weight_parts, split(grad_inputs[chunk(i)]), BOTH_LAST) * alive
        grad_att[i, 0:channels] = grad
        both = grad * attended_turned[i]
        for head in range(heads):
            at = channels + head
            grad_att[i, at : at + 1] = log_total[i, head : head + 1]
            grad_att[i, at + heads : at + heads + 1] = down_rows(both[head_lanes(head)])
        grad_spreads[i].begin()
        keep_grad.append(comm.local(grad_att.at[i], all_grads.at[seq, i], keep=False))
    result_sum.chip()
    for i in range(sequences):
        for head in range(heads):
            query_cat[i, head] = against(queries[i, head_lanes(head)] * HSIZE ** (-0.5))
            grad_cat[i, head] = against(grad_att[i, head_lanes(head)])
    for spread in grad_spreads:
        spread.pass_pair()
    grad_rest = weight_b
    output_grad = jnp.zeros((channels, model), jnp.float32)
    for i in range(sequences):
        output_grad = output_grad + dot_three(split(attended_turned[i]), split(grad_inputs[chunk(i)]), PLAIN)
    grad_rest[0:channels] = output_grad
    vectors[0:1] = down_rows(grad_inputs[...])
    outer_row = jnp.zeros((1, model), jnp.float32)
    for i in range(sequences):
        outer_row = outer_row + down_rows(cotangent[order[i]])
    vectors[1:2] = outer_row
    add_sums(2, grad_rest, rest_out)
    crew.tick(TICKS)

    grad_query[...] = jnp.zeros_like(grad_query)
    grad_keyval[...] = jnp.zeros_like(grad_keyval)

    def query_side(i, start, end):
        count = jnp.where(z < ends[i], jnp.minimum(seq + 1, end), 0)

        def load(slot, block):
            return pltpu.make_async_copy(keyvals.at[block, i], key_slots.at[slot], slot_sems.at[slot])

        pl.when(count > start)(lambda: load(start % 2, seq - start).start())

        def step(t, carry):
            slot = lax.rem(t, 2)
            load(slot, seq - t).wait()
            pl.when(t + 1 < count)(lambda: load(1 - slot, seq - t - 1).start())
            block = key_slots.at[slot]
            for head in range(heads):
                key_high, key_low = split(block[:, head_lanes(head)])
                scores = dot(jnp.concatenate([key_high, key_high, key_low], 1), query_cat[i, head], PLAIN)
                at = channels + head
                scores = scores - grad_att[i, at : at + 1]
                powers = jnp.exp(jnp.where(allowed_from(scores.shape, t * rows), scores, NEGATIVE))
                slopes = dot(beside(block[:, head_lanes(head, channels)]), grad_cat[i, head], PLAIN)
                slopes = powers * (slopes - grad_att[i, at + heads : at + heads + 1])
                high, low = split(slopes)
                both = dot(jnp.concatenate([key_high, key_low], 1), high, BOTH_FIRST)
                term = both[:HSIZE] + both[HSIZE:] + dot(key_high, low, BOTH_FIRST)
                grad_query[i, head_lanes(head)] = grad_query[i, head_lanes(head)] + term
            return carry

        lax.fori_loop(start, jnp.maximum(count, start), step, 0)

    def key_side(i, offset, query_ref, grad_ref):
        for head in range(heads):
            lanes = head_lanes(head)
            query_high, query_low = split(query_ref[lanes] * HSIZE ** (-0.5))
            grad_high, grad_low = split(grad_ref[lanes])
            scores = dot(
                key_cat[i, head, :, 0 : 3 * HSIZE],
                jnp.concatenate([query_high, query_low, query_high], 0),
                PLAIN,
            )
            at = channels + head
            scores = scores - grad_ref[at : at + 1]
            powers = jnp.exp(jnp.where(allowed_from(scores.shape, offset), scores, NEGATIVE))
            slopes = dot(
                value_cat[i, head, :, 0 : 3 * HSIZE],
                jnp.concatenate([grad_high, grad_low, grad_high], 0),
                PLAIN,
            )
            slopes = powers * (slopes - grad_ref[at + heads : at + heads + 1])
            for base, (far_high, far_low), value in (
                (0, (query_high, query_low), slopes),
                (channels, (grad_high, grad_low), powers),
            ):
                high, low = split(value)
                both = dot(jnp.concatenate([far_high, far_low], 0), high, BOTH_LAST)
                term = both[:HSIZE] + both[HSIZE:] + dot(far_high, low, BOTH_LAST)
                where = slice(base + head * HSIZE, base + (head + 1) * HSIZE)
                grad_keyval[i, where] = grad_keyval[i, where] + term

    def key_level(level, pairs):
        items = [(i, slot) for i in range(sequences) for slot in range(2)]

        def inside(i):
            return z + level < jnp.where(i == 0, ends[0], ends[1])

        def wanted(t):
            i, slot = t // 2, t % 2
            if level:
                return inside(i)
            if pairs:
                return inside(i) & (slot == 1) & (y == 0)
            return inside(i) & (slot == y)

        def loads(t):
            i, slot = t // 2, t % 2
            block = 2 * (z + level) + slot
            return (
                pltpu.make_async_copy(all_queries.at[block, i], query_slots.at[t], slot_sems.at[2 * t]),
                pltpu.make_async_copy(all_grads.at[block, i], grad_slots.at[t], slot_sems.at[2 * t + 1]),
            )

        for t in range(len(items)):
            @pl.when(wanted(t))
            def _(t=t):
                for made in loads(t):
                    made.start()

        def step(t, carry):
            @pl.when(wanted(t))
            def _():
                for made in loads(t):
                    made.wait()
                i, slot = t // 2, t % 2
                offset = (2 * (z + level) + slot - seq) * rows
                key_side(i, offset, query_slots.at[t], grad_slots.at[t])

            return carry

        lax.fori_loop(0, len(items), step, 0)

    def pass_level(level):
        for spread in grad_spreads:
            spread.pass_level(level)

    def have_level(level):
        for spread in query_spreads + grad_spreads:
            spread.have_level(level)

    pass_level(1)
    for i in range(sequences):
        keep_keys[i].wait()
        for head in range(heads):
            key_cat[i, head, :, 0 : 3 * HSIZE] = beside(own_keys[i, :, head_lanes(head)])
            value_cat[i, head, :, 0 : 3 * HSIZE] = beside(own_keys[i, :, head_lanes(head, channels)])
        keep_query[i].wait()
        keep_grad[i].wait()
    key_level(0, False)
    crew.tick(TICKS)
    for spread in query_spreads + grad_spreads:
        spread.have_pair()
    key_level(0, True)
    query_side(0, 0, 4)
    pass_level(2)
    crew.tick(TICKS)
    query_side(0, 4, 8)
    query_side(1, 0, 8)
    have_level(1)
    key_level(1, False)
    crew.tick(TICKS)
    pass_level(3)
    have_level(2)
    key_level(2, False)
    crew.tick(TICKS)
    have_level(3)
    key_level(3, False)
    crew.tick(TICKS)
    returned = []
    for p in range(result_sum.pieces):
        at = result_sum.rows_of(p)
        result[at] = result[at] + as_row(outer_bias) + result_sum.piece(p)
        returned.append(comm.copy(result.at[at], result.at[at], place.sibling))

    for i in range(sequences):
        grad_conv[0, i, pl.ds(0, rows)] = (grad_query[i] * HSIZE ** (-0.5)).T
        grad_conv[1, i, pl.ds(0, rows)] = grad_keyval[i, 0:channels].T
        grad_conv[2, i, pl.ds(0, rows)] = grad_keyval[i, channels : 2 * channels].T

    @pl.when(seq == devices - 1)
    def _():
        grad_conv[:, :, pl.ds(rows, edge)] = jnp.zeros((3, sequences, edge, channels), jnp.float32)

    before = (seq - 1, place.head)
    rim = comm.copy(
        grad_conv.at[:, :, pl.ds(0, edge)], grad_conv.at[:, :, pl.ds(rows, edge)], before, seq > 0
    )
    for k in range(3):
        for j in range(3):
            total = jnp.zeros((1, channels), jnp.float32)
            for i in range(sequences):
                total = total + down_rows(grad_conv[k, i, pl.ds(0, rows)] * raw[k, i, pl.ds(edge - j, rows)])
            vectors[3 + j : 4 + j, k * channels : (k + 1) * channels] = total
    crew.tick(2.0)
    wait_for(rim, seq < devices - 1)
    for k, kernel in enumerate((query_kernel, key_kernel, value_kernel)):
        for i in range(sequences):
            grad_hidden[chunk(i), k * channels : (k + 1) * channels] = (
                kernel[0:1] * grad_conv[k, i, pl.ds(0, rows)]
                + kernel[1:2] * grad_conv[k, i, pl.ds(1, rows)]
                + kernel[2:3] * grad_conv[k, i, pl.ds(2, rows)]
            )
    def first_chunk(which):
        at = pl.ds(pl.multiple_of(which * rows, rows), rows)
        parts = split(grad_hidden[at, 0 : 3 * channels])

        def tile(columns):
            weight = jnp.concatenate([one[:, columns] for one in joined], 0)
            active[at, columns] = dot_three(parts, split(weight), PLAIN)

        tiles(model, tile)

    first_sum = HeadSum(comm, place, active, from_sibling.at[2], from_facing.at[2], 0, rows, 4)
    first_chunk(1 - core)
    first_sum.lend()
    first_chunk(core)
    first_sum.chip()
    crew.tick(3.0)
    for i in range(sequences):
        normed_two[chunk(i)] = first_normed(inputs[order[i]])
    projected_parts = split(grad_hidden[:, 0 : 3 * channels])

    def joined_tile(columns):
        grad_rest[channels : 4 * channels, columns] = dot_three(
            projected_parts, split(normed_two[:, columns]), BOTH_FIRST
        )

    tiles(model, joined_tile, crew, 0.9)
    add_sums(3, grad_rest, rest_out)
    add_sums(4, vectors, vectors_out)
    crew.tick(0.0)

    for p in range(first_sum.pieces):
        at = first_sum.rows_of(p)
        incoming = first_sum.piece(p)
        here = pl.ds(p * first_sum.size, first_sum.size)
        rows_in = jnp.where(core == 0, inputs[order[0], here], inputs[order[1], here])
        unit, inverse = unit_rows(rows_in)
        grad_inputs[at] = grad_inputs[at] + norm_back(incoming, as_row(first_gain), unit, inverse)
        late_out[0:1] = late_out[0:1] + down_rows(incoming * unit)
        late_out[1:2] = late_out[1:2] + down_rows(incoming)
        returned.append(comm.copy(grad_inputs.at[at], grad_inputs.at[at], place.sibling))
        crew.tick(3.5)
    late_sent = comm.copy(late_out, late_from, place.sibling)
    crew.tick(0.0)
    late_sent.wait_recv()
    late_all[seq] = late_out[...] + late_from[...]
    mine = late_all.at[seq]
    shared = [comm.copy(mine, mine, device) for device, _ in column]
    crew.drain()
    for made in returned + shared:
        made.wait_recv()
    comm.settle(late_sent)
    total = late_all[0]
    for k in range(1, devices):
        total = total + late_all[k]
    late_out[...] = total
    comm.finish()
    assert comm.used <= COPIES and comm.used_local <= local_sems.shape[0]


COPIES = 340
LOCALS = 64
SPACE = 5.0
HOP = 5.0
TICKS = 4.0


def sum_plan(hidden_units, model, channels):
    size = channels // 2
    plan = [(k % 3 < 2, 0, k * size, size, k * SPACE) for k in range(hidden_units // size)]
    plan += [(k % 3 == 1, 1, k * size, size, k * SPACE) for k in range(model // size)]
    plan += [(True, 2, 0, size, 0.0), (False, 2, size, size, SPACE / 2)]
    size = channels // 4
    plan += [(True, 3, channels + k * size, size, k * SPACE / 2) for k in range(6)]
    plan += [(False, 3, channels + (6 + k) * size, size, (k + 0.5) * SPACE / 2) for k in range(6)]
    plan += [(True, 4, 0, 16, 0.0)]
    return plan


def layer(ends, collective, lengths, inputs, cotangent, weights, vectors, kernels):
    query_weight, key_weight, value_weight, output_weight, inner_weight, outer_weight = weights
    sequences, rows, model = inputs.shape
    channels = output_weight.shape[0]
    heads = channels // HSIZE
    hidden_units = inner_weight.shape[1]
    tokens = sequences * rows
    devices = lax.axis_size("seq")
    plan = sum_plan(hidden_units, model, channels)
    land_rows = sum(3 * count // 2 if pair_first else 2 * count for pair_first, _, _, count, _ in plan)
    vmem = pl.BlockSpec(memory_space=pltpu.VMEM)
    far = pl.BlockSpec(memory_space=pl.ANY)

    def f32(*shape):
        return jax.ShapeDtypeStruct(shape, jnp.float32)

    def room(*shape, dtype=jnp.float32):
        return pltpu.VMEM(shape, dtype)

    edge = 8
    grad_rows = channels + 16
    half = functools.partial(room, dtype=jnp.bfloat16)
    return pl.pallas_call(
        functools.partial(layer_kernel, ends, plan),
        out_shape=[
            f32(tokens, model),
            f32(tokens, model),
            f32(hidden_units, model),
            f32(model, hidden_units),
            f32(4 * channels, model),
            f32(16, model),
            f32(8, model),
            f32(devices, sequences, rows, 2 * channels),
            f32(devices, sequences, channels, rows),
            f32(devices, sequences, grad_rows, rows),
        ],
        in_specs=[pl.BlockSpec(memory_space=pltpu.SMEM)] + [vmem] * 16 + [far] * 2,
        out_specs=[vmem] * 2 + [far] * 4 + [vmem] + [far] * 3,
        scratch_shapes=[
            room(sequences, edge, model),
            room(model, model),
            room(model, hidden_units),
            room(hidden_units, model),
            room(3, sequences, rows + edge, channels),
            room(4, sequences, channels, rows),
            room(sequences, channels, rows),
            room(sequences, channels, rows),
            room(sequences, 8, rows),
            room(sequences, 8, rows),
            room(sequences, channels, rows),
            room(sequences, 8, rows),
            room(tokens, model),
            room(tokens, hidden_units),
            room(tokens, hidden_units),
            room(tokens, model),
            room(3, rows, model),
            room(3, rows, model),
            room(hidden_units, model),
            room(model, hidden_units),
            room(16, model),
            room(land_rows, model),
            room(2 * sequences, rows, 2 * channels),
            room(sequences, rows, 2 * channels),
            room(2 * sequences, channels, rows),
            room(2 * sequences, grad_rows, rows),
            half(sequences, heads, 3 * HSIZE, rows),
            half(sequences, heads, 3 * HSIZE, rows),
            half(sequences, heads, rows, 256),
            half(sequences, heads, rows, 256),
            room(sequences, grad_rows, rows),
            room(sequences, channels, rows),
            room(sequences, 2 * channels, rows),
            room(3, sequences, rows + edge, channels),
            room(8, model),
            room(devices, 8, model),
            pltpu.SemaphoreType.DMA((COPIES,)),
            pltpu.SemaphoreType.DMA((COPIES,)),
            pltpu.SemaphoreType.DMA((LOCALS,)),
            pltpu.SemaphoreType.DMA((4 * sequences,)),
        ],
        compiler_params=pltpu.CompilerParams(
            collective_id=collective, has_side_effects=True, vmem_limit_bytes=63 * 2**20
        ),
        name="mega",
    )(
        lengths,
        inputs,
        cotangent,
        query_weight.T,
        key_weight.T,
        value_weight.T,
        output_weight,
        *vectors,
        *kernels,
        inner_weight,
        outer_weight,
    )


def shards(
    inputs,
    seq_lengths,
    first_gain,
    first_shift,
    query_weight,
    key_weight,
    value_weight,
    query_kernel,
    key_kernel,
    value_kernel,
    output_weight,
    output_bias,
    second_gain,
    second_shift,
    inner_weight,
    hidden_layer_bias,
    outer_weight,
    outer_bias,
    cotangent,
):
    channels = query_weight.shape[1]
    kernels = (query_kernel, key_kernel, value_kernel)

    def run(short_end, collective):
        ends = (LINE, short_end)
        result, grad_inputs, grad_outer, grad_inner, rest, vectors, late = layer(
            ends,
            collective,
            seq_lengths,
            inputs,
            cotangent,
            (query_weight, key_weight, value_weight, output_weight, inner_weight, outer_weight),
            (
                output_bias,
                first_gain,
                first_shift,
                second_gain,
                second_shift,
                hidden_layer_bias,
                outer_bias,
            ),
            kernels,
        )[:7]
        swap = seq_lengths[1] > seq_lengths[0]

        def placed(array):
            array = array.reshape(inputs.shape)
            return jnp.where(swap, jnp.flip(array, 0), array)

        mixes = vectors[3:6, : 3 * channels]
        return (
            placed(result),
            placed(grad_inputs),
            late[0],
            late[1],
            rest[channels : 2 * channels].T,
            rest[2 * channels : 3 * channels].T,
            rest[3 * channels : 4 * channels].T,
            mixes[:, :channels],
            mixes[:, channels : 2 * channels],
            mixes[:, 2 * channels :],
            rest[:channels],
            vectors[0],
            late[2],
            late[3],
            grad_inner,
            vectors[2],
            grad_outer,
            vectors[1],
        )

    pair_rows = 2 * inputs.shape[1]
    shorter = jnp.minimum(seq_lengths[0], seq_lengths[1])
    reach = (shorter > pair_rows).astype(jnp.int32) + (shorter > 2 * pair_rows)
    cases = [functools.partial(run, end, 1 + k) for k, end in enumerate((1, 2, LINE))]
    return lax.switch(reach, cases)


def solution(mesh):
    lines = mesh.shape["seq"] == 2 * LINE and mesh.shape["head"] == 4
    return jax.shard_map(
        shards if lines else general_shards,
        mesh=mesh,
        in_specs=(
            P(None, "seq", None),
            P(),
            P(),
            P(),
            P(None, "head"),
            P(None, "head"),
            P(None, "head"),
            P(None, "head"),
            P(None, "head"),
            P(None, "head"),
            P("head", None),
            P(),
            P(),
            P(),
            P(None, "head"),
            P("head"),
            P("head", None),
            P(),
            P(None, "seq", None),
        ),
        out_specs=(
            P(None, "seq", None),
            P(None, "seq", None),
            P(),
            P(),
            P(None, "head"),
            P(None, "head"),
            P(None, "head"),
            P(None, "head"),
            P(None, "head"),
            P(None, "head"),
            P("head", None),
            P(),
            P(),
            P(),
            P(None, "head"),
            P("head"),
            P("head", None),
            P(),
        ),
        check_vma=False,
    )
```

```python
import functools

import jax
import jax.numpy as jnp
from jax import lax
from jax.experimental import pallas as pl
from jax.experimental.pallas import tpu as pltpu
from jax.sharding import PartitionSpec as P

MESH = pl.DeviceIdType.MESH

HSIZE = 64


EXACT_FLOAT_MODE = lax.Precision.HIGH
EPSILON = 1e-05
NEGATIVE = -1e30


def shifted(block, axis, distance):
    devices = range(lax.axis_size(axis))
    route = [(i - distance, i) for i in devices if i - distance in devices]
    return lax.ppermute(block, axis, route)


def matmul(input_operand, weight_matrix):
    return jnp.einsum("scd,df->scf", input_operand, weight_matrix, precision=EXACT_FLOAT_MODE)


def transposed(input_operand, weight_matrix):
    return jnp.einsum("scf,df->scd", input_operand, weight_matrix, precision=EXACT_FLOAT_MODE)


def outer_sum(first_rows, second_rows):
    return jnp.einsum("scd,scf->df", first_rows, second_rows, precision=EXACT_FLOAT_MODE)


def normalize(stream, norm_gain, norm_shift):
    centered = stream - jnp.mean(stream, -1, keepdims=True)
    inverse = lax.rsqrt(jnp.mean(centered * centered, -1, keepdims=True) + EPSILON)
    unit_rows = centered * inverse
    return (unit_rows * norm_gain + norm_shift, unit_rows, inverse)


def normalize_back(gradient, norm_gain, unit_rows, inverse):
    scaled = gradient * norm_gain
    middle = (
        scaled
        - jnp.mean(scaled, -1, keepdims=True)
        - unit_rows * jnp.mean(scaled * unit_rows, -1, keepdims=True)
    )
    return (inverse * middle, jnp.sum(gradient * unit_rows, (0, 1)), jnp.sum(gradient, (0, 1)))


def split_heads(flat):
    return flat.reshape(flat.shape[0], flat.shape[1], flat.shape[2] // HSIZE, HSIZE)


def allowed_pairs(query_pos, key_pos, lengths):
    return (key_pos[None, None, :] <= query_pos[None, :, None]) & (
        key_pos[None, None, :] < lengths[:, None, None]
    )


def pair_terms(queries, gradients, log_total, row_dots, query_pos, keyvals, key_pos, lengths):
    channels = queries.shape[2]
    query_heads = split_heads(queries)
    key_heads = split_heads(keyvals[:, :, :channels])
    value_heads = split_heads(keyvals[:, :, channels:])
    grad_heads = split_heads(gradients)
    scores = jnp.einsum(
        "sqhe,skhe->shqk", query_heads, key_heads, precision=EXACT_FLOAT_MODE
    ) * HSIZE ** (-0.5)
    allowed = allowed_pairs(query_pos, key_pos, lengths)[:, None]
    weight_values = jnp.exp(jnp.where(allowed, scores - log_total[..., None], NEGATIVE))
    weight_grads = jnp.einsum(
        "sqhe,skhe->shqk", grad_heads, value_heads, precision=EXACT_FLOAT_MODE
    )
    score_grads = weight_values * (weight_grads - row_dots[..., None])
    return (weight_values, score_grads, query_heads, key_heads, grad_heads)


def key_facing_term(terms, keyvals, channels):
    value_part = jnp.einsum("shqk,sqhe->skhe", terms[0], terms[4], precision=EXACT_FLOAT_MODE)
    key_part = jnp.einsum(
        "shqk,sqhe->skhe", terms[1], terms[2], precision=EXACT_FLOAT_MODE
    ) * HSIZE ** (-0.5)
    shape = (keyvals.shape[0], keyvals.shape[1], channels)
    return jnp.concatenate([key_part.reshape(shape), value_part.reshape(shape)], 2)


def query_side_term(terms):
    return jnp.einsum(
        "shqk,skhe->sqhe", terms[1], terms[3], precision=EXACT_FLOAT_MODE
    ) * HSIZE ** (-0.5)


def key_terms(queries, gradients, log_total, row_dots, query_pos, keyvals, key_pos, lengths):
    terms = pair_terms(
        queries, gradients, log_total, row_dots, query_pos, keyvals, key_pos, lengths
    )
    return key_facing_term(terms, keyvals, queries.shape[2])


def general_shards(
    inputs,
    seq_lengths,
    first_gain,
    first_shift,
    query_weight,
    key_weight,
    value_weight,
    query_kernel,
    key_kernel,
    value_kernel,
    output_weight,
    output_bias,
    second_gain,
    second_shift,
    inner_weight,
    hidden_layer_bias,
    outer_weight,
    outer_bias,
    cotangent,
):
    sequences, rows, model = inputs.shape
    channels = query_weight.shape[1]
    heads = channels // HSIZE
    positions = lax.axis_index("seq") * rows + jnp.arange(rows, dtype=jnp.int32)
    live_rows = (positions[None, :] < seq_lengths[:, None]).astype(jnp.float32)
    joined_weight = jnp.concatenate([query_weight, key_weight, value_weight], 1)
    joined_kernel = jnp.concatenate([query_kernel, key_kernel, value_kernel], 1)
    normed, leading_unit_value, first_inverse = normalize(inputs, first_gain, first_shift)
    projected = matmul(normed, joined_weight)
    rims = shifted(projected[:, rows - 2 :, :], "seq", 1)
    extended = jnp.concatenate([rims, projected], 1)
    convolved = (
        joined_kernel[0] * extended[:, 2:]
        + joined_kernel[1] * extended[:, 1:-1]
        + joined_kernel[2] * extended[:, :-2]
    )
    queries = convolved[:, :, :channels]
    keyvals = convolved[:, :, channels:]
    query_heads = split_heads(queries)
    portion = lax.all_gather(keyvals, "seq", axis=1, tiled=True)
    highest = jnp.full((sequences, heads, rows), NEGATIVE, jnp.float32)
    key_pos = jnp.arange(portion.shape[1], dtype=jnp.int32)
    key_heads = split_heads(portion[:, :, :channels])
    value_heads = split_heads(portion[:, :, channels:])
    scores = jnp.einsum(
        "sqhe,skhe->shqk", query_heads, key_heads, precision=EXACT_FLOAT_MODE
    ) * HSIZE ** (-0.5)
    allowed = allowed_pairs(positions, key_pos, seq_lengths)[:, None]
    masked = jnp.where(allowed, scores, NEGATIVE)
    new_high = jnp.maximum(highest, jnp.max(masked, -1))
    weight_values = jnp.where(allowed, jnp.exp(masked - new_high[..., None]), 0.0)
    summed = jnp.sum(weight_values, -1)
    weighted = jnp.einsum("shqk,skhe->shqe", weight_values, value_heads, precision=EXACT_FLOAT_MODE)
    highest, summed, weighted = (new_high, summed, weighted)
    log_total = highest + jnp.log(summed)
    attended = (weighted / summed[..., None]).transpose(0, 2, 1, 3).reshape(
        sequences, rows, channels
    ) * live_rows[..., None]
    branch = lax.psum(matmul(attended, output_weight), "head")
    mixed = inputs + branch + output_bias
    normed_two, second_unit, second_inverse = normalize(mixed, second_gain, second_shift)
    hidden = matmul(normed_two, inner_weight) + hidden_layer_bias
    rectified = jnp.maximum(hidden, 0.0)
    active = rectified * rectified
    result = mixed + lax.psum(matmul(active, outer_weight), "head") + outer_bias
    grad_outer_weight = outer_sum(active, cotangent)
    grad_outer_bias = jnp.sum(cotangent, (0, 1))
    grad_hidden = transposed(cotangent, outer_weight) * (2.0 * rectified)
    grad_inner_weight = outer_sum(normed_two, grad_hidden)
    grad_inner_bias = jnp.sum(grad_hidden, (0, 1))
    grad_normed_two = lax.psum(transposed(grad_hidden, inner_weight), "head")
    through_two, grad_second_gain, grad_second_shift = normalize_back(
        grad_normed_two, second_gain, second_unit, second_inverse
    )
    grad_mixed = cotangent + through_two
    grad_output_weight = outer_sum(attended, grad_mixed)
    grad_output_bias = jnp.sum(grad_mixed, (0, 1))
    grad_attended = transposed(grad_mixed, output_weight) * live_rows[..., None]
    row_dots = jnp.sum(split_heads(grad_attended) * split_heads(attended), -1).transpose(0, 2, 1)
    terms = pair_terms(
        queries, grad_attended, log_total, row_dots, positions, portion, key_pos, seq_lengths
    )
    grad_queries = query_side_term(terms).reshape(jnp.zeros_like(queries).shape)
    query_side = jnp.concatenate([queries, grad_attended], 2)
    row_stats = jnp.concatenate([log_total, row_dots], 1).transpose(0, 2, 1)
    side_rows = lax.all_gather(query_side, "seq", axis=1, tiled=True)
    stat_rows = lax.all_gather(row_stats, "seq", axis=1, tiled=True)
    query_pos = jnp.arange(side_rows.shape[1], dtype=jnp.int32)
    portion_total = stat_rows[:, :, :heads].transpose(0, 2, 1)
    portion_dots = stat_rows[:, :, heads:].transpose(0, 2, 1)
    grad_keyvals = key_terms(
        side_rows[:, :, :channels],
        side_rows[:, :, channels:],
        portion_total,
        portion_dots,
        query_pos,
        keyvals,
        positions,
        seq_lengths,
    )
    grad_convolved = jnp.concatenate([grad_queries, grad_keyvals], 2)
    following = shifted(grad_convolved[:, :2, :], "seq", -1)
    grad_extended = jnp.concatenate([grad_convolved, following], 1)
    grad_projected = (
        joined_kernel[0] * grad_extended[:, :rows]
        + joined_kernel[1] * grad_extended[:, 1 : rows + 1]
        + joined_kernel[2] * grad_extended[:, 2:]
    )
    grad_kernel = jnp.stack(
        [
            jnp.sum(grad_convolved * extended[:, 2:], (0, 1)),
            jnp.sum(grad_convolved * extended[:, 1:-1], (0, 1)),
            jnp.sum(grad_convolved * extended[:, :-2], (0, 1)),
        ]
    )
    grad_joined = outer_sum(normed, grad_projected)
    grad_normed = lax.psum(transposed(grad_projected, joined_weight), "head")
    through_one, grad_first_gain, grad_first_shift = normalize_back(
        grad_normed, first_gain, leading_unit_value, first_inverse
    )
    grad_inputs = grad_mixed + through_one
    grad_query_weight = grad_joined[:, :channels]
    grad_key_weight = grad_joined[:, channels : 2 * channels]
    grad_value_weight = grad_joined[:, 2 * channels :]
    grad_query_kernel = grad_kernel[:, :channels]
    grad_key_kernel = grad_kernel[:, channels : 2 * channels]
    grad_value_kernel = grad_kernel[:, 2 * channels :]
    (
        grad_first_gain,
        grad_first_shift,
        grad_query_weight,
        grad_key_weight,
        grad_value_weight,
        grad_query_kernel,
        grad_key_kernel,
        grad_value_kernel,
        grad_output_weight,
        grad_output_bias,
        grad_second_gain,
        grad_second_shift,
        grad_inner_weight,
        grad_inner_bias,
        grad_outer_weight,
        grad_outer_bias,
    ) = lax.psum(
        (
            grad_first_gain,
            grad_first_shift,
            grad_query_weight,
            grad_key_weight,
            grad_value_weight,
            grad_query_kernel,
            grad_key_kernel,
            grad_value_kernel,
            grad_output_weight,
            grad_output_bias,
            grad_second_gain,
            grad_second_shift,
            grad_inner_weight,
            grad_inner_bias,
            grad_outer_weight,
            grad_outer_bias,
        ),
        "seq",
    )
    return (
        result,
        grad_inputs,
        grad_first_gain,
        grad_first_shift,
        grad_query_weight,
        grad_key_weight,
        grad_value_weight,
        grad_query_kernel,
        grad_key_kernel,
        grad_value_kernel,
        grad_output_weight,
        grad_output_bias,
        grad_second_gain,
        grad_second_shift,
        grad_inner_weight,
        grad_inner_bias,
        grad_outer_weight,
        grad_outer_bias,
    )


class Comm:
    def __init__(self, send_sems, recv_sems, local_sems=None):
        self.send_sems, self.recv_sems, self.local_sems = send_sems, recv_sems, local_sems
        self.used = 0
        self.used_local = 0
        self.sent = []
        self.stored = []

    def copy(self, source, target, device, when=None):
        index = self.used
        self.used += 1
        made = pltpu.make_async_remote_copy(
            src_ref=source,
            dst_ref=target,
            send_sem=self.send_sems.at[index],
            recv_sem=self.recv_sems.at[index],
            device_id=device,
            device_id_type=MESH,
        )
        if when is None:
            made.start()
        else:
            pl.when(when)(made.start)
        self.sent.append((made, when))
        return made

    def settle(self, made):
        self.sent = [one for one in self.sent if one[0] is not made]
        made.wait_send()

    def local(self, source, target, when=None, keep=True):
        made = pltpu.make_async_copy(source, target, self.local_sems.at[self.used_local])
        self.used_local += 1
        if when is None:
            made.start()
        else:
            pl.when(when)(made.start)
        if keep:
            self.stored.append((made, when))
        return made

    def finish(self):
        for made, when in self.sent:
            if when is None:
                made.wait_send()
            else:
                pl.when(when)(made.wait_send)
        for made, when in self.stored:
            if when is None:
                made.wait()
            else:
                pl.when(when)(made.wait)


def wait_for(made, when=None):
    if when is None:
        made.wait_recv()
    else:
        pl.when(when)(made.wait_recv)


class Place:
    def __init__(self):
        self.seq = lax.axis_index("seq")
        self.head = lax.axis_index("head")
        self.z = self.seq // 2
        self.y = self.seq % 2
        self.other = 1 - self.y
        self.core = self.head % 2
        self.at_end = (self.z == 0) | (self.z == LINE - 1)
        self.at_middle = jnp.logical_not(self.at_end)
        step = 2 - 4 * (self.z // 2)
        self.pair = (2 * self.z + self.other, self.head)
        self.inward = (self.seq + step, self.head)
        self.outward = (self.seq - step, self.head)
        self.sibling = (self.seq, self.head + 1 - 2 * self.core)
        self.facing = (self.seq, (self.head + 2) % 4)


LINE = 4


def rows_at(ref, start, count):
    return ref.at[pl.ds(pl.multiple_of(start, 8), count)]


class Land:
    def __init__(self, ref):
        self.ref, self.used = ref, 0

    def take(self, rows):
        got = self.ref.at[pl.ds(self.used, rows)]
        self.used += rows
        return got


def sum_pair_first(comm, place, land, source, target, start, count):
    half = count // 2
    line, from_end, from_middle = land.take(half), land.take(half), land.take(half)
    own = rows_at(target, start + place.y * half, half)
    far = rows_at(source, start + place.other * half, half)
    near = rows_at(source, start + place.y * half, half)
    made = comm.copy(far, line, place.pair)
    yield
    made.wait_recv()
    line[...] = line[...] + near[...]
    inward = comm.copy(line, from_end, place.inward, place.at_end)
    yield

    @pl.when(place.at_middle)
    def _():
        inward.wait_recv()
        from_end[...] = from_end[...] + line[...]

    across = comm.copy(from_end, from_middle, place.inward, place.at_middle)
    yield

    @pl.when(place.at_middle)
    def _():
        across.wait_recv()
        from_middle[...] = from_middle[...] + from_end[...]

    outward = comm.copy(from_middle, own, place.outward, place.at_middle)
    early = comm.copy(from_middle, own, place.pair, place.at_middle)
    comm.local(from_middle, own, place.at_middle)
    yield
    wait_for(outward, place.at_end)
    late = comm.copy(own, own, place.pair, place.at_end)
    yield
    wait_for(early, place.at_middle)
    wait_for(late, place.at_end)
    yield


def sum_line_first(comm, place, land, source, target, start, count):
    half = count // 2
    whole, from_middle, from_pair = land.take(count), land.take(half), land.take(half)
    all_rows = rows_at(source, start, count)
    mine, theirs = place.z // 2, 1 - place.z // 2
    own, rest = rows_at(target, start + mine * half, half), rows_at(target, start + theirs * half, half)
    inward = comm.copy(all_rows, whole, place.inward, place.at_end)
    yield

    @pl.when(place.at_middle)
    def _():
        inward.wait_recv()
        whole[...] = whole[...] + all_rows[...]

    across = comm.copy(rows_at(whole, theirs * half, half), from_middle, place.inward, place.at_middle)
    yield

    @pl.when(place.at_middle)
    def _():
        across.wait_recv()
        from_middle[...] = from_middle[...] + rows_at(whole, mine * half, half)[...]

    paired = comm.copy(from_middle, from_pair, place.pair, place.at_middle)
    yield

    @pl.when(place.at_middle)
    def _():
        paired.wait_recv()
        from_pair[...] = from_pair[...] + from_middle[...]

    back = comm.copy(from_pair, own, place.inward, place.at_middle)
    outward = comm.copy(from_pair, own, place.outward, place.at_middle)
    comm.local(from_pair, own, place.at_middle)
    yield
    wait_for(back, place.at_middle)
    last = comm.copy(rest, rest, place.outward, place.at_middle)
    yield
    wait_for(outward, place.at_end)
    wait_for(last, place.at_end)
    yield


class Crew:
    def __init__(self):
        self.due = []
        self.now = 0.0
        self.added = 0

    def add(self, one, delay=0.0, hop=6.0):
        self.added += 1
        self.due.append((self.now + delay, self.added, one, hop))

    def step(self):
        entry = min(self.due, key=lambda each: each[:2])
        self.due.remove(entry)
        time, number, one, hop = entry
        try:
            next(one)
            self.due.append((time + hop, number, one, hop))
        except StopIteration:
            pass

    def tick(self, length):
        self.now += length
        while self.due and min(each[0] for each in self.due) <= self.now:
            self.step()

    def drain(self):
        while self.due:
            self.step()


def split(value):
    high = value.astype(jnp.bfloat16)
    return high, (value - high.astype(jnp.float32)).astype(jnp.bfloat16)


def dot(left, right, dims):
    return lax.dot_general(left, right, (dims, ((), ())), preferred_element_type=jnp.float32)


def dot_three(left, right, dims):
    return dot(left[0], right[0], dims) + (dot(left[0], right[1], dims) + dot(left[1], right[0], dims))


PLAIN, BOTH_LAST, BOTH_FIRST = ((1,), (0,)), ((1,), (1,)), ((0,), (0,))


def product(left, right, dims=PLAIN):
    return dot_three(split(left), split(right), dims)


def beside(value):
    high, low = split(value)
    return jnp.concatenate([high, high, low], 1)


def against(value):
    high, low = split(value)
    return jnp.concatenate([high, low, high], 0)


def as_row(ref):
    return ref[...].reshape(1, ref.shape[0])


def unit_rows(rows):
    centered = rows - jnp.mean(rows, -1, keepdims=True)
    inverse = lax.rsqrt(jnp.mean(centered * centered, -1, keepdims=True) + EPSILON)
    return centered * inverse, inverse


def longer_first(lengths):
    return jnp.where(lengths[1] > lengths[0], 1, 0).astype(jnp.int32)


def head_lanes(head, base=0):
    return slice(base + head * HSIZE, base + (head + 1) * HSIZE)


class Spread:
    def __init__(self, comm, place, part, ends, upward=True, own=None):
        self.comm, self.place, self.part, self.ends = comm, place, part, ends
        self.own = own or (lambda half: part(place.seq, half))
        z, y = place.z, place.y
        self.rank = z if upward else ends - 1 - z
        self.inside = z < ends
        self.more = self.inside & ((z < ends - 1) if upward else (z > 0))
        self.leads = (y == 0) if upward else (y == 1)
        self.next = (place.seq + (2 if upward else -2), place.head)
        self.sign = 1 if upward else -1
        self.up = {}
        self.over = {}

    def block(self, level, slot):
        place = self.place
        side = place.y if slot == 0 else place.other
        return 2 * (place.z - self.sign * level) + side

    def begin(self):
        comm, place, part = self.comm, self.place, self.part
        near, far = part(place.seq, place.y), part(place.seq, place.other)
        mine = self.own(place.y)
        self.lend = comm.copy(self.own(place.other), far, place.pair, self.inside & (self.more | self.leads))
        self.up[1, 0] = comm.copy(mine, near, self.next, self.more)
        self.give = comm.copy(mine, near, place.pair, self.inside & self.leads)

    def pass_pair(self):
        comm, place, part = self.comm, self.place, self.part
        follows = jnp.logical_not(self.leads)
        wait_for(self.lend, self.inside & (self.more | follows))
        lent = part(self.block(0, 1), place.y)
        self.up[1, 1] = comm.copy(lent, lent, self.next, self.more)

    def have_pair(self):
        wait_for(self.give, self.inside & jnp.logical_not(self.leads))

    def pass_level(self, level):
        comm, place, part = self.comm, self.place, self.part
        if level >= self.ends:
            return
        here = self.inside & (self.rank >= level)
        for slot in range(2):
            half = part(self.block(level, slot), place.y)
            wait_for(self.up[level, slot], here)
            if level < self.ends - 1:
                self.up[level + 1, slot] = comm.copy(half, half, self.next, here & self.more)
            self.over[level, slot] = comm.copy(half, half, place.pair, here)

    def have_level(self, level):
        if level >= self.ends:
            return
        here = self.inside & (self.rank >= level)
        for slot in range(2):
            wait_for(self.over[level, slot], here)


def greet(partners):
    barrier = pltpu.get_barrier_semaphore()
    count = jnp.int32(0)
    for device, when in partners:
        def tell(device=device):
            pl.semaphore_signal(barrier, inc=1, device_id=device, device_id_type=MESH)

        if when is None:
            tell()
            count = count + 1
        else:
            pl.when(when)(tell)
            count = count + when.astype(jnp.int32)
    pl.semaphore_wait(barrier, count)


def line_partners(place):
    return [
        (place.pair, None),
        ((place.seq + 2, place.head), place.z < LINE - 1),
        ((place.seq - 2, place.head), place.z > 0),
    ]


def head_partners(place):
    return [(place.sibling, None), (place.facing, None)]


def step_partners(place):
    return [
        ((place.seq + 1, place.head), (place.y == 1) & (place.z < LINE - 1)),
        ((place.seq - 1, place.head), (place.y == 0) & (place.z > 0)),
    ]


class HeadSum:
    def __init__(self, comm, place, partial, from_sibling, from_facing, start, rows, pieces):
        self.comm, self.place = comm, place
        self.from_sibling, self.from_facing = from_sibling, from_facing
        self.rows, self.pieces, self.start = rows, pieces, start
        self.size = rows // pieces
        self.near = rows_at(partial, start + place.core * rows, rows)
        self.far = rows_at(partial, start + (1 - place.core) * rows, rows)

    def lend(self):
        self.lent = self.comm.copy(self.far, self.from_sibling, self.place.sibling)

    def rows_of(self, p):
        return pl.ds(pl.multiple_of(self.start + self.place.core * self.rows + p * self.size, 8), self.size)

    def chip(self):
        self.lent.wait_recv()
        self.near[...] = self.near[...] + self.from_sibling[...]
        self.sent = []
        for p in range(self.pieces):
            at = pl.ds(p * self.size, self.size)
            self.sent.append(self.comm.copy(self.near.at[at], self.from_facing.at[at], self.place.facing))

    def piece(self, p):
        self.sent[p].wait_recv()
        at = pl.ds(p * self.size, self.size)
        return self.near[at] + self.from_facing[at]


def norm_back(grad, gain, unit, inverse):
    scaled = grad * gain
    return inverse * (
        scaled - jnp.mean(scaled, -1, keepdims=True) - unit * jnp.mean(scaled * unit, -1, keepdims=True)
    )


def spread_steps(spreads):
    for spread in spreads:
        spread.begin()
    yield
    for spread in spreads:
        spread.pass_pair()
    yield
    for level in range(1, LINE):
        for spread in spreads:
            spread.pass_level(level)
        yield


TILE = 256


def tiles(width, body, crew=None, length=0.0):
    def step(j, carry):
        body(pl.ds(pl.multiple_of(j * TILE, TILE), TILE))
        return carry

    lax.fori_loop(0, width // TILE, step, 0)
    if crew is not None:
        crew.tick(length * (width // TILE))


def down_rows(value):
    return jnp.sum(value, 0, keepdims=True)


def allowed_from(shape, offset):
    key_pos = lax.broadcasted_iota(jnp.int32, shape, 0)
    query_pos = lax.broadcasted_iota(jnp.int32, shape, 1)
    return key_pos <= query_pos + offset


def layer_kernel(
    ends,
    plan,
    lengths,
    inputs,
    cotangent,
    query_weight,
    key_weight,
    value_weight,
    output_weight,
    output_bias,
    first_gain,
    first_shift,
    second_gain,
    second_shift,
    hidden_bias,
    outer_bias,
    query_kernel,
    key_kernel,
    value_kernel,
    inner_weight,
    outer_weight,
    result,
    grad_inputs,
    outer_out,
    inner_out,
    rest_out,
    vectors_out,
    late_out,
    keyvals,
    all_queries,
    all_grads,
    halo,
    weight_a,
    weight_b,
    weight_c,
    raw,
    groups,
    attended_turned,
    queries,
    highest,
    summed,
    weighted,
    log_total,
    normed_two,
    active,
    grad_hidden,
    grad_normed,
    from_sibling,
    from_facing,
    grad_outer,
    grad_inner,
    vectors,
    land_ref,
    key_slots,
    own_keys,
    query_slots,
    grad_slots,
    query_cat,
    grad_cat,
    key_cat,
    value_cat,
    grad_att,
    grad_query,
    grad_keyval,
    grad_conv,
    late_from,
    late_all,
    send_sems,
    recv_sems,
    local_sems,
    slot_sems,
):
    place = Place()
    comm = Comm(send_sems, recv_sems, local_sems)
    land = Land(land_ref)
    crew = Crew()
    sequences, rows, model = inputs.shape
    channels = output_weight.shape[0]
    heads = channels // HSIZE
    hidden_units = hidden_bias.shape[0]
    tokens = sequences * rows
    z, y, seq, core = place.z, place.y, place.seq, place.core
    first = longer_first(lengths)
    order = (first, 1 - first)
    devices = 2 * LINE
    edge = halo.shape[1]
    long, short = 0, 1
    joined = (query_weight, key_weight, value_weight)
    column = [((lax.rem(seq + k, devices), place.head), None) for k in range(1, devices)]
    greet(column + head_partners(place))

    def chunk(i):
        return pl.ds(i * rows, rows)

    rim = comm.copy(
        inputs.at[:, pl.ds(rows - edge, edge)], halo, (seq + 1, place.head), seq < devices - 1
    )
    own_weight = rows_at(weight_a, place.head * channels, channels)
    own_weight[...] = output_weight[...]
    weight_to_sibling = comm.copy(own_weight, own_weight, place.sibling)
    weight_to_facing = comm.copy(own_weight, own_weight, place.facing)
    load_b = comm.local(inner_weight, weight_b, keep=False)
    load_c = comm.local(outer_weight, weight_c, keep=False)

    def first_normed(value):
        return unit_rows(value)[0] * as_row(first_gain) + as_row(first_shift)

    for i in range(sequences):
        normed_two[chunk(i)] = first_normed(inputs[order[i]])
    wait_for(rim, seq > 0)
    rim_parts = split(jnp.concatenate([first_normed(halo[order[i]]) for i in range(sequences)], 0))
    normed_parts = split(normed_two[...])
    for k, weight in enumerate(joined):
        parts = split(weight[...])
        whole = dot_three(normed_parts, parts, BOTH_LAST)
        before = jnp.where(seq > 0, dot_three(rim_parts, parts, BOTH_LAST), 0.0)
        for i in range(sequences):
            raw[k, i, pl.ds(0, edge)] = before[i * edge : (i + 1) * edge]
            raw[k, i, pl.ds(edge, rows)] = whole[i * rows : (i + 1) * rows]

    def convolved(k, i, kernel):
        return (
            kernel[0:1] * raw[k, i, pl.ds(edge, rows)]
            + kernel[1:2] * raw[k, i, pl.ds(edge - 1, rows)]
            + kernel[2:3] * raw[k, i, pl.ds(edge - 2, rows)]
        )

    def key_part(block, half, i):
        return keyvals.at[block, i, pl.ds(pl.multiple_of(half * (rows // 2), 8), rows // 2)]

    def key_own(half, i):
        return own_keys.at[i, pl.ds(pl.multiple_of(half * (rows // 2), 8), rows // 2)]

    key_spreads = []
    keep_keys = []
    for i in range(sequences):
        own_keys[i, :, 0:channels] = convolved(1, i, key_kernel)
        own_keys[i, :, channels : 2 * channels] = convolved(2, i, value_kernel)
        key_spreads.append(
            Spread(
                comm,
                place,
                functools.partial(key_part, i=i),
                ends[i],
                True,
                functools.partial(key_own, i=i),
            )
        )
        key_spreads[i].begin()
        keep_keys.append(comm.local(own_keys.at[i], keyvals.at[seq, i], keep=False))
    keep_query = []
    for i in range(sequences):
        query = convolved(0, i, query_kernel).T
        queries[i] = query
        for head in range(heads):
            query_cat[i, head] = against(query[head_lanes(head)] * HSIZE ** (-0.5))
        keep_query.append(comm.local(queries.at[i], all_queries.at[seq, i], keep=False))

    def query_part(block, half, i):
        return all_queries.at[block, i, pl.ds(pl.multiple_of(half * (channels // 2), 8), channels // 2)]

    def query_own(half, i):
        return queries.at[i, pl.ds(pl.multiple_of(half * (channels // 2), 8), channels // 2)]

    def grad_part(block, half, i):
        size = grad_att.shape[1] // 2
        return all_grads.at[block, i, pl.ds(pl.multiple_of(half * size, 8), size)]

    def grad_own(half, i):
        size = grad_att.shape[1] // 2
        return grad_att.at[i, pl.ds(pl.multiple_of(half * size, 8), size)]

    query_spreads = [
        Spread(
            comm,
            place,
            functools.partial(query_part, i=i),
            ends[i],
            False,
            functools.partial(query_own, i=i),
        )
        for i in range(sequences)
    ]
    grad_spreads = [
        Spread(
            comm,
            place,
            functools.partial(grad_part, i=i),
            ends[i],
            False,
            functools.partial(grad_own, i=i),
        )
        for i in range(sequences)
    ]

    def attend(i, own, diagonal):
        for head in range(heads):
            scores = dot(beside(own[:, head_lanes(head)]), query_cat[i, head], PLAIN)
            lane = pl.ds(head, 1)
            if diagonal:
                scores = jnp.where(allowed_from(scores.shape, 0), scores, NEGATIVE)
                high = jnp.max(scores, 0, keepdims=True)
            else:
                old = highest[i, lane]
                high = jnp.maximum(old, jnp.max(scores, 0, keepdims=True))
            powers = jnp.exp(scores - high)
            total = jnp.sum(powers, 0, keepdims=True)
            power_high, power_low = split(powers)
            value_high, value_low = split(own[:, head_lanes(head, channels)])
            both = dot(jnp.concatenate([value_high, value_low], 1), power_high, BOTH_FIRST)
            term = both[:HSIZE] + both[HSIZE:] + dot(value_high, power_low, BOTH_FIRST)
            at = pl.ds(head * HSIZE, HSIZE)
            if diagonal:
                summed[i, lane] = total
                weighted[i, at] = term
            else:
                scale = jnp.exp(old - high)
                summed[i, lane] = summed[i, lane] * scale + total
                weighted[i, at] = weighted[i, at] * scale + term
            highest[i, lane] = high

    def attend_level(i, level):
        if level and level >= ends[i]:
            return
        here = (z >= level) & (z < ends[i]) if level else (y == 1) & (z < ends[i])
        count = jnp.where(here, 2 if level else 1, 0)

        def load(slot):
            at = 2 * i + slot
            return pltpu.make_async_copy(
                keyvals.at[2 * (z - level) + slot, i], key_slots.at[at], slot_sems.at[at]
            )

        lax.fori_loop(0, count, lambda slot, carry: (load(slot).start(), carry)[1], 0)

        def step(slot, carry):
            load(slot).wait()
            attend(i, key_slots.at[2 * i + slot], False)
            return carry

        lax.fori_loop(0, count, step, 0)

    def alive_lanes(i):
        live = jnp.minimum(lengths[order[i]] - seq * rows, rows)
        return (lax.broadcasted_iota(jnp.int32, (1, rows), 1) < live).astype(jnp.float32)

    to_sibling, to_facing, onward = {}, {}, {}
    sibling, facing = place.sibling[1], place.facing[1]
    last = facing + 1 - 2 * (facing % 2)

    def finish_attention(i):
        alive = alive_lanes(i)
        for head in range(heads):
            at = pl.ds(head * HSIZE, HSIZE)
            total = summed[i, pl.ds(head, 1)]
            attended_turned[i, at] = weighted[i, at] * (alive / total)
            log_total[i, pl.ds(head, 1)] = highest[i, pl.ds(head, 1)] + jnp.log(total)
        mine = attended_turned.at[i]
        there = groups.at[place.head, i]
        to_sibling[i] = comm.copy(mine, there, place.sibling)
        to_facing[i] = comm.copy(mine, there, place.facing)

    def add_groups(i, total, near, far):
        parts = [split(source) for source, _ in (near, far)]

        def tile(columns):
            terms = []
            for part, (_, group) in zip(parts, (near, far)):
                weight = weight_a[pl.ds(pl.multiple_of(group * channels, 8), channels), columns]
                terms.append(dot_three(part, split(weight), BOTH_FIRST))
            total[chunk(i), columns] = terms[0] + terms[1]

        tiles(model, tile)

    def mix_near(i):
        to_sibling[i].wait_recv()
        add_groups(i, grad_inputs, (attended_turned[i], place.head), (groups[sibling, i], sibling))

    def mix_far(i):
        to_facing[i].wait_recv()
        theirs = groups.at[facing, i]
        onward[i] = comm.copy(theirs, theirs, place.sibling)
        onward[i].wait_recv()
        add_groups(i, result, (groups[facing, i], facing), (groups[last, i], last))
        mixed = inputs[order[i]] + as_row(output_bias) + (grad_inputs[chunk(i)] + result[chunk(i)])
        result[chunk(i)] = mixed
        normed_two[chunk(i)] = unit_rows(mixed)[0] * as_row(second_gain) + as_row(second_shift)

    half_rows = rows // 2
    second_sums = [
        HeadSum(
            comm,
            place,
            grad_normed,
            from_sibling.at[0, pl.ds(i * half_rows, half_rows)],
            from_facing.at[0, pl.ds(i * half_rows, half_rows)],
            i * rows,
            half_rows,
            2,
        )
        for i in range(sequences)
    ]

    def feed(i):
        parts = split(normed_two[chunk(i)])

        def tile(columns):
            hidden = dot_three(parts, split(weight_b[:, columns]), PLAIN)
            hidden = hidden + hidden_bias[columns].reshape(1, TILE)
            rectified = jnp.maximum(hidden, 0.0)
            active[chunk(i), columns] = rectified * rectified
            grad_hidden[chunk(i), columns] = 2.0 * rectified

        tiles(hidden_units, tile)

    def feed_back(i, begin):
        cot_parts = split(cotangent[order[i]])

        def tile(columns):
            grad = dot_three(cot_parts, split(weight_c[columns]), BOTH_LAST) * grad_hidden[chunk(i), columns]
            grad_hidden[chunk(i), columns] = grad
            row = down_rows(grad)
            vectors[2:3, columns] = row if begin else vectors[2:3, columns] + row

        tiles(hidden_units, tile)

    def second_grad(i):
        parts = split(grad_hidden[chunk(i)])

        def tile(columns):
            grad_normed[chunk(i), columns] = dot_three(parts, split(weight_b[columns]), BOTH_LAST)

        tiles(model, tile)
        second_sums[i].lend()

    swaps = {}

    def second_back(i):
        head_sum = second_sums[i]
        swaps[i] = []
        for p in range(head_sum.pieces):
            at = head_sum.rows_of(p)
            incoming = head_sum.piece(p)
            unit, inverse = unit_rows(result[at])
            through = norm_back(incoming, as_row(second_gain), unit, inverse)
            here = pl.ds(pl.multiple_of(core * half_rows + p * head_sum.size, 8), head_sum.size)
            grad_inputs[at] = cotangent[order[i], here] + through
            late_out[2:3] = late_out[2:3] + down_rows(incoming * unit)
            late_out[3:4] = late_out[3:4] + down_rows(incoming)
            swaps[i].append(comm.copy(grad_inputs.at[at], grad_inputs.at[at], place.sibling))

    late_out[...] = jnp.zeros_like(late_out)
    vectors[...] = jnp.zeros_like(vectors)
    attend(long, own_keys.at[long], True)
    for spread in key_spreads:
        spread.pass_pair()
    attend(short, own_keys.at[short], True)
    weight_to_facing.wait_recv()
    far_weight = rows_at(weight_a, facing * channels, channels)
    weight_onward = comm.copy(far_weight, far_weight, place.sibling)
    key_spreads[short].have_pair()
    attend_level(short, 0)
    for level in range(1, ends[short]):
        key_spreads[short].pass_level(level)
        key_spreads[short].have_level(level)
        attend_level(short, level)
    finish_attention(short)
    key_spreads[long].pass_level(1)
    crew.add(spread_steps(query_spreads), 0.0, 4.0)
    crew.tick(0.0)
    key_spreads[long].have_pair()
    attend_level(long, 0)
    weight_to_sibling.wait_recv()
    weight_onward.wait_recv()
    mix_near(short)
    key_spreads[long].pass_level(2)
    crew.tick(4.0)
    mix_far(short)
    key_spreads[long].have_level(1)
    attend_level(long, 1)
    load_b.wait()
    load_c.wait()
    key_spreads[long].pass_level(3)
    crew.tick(4.0)
    feed(short)
    feed_back(short, True)
    crew.tick(4.0)
    second_grad(short)
    key_spreads[long].have_level(2)
    attend_level(long, 2)
    second_sums[short].chip()
    key_spreads[long].have_level(3)
    attend_level(long, 3)
    finish_attention(long)
    second_back(short)
    crew.tick(4.0)
    mix_near(long)
    crew.tick(4.0)
    mix_far(long)
    crew.tick(4.0)
    feed(long)
    feed_back(long, False)
    crew.tick(4.0)
    second_grad(long)

    def cot_columns(columns):
        return jnp.concatenate([cotangent[order[i], :, columns] for i in range(sequences)], 0)

    active_parts = split(active[...])

    def outer_tile(columns):
        grad_outer[:, columns] = dot_three(active_parts, split(cot_columns(columns)), BOTH_FIRST)

    tiles(model, outer_tile, crew, 0.9)
    def add_sums(wanted, source, target):
        for pair_first, which, start, count, delay in plan:
            if which == wanted:
                make = sum_pair_first if pair_first else sum_line_first
                crew.add(make(comm, place, land, source, target, start, count), delay, HOP)

    add_sums(0, grad_outer, outer_out)
    second_sums[long].chip()

    normed_parts = split(normed_two[...])

    def inner_tile(columns):
        grad_inner[:, columns] = dot_three(normed_parts, split(grad_hidden[:, columns]), BOTH_FIRST)

    tiles(hidden_units, inner_tile, crew, 0.9)
    add_sums(1, grad_inner, inner_out)

    for made in (weight_to_sibling, weight_to_facing, weight_onward):
        comm.settle(made)
    outer_term = weight_a.at[pl.ds(0, tokens)]

    def outer_term_tile(columns):
        outer_term[:, columns] = dot_three(active_parts, split(weight_c[:, columns]), PLAIN)

    tiles(model, outer_term_tile, crew, 0.9)
    second_back(long)
    result_sum = HeadSum(comm, place, outer_term, from_sibling.at[1], from_facing.at[1], 0, rows, 4)
    result_sum.lend()
    for i in (short, long):
        for made in swaps[i]:
            made.wait_recv()
            comm.settle(made)
    crew.tick(8.0)

    weight_parts = split(output_weight[...])
    grad_att[:, channels:] = jnp.zeros((sequences, grad_att.shape[1] - channels, rows), jnp.float32)
    keep_grad = []
    for i in range(sequences):
        alive = alive_lanes(i)
        grad = dot_three(weight_parts, split(grad_inputs[chunk(i)]), BOTH_LAST) * alive
        grad_att[i, 0:channels] = grad
        both = grad * attended_turned[i]
        for head in range(heads):
            at = channels + head
            grad_att[i, at : at + 1] = log_total[i, head : head + 1]
            grad_att[i, at + heads : at + heads + 1] = down_rows(both[head_lanes(head)])
        grad_spreads[i].begin()
        keep_grad.append(comm.local(grad_att.at[i], all_grads.at[seq, i], keep=False))
    result_sum.chip()
    for i in range(sequences):
        for head in range(heads):
            query_cat[i, head] = against(queries[i, head_lanes(head)] * HSIZE ** (-0.5))
            grad_cat[i, head] = against(grad_att[i, head_lanes(head)])
    for spread in grad_spreads:
        spread.pass_pair()
    grad_rest = weight_b
    output_grad = jnp.zeros((channels, model), jnp.float32)
    for i in range(sequences):
        output_grad = output_grad + dot_three(split(attended_turned[i]), split(grad_inputs[chunk(i)]), PLAIN)
    grad_rest[0:channels] = output_grad
    vectors[0:1] = down_rows(grad_inputs[...])
    outer_row = jnp.zeros((1, model), jnp.float32)
    for i in range(sequences):
        outer_row = outer_row + down_rows(cotangent[order[i]])
    vectors[1:2] = outer_row
    add_sums(2, grad_rest, rest_out)
    crew.tick(TICKS)

    grad_query[...] = jnp.zeros_like(grad_query)
    grad_keyval[...] = jnp.zeros_like(grad_keyval)

    def query_side(i, start, end):
        count = jnp.where(z < ends[i], jnp.minimum(seq + 1, end), 0)

        def load(slot, block):
            return pltpu.make_async_copy(keyvals.at[block, i], key_slots.at[slot], slot_sems.at[slot])

        pl.when(count > start)(lambda: load(start % 2, seq - start).start())

        def step(t, carry):
            slot = lax.rem(t, 2)
            load(slot, seq - t).wait()
            pl.when(t + 1 < count)(lambda: load(1 - slot, seq - t - 1).start())
            block = key_slots.at[slot]
            for head in range(heads):
                key_high, key_low = split(block[:, head_lanes(head)])
                scores = dot(jnp.concatenate([key_high, key_high, key_low], 1), query_cat[i, head], PLAIN)
                at = channels + head
                scores = scores - grad_att[i, at : at + 1]
                powers = jnp.exp(jnp.where(allowed_from(scores.shape, t * rows), scores, NEGATIVE))
                slopes = dot(beside(block[:, head_lanes(head, channels)]), grad_cat[i, head], PLAIN)
                slopes = powers * (slopes - grad_att[i, at + heads : at + heads + 1])
                high, low = split(slopes)
                both = dot(jnp.concatenate([key_high, key_low], 1), high, BOTH_FIRST)
                term = both[:HSIZE] + both[HSIZE:] + dot(key_high, low, BOTH_FIRST)
                grad_query[i, head_lanes(head)] = grad_query[i, head_lanes(head)] + term
            return carry

        lax.fori_loop(start, jnp.maximum(count, start), step, 0)

    def key_side(i, offset, query_ref, grad_ref):
        for head in range(heads):
            lanes = head_lanes(head)
            query_high, query_low = split(query_ref[lanes] * HSIZE ** (-0.5))
            grad_high, grad_low = split(grad_ref[lanes])
            scores = dot(
                key_cat[i, head, :, 0 : 3 * HSIZE],
                jnp.concatenate([query_high, query_low, query_high], 0),
                PLAIN,
            )
            at = channels + head
            scores = scores - grad_ref[at : at + 1]
            powers = jnp.exp(jnp.where(allowed_from(scores.shape, offset), scores, NEGATIVE))
            slopes = dot(
                value_cat[i, head, :, 0 : 3 * HSIZE],
                jnp.concatenate([grad_high, grad_low, grad_high], 0),
                PLAIN,
            )
            slopes = powers * (slopes - grad_ref[at + heads : at + heads + 1])
            for base, (far_high, far_low), value in (
                (0, (query_high, query_low), slopes),
                (channels, (grad_high, grad_low), powers),
            ):
                high, low = split(value)
                both = dot(jnp.concatenate([far_high, far_low], 0), high, BOTH_LAST)
                term = both[:HSIZE] + both[HSIZE:] + dot(far_high, low, BOTH_LAST)
                where = slice(base + head * HSIZE, base + (head + 1) * HSIZE)
                grad_keyval[i, where] = grad_keyval[i, where] + term

    def key_level(level, pairs):
        items = [(i, slot) for i in range(sequences) for slot in range(2)]

        def inside(i):
            return z + level < jnp.where(i == 0, ends[0], ends[1])

        def wanted(t):
            i, slot = t // 2, t % 2
            if level:
                return inside(i)
            if pairs:
                return inside(i) & (slot == 1) & (y == 0)
            return inside(i) & (slot == y)

        def loads(t):
            i, slot = t // 2, t % 2
            block = 2 * (z + level) + slot
            return (
                pltpu.make_async_copy(all_queries.at[block, i], query_slots.at[t], slot_sems.at[2 * t]),
                pltpu.make_async_copy(all_grads.at[block, i], grad_slots.at[t], slot_sems.at[2 * t + 1]),
            )

        for t in range(len(items)):
            @pl.when(wanted(t))
            def _(t=t):
                for made in loads(t):
                    made.start()

        def step(t, carry):
            @pl.when(wanted(t))
            def _():
                for made in loads(t):
                    made.wait()
                i, slot = t // 2, t % 2
                offset = (2 * (z + level) + slot - seq) * rows
                key_side(i, offset, query_slots.at[t], grad_slots.at[t])

            return carry

        lax.fori_loop(0, len(items), step, 0)

    def pass_level(level):
        for spread in grad_spreads:
            spread.pass_level(level)

    def have_level(level):
        for spread in query_spreads + grad_spreads:
            spread.have_level(level)

    pass_level(1)
    for i in range(sequences):
        keep_keys[i].wait()
        for head in range(heads):
            key_cat[i, head, :, 0 : 3 * HSIZE] = beside(own_keys[i, :, head_lanes(head)])
            value_cat[i, head, :, 0 : 3 * HSIZE] = beside(own_keys[i, :, head_lanes(head, channels)])
        keep_query[i].wait()
        keep_grad[i].wait()
    key_level(0, False)
    crew.tick(TICKS)
    for spread in query_spreads + grad_spreads:
        spread.have_pair()
    key_level(0, True)
    query_side(0, 0, 4)
    pass_level(2)
    crew.tick(TICKS)
    query_side(0, 4, 8)
    query_side(1, 0, 8)
    have_level(1)
    key_level(1, False)
    crew.tick(TICKS)
    pass_level(3)
    have_level(2)
    key_level(2, False)
    crew.tick(TICKS)
    have_level(3)
    key_level(3, False)
    crew.tick(TICKS)
    returned = []
    for p in range(result_sum.pieces):
        at = result_sum.rows_of(p)
        result[at] = result[at] + as_row(outer_bias) + result_sum.piece(p)
        returned.append(comm.copy(result.at[at], result.at[at], place.sibling))

    for i in range(sequences):
        grad_conv[0, i, pl.ds(0, rows)] = (grad_query[i] * HSIZE ** (-0.5)).T
        grad_conv[1, i, pl.ds(0, rows)] = grad_keyval[i, 0:channels].T
        grad_conv[2, i, pl.ds(0, rows)] = grad_keyval[i, channels : 2 * channels].T

    @pl.when(seq == devices - 1)
    def _():
        grad_conv[:, :, pl.ds(rows, edge)] = jnp.zeros((3, sequences, edge, channels), jnp.float32)

    before = (seq - 1, place.head)
    rim = comm.copy(
        grad_conv.at[:, :, pl.ds(0, edge)], grad_conv.at[:, :, pl.ds(rows, edge)], before, seq > 0
    )
    for k in range(3):
        for j in range(3):
            total = jnp.zeros((1, channels), jnp.float32)
            for i in range(sequences):
                total = total + down_rows(grad_conv[k, i, pl.ds(0, rows)] * raw[k, i, pl.ds(edge - j, rows)])
            vectors[3 + j : 4 + j, k * channels : (k + 1) * channels] = total
    crew.tick(2.0)
    wait_for(rim, seq < devices - 1)
    for k, kernel in enumerate((query_kernel, key_kernel, value_kernel)):
        for i in range(sequences):
            grad_hidden[chunk(i), k * channels : (k + 1) * channels] = (
                kernel[0:1] * grad_conv[k, i, pl.ds(0, rows)]
                + kernel[1:2] * grad_conv[k, i, pl.ds(1, rows)]
                + kernel[2:3] * grad_conv[k, i, pl.ds(2, rows)]
            )
    def first_chunk(which):
        at = pl.ds(pl.multiple_of(which * rows, rows), rows)
        parts = split(grad_hidden[at, 0 : 3 * channels])

        def tile(columns):
            weight = jnp.concatenate([one[:, columns] for one in joined], 0)
            active[at, columns] = dot_three(parts, split(weight), PLAIN)

        tiles(model, tile)

    first_sum = HeadSum(comm, place, active, from_sibling.at[2], from_facing.at[2], 0, rows, 4)
    first_chunk(1 - core)
    first_sum.lend()
    first_chunk(core)
    first_sum.chip()
    crew.tick(3.0)
    for i in range(sequences):
        normed_two[chunk(i)] = first_normed(inputs[order[i]])
    projected_parts = split(grad_hidden[:, 0 : 3 * channels])

    def joined_tile(columns):
        grad_rest[channels : 4 * channels, columns] = dot_three(
            projected_parts, split(normed_two[:, columns]), BOTH_FIRST
        )

    tiles(model, joined_tile, crew, 0.9)
    add_sums(3, grad_rest, rest_out)
    add_sums(4, vectors, vectors_out)
    crew.tick(0.0)

    for p in range(first_sum.pieces):
        at = first_sum.rows_of(p)
        incoming = first_sum.piece(p)
        here = pl.ds(p * first_sum.size, first_sum.size)
        rows_in = jnp.where(core == 0, inputs[order[0], here], inputs[order[1], here])
        unit, inverse = unit_rows(rows_in)
        grad_inputs[at] = grad_inputs[at] + norm_back(incoming, as_row(first_gain), unit, inverse)
        late_out[0:1] = late_out[0:1] + down_rows(incoming * unit)
        late_out[1:2] = late_out[1:2] + down_rows(incoming)
        returned.append(comm.copy(grad_inputs.at[at], grad_inputs.at[at], place.sibling))
        crew.tick(3.5)
    late_sent = comm.copy(late_out, late_from, place.sibling)
    crew.tick(0.0)
    late_sent.wait_recv()
    late_all[seq] = late_out[...] + late_from[...]
    mine = late_all.at[seq]
    shared = [comm.copy(mine, mine, device) for device, _ in column]
    crew.drain()
    for made in returned + shared:
        made.wait_recv()
    comm.settle(late_sent)
    total = late_all[0]
    for k in range(1, devices):
        total = total + late_all[k]
    late_out[...] = total
    comm.finish()
    assert comm.used <= COPIES and comm.used_local <= local_sems.shape[0]


COPIES = 340
LOCALS = 64
SPACE = 5.0
HOP = 5.0
TICKS = 4.0


def sum_plan(hidden_units, model, channels):
    size = channels // 2
    plan = [(k % 3 < 2, 0, k * size, size, k * SPACE) for k in range(hidden_units // size)]
    plan += [(k % 3 == 1, 1, k * size, size, k * SPACE) for k in range(model // size)]
    plan += [(True, 2, 0, size, 0.0), (False, 2, size, size, SPACE / 2)]
    size = channels // 4
    plan += [(True, 3, channels + k * size, size, k * SPACE / 2) for k in range(6)]
    plan += [(False, 3, channels + (6 + k) * size, size, (k + 0.5) * SPACE / 2) for k in range(6)]
    plan += [(True, 4, 0, 16, 0.0)]
    return plan


def layer(ends, collective, lengths, inputs, cotangent, weights, vectors, kernels):
    query_weight, key_weight, value_weight, output_weight, inner_weight, outer_weight = weights
    sequences, rows, model = inputs.shape
    channels = output_weight.shape[0]
    heads = channels // HSIZE
    hidden_units = inner_weight.shape[1]
    tokens = sequences * rows
    devices = lax.axis_size("seq")
    plan = sum_plan(hidden_units, model, channels)
    land_rows = sum(3 * count // 2 if pair_first else 2 * count for pair_first, _, _, count, _ in plan)
    vmem = pl.BlockSpec(memory_space=pltpu.VMEM)
    far = pl.BlockSpec(memory_space=pl.ANY)

    def f32(*shape):
        return jax.ShapeDtypeStruct(shape, jnp.float32)

    def room(*shape, dtype=jnp.float32):
        return pltpu.VMEM(shape, dtype)

    edge = 8
    grad_rows = channels + 16
    half = functools.partial(room, dtype=jnp.bfloat16)
    return pl.pallas_call(
        functools.partial(layer_kernel, ends, plan),
        out_shape=[
            f32(tokens, model),
            f32(tokens, model),
            f32(hidden_units, model),
            f32(model, hidden_units),
            f32(4 * channels, model),
            f32(16, model),
            f32(8, model),
            f32(devices, sequences, rows, 2 * channels),
            f32(devices, sequences, channels, rows),
            f32(devices, sequences, grad_rows, rows),
        ],
        in_specs=[pl.BlockSpec(memory_space=pltpu.SMEM)] + [vmem] * 16 + [far] * 2,
        out_specs=[vmem] * 2 + [far] * 4 + [vmem] + [far] * 3,
        scratch_shapes=[
            room(sequences, edge, model),
            room(model, model),
            room(model, hidden_units),
            room(hidden_units, model),
            room(3, sequences, rows + edge, channels),
            room(4, sequences, channels, rows),
            room(sequences, channels, rows),
            room(sequences, channels, rows),
            room(sequences, 8, rows),
            room(sequences, 8, rows),
            room(sequences, channels, rows),
            room(sequences, 8, rows),
            room(tokens, model),
            room(tokens, hidden_units),
            room(tokens, hidden_units),
            room(tokens, model),
            room(3, rows, model),
            room(3, rows, model),
            room(hidden_units, model),
            room(model, hidden_units),
            room(16, model),
            room(land_rows, model),
            room(2 * sequences, rows, 2 * channels),
            room(sequences, rows, 2 * channels),
            room(2 * sequences, channels, rows),
            room(2 * sequences, grad_rows, rows),
            half(sequences, heads, 3 * HSIZE, rows),
            half(sequences, heads, 3 * HSIZE, rows),
            half(sequences, heads, rows, 256),
            half(sequences, heads, rows, 256),
            room(sequences, grad_rows, rows),
            room(sequences, channels, rows),
            room(sequences, 2 * channels, rows),
            room(3, sequences, rows + edge, channels),
            room(8, model),
            room(devices, 8, model),
            pltpu.SemaphoreType.DMA((COPIES,)),
            pltpu.SemaphoreType.DMA((COPIES,)),
            pltpu.SemaphoreType.DMA((LOCALS,)),
            pltpu.SemaphoreType.DMA((4 * sequences,)),
        ],
        compiler_params=pltpu.CompilerParams(
            collective_id=collective, has_side_effects=True, vmem_limit_bytes=63 * 2**20
        ),
        name="mega",
    )(
        lengths,
        inputs,
        cotangent,
        query_weight.T,
        key_weight.T,
        value_weight.T,
        output_weight,
        *vectors,
        *kernels,
        inner_weight,
        outer_weight,
    )


def shards(
    inputs,
    seq_lengths,
    first_gain,
    first_shift,
    query_weight,
    key_weight,
    value_weight,
    query_kernel,
    key_kernel,
    value_kernel,
    output_weight,
    output_bias,
    second_gain,
    second_shift,
    inner_weight,
    hidden_layer_bias,
    outer_weight,
    outer_bias,
    cotangent,
):
    channels = query_weight.shape[1]
    kernels = (query_kernel, key_kernel, value_kernel)

    def run(short_end, collective):
        ends = (LINE, short_end)
        result, grad_inputs, grad_outer, grad_inner, rest, vectors, late = layer(
            ends,
            collective,
            seq_lengths,
            inputs,
            cotangent,
            (query_weight, key_weight, value_weight, output_weight, inner_weight, outer_weight),
            (
                output_bias,
                first_gain,
                first_shift,
                second_gain,
                second_shift,
                hidden_layer_bias,
                outer_bias,
            ),
            kernels,
        )[:7]
        swap = seq_lengths[1] > seq_lengths[0]

        def written(array):
            return jnp.where(seq_lengths[0] >= 0, array, 0.0)

        def placed(array):
            array = array.reshape(inputs.shape)
            return jnp.where(swap, jnp.flip(array, 0), array)

        mixes = vectors[3:6, : 3 * channels]
        return (
            placed(result),
            placed(grad_inputs),
            late[0],
            late[1],
            rest[channels : 2 * channels].T,
            rest[2 * channels : 3 * channels].T,
            rest[3 * channels : 4 * channels].T,
            mixes[:, :channels],
            mixes[:, channels : 2 * channels],
            mixes[:, 2 * channels :],
            rest[:channels],
            vectors[0],
            late[2],
            late[3],
            written(grad_inner),
            vectors[2],
            written(grad_outer),
            vectors[1],
        )

    pair_rows = 2 * inputs.shape[1]
    shorter = jnp.minimum(seq_lengths[0], seq_lengths[1])
    reach = (shorter > pair_rows).astype(jnp.int32) + (shorter > 2 * pair_rows)
    cases = [functools.partial(run, end, 1 + k) for k, end in enumerate((1, 2, LINE))]
    return lax.switch(reach, cases)


def solution(mesh):
    lines = mesh.shape["seq"] == 2 * LINE and mesh.shape["head"] == 4
    return jax.shard_map(
        shards if lines else general_shards,
        mesh=mesh,
        in_specs=(
            P(None, "seq", None),
            P(),
            P(),
            P(),
            P(None, "head"),
            P(None, "head"),
            P(None, "head"),
            P(None, "head"),
            P(None, "head"),
            P(None, "head"),
            P("head", None),
            P(),
            P(),
            P(),
            P(None, "head"),
            P("head"),
            P("head", None),
            P(),
            P(None, "seq", None),
        ),
        out_specs=(
            P(None, "seq", None),
            P(None, "seq", None),
            P(),
            P(),
            P(None, "head"),
            P(None, "head"),
            P(None, "head"),
            P(None, "head"),
            P(None, "head"),
            P(None, "head"),
            P("head", None),
            P(),
            P(),
            P(),
            P(None, "head"),
            P("head"),
            P("head", None),
            P(),
        ),
        check_vma=False,
    )
```
